128 devices in a mesh: gx: 16 (over z, x), gy: 8 (over y, core).
Axes of the slice: x: 4, y: 4, z: 4, core: 2. Of those that a mesh axis runs over, the one named last changes fastest.
Arguments:
- ion_charge: float32 [512, 512, 128], P('gx', 'gy'), may hold values from -6 to 6
- density: float32 [512, 512, 128], P('gx', 'gy'), may hold values from 0.05 to 2
- charge_blocks: float32 [65536, 128], P(('gx', 'gy')), may hold values from -6 to 6
- panel_brick: int32 [16384], P(('gx', 'gy')), may hold values from 0 to 127, as said below
- row_counts: int32 [16384], P(('gx', 'gy')), may hold values from 1 to 4, as said below
- block_offset: int32 [65536], P(('gx', 'gy')), may hold values from 0 to 262136, as said below
- aperture_panel: int32 [2048], P(('gx', 'gy')), may hold values from 0 to 127
Outputs:
- potential: float32 [512, 512, 128], P('gx', 'gy')
- aperture_potential: float32 [2048], P(('gx', 'gy'))
The draws below stay inside these ranges and needn't reach their ends.
Inputs may be any that keep to these rules, and one draw needn't show every extreme that they name: `panel_brick`: on every owner the 128 panels lie in the 128 bricks one each (a permutation for each owner). `row_counts`: on every owner some panel has exactly 4 live rows. `block_offset`: x below 32, y below 64, z at most 120.
All inputs are finite; a program needn't handle non-finite values.
Results may differ from the reference program's by a relative error of at most 0.00013.
Values sent between devices are 32-bit elements; how exact they have to be, the bound alone decides.
No kernel may reach another device: no remote copies, remote signals or barrier semaphores. Data moves between devices by JAX's collectives and lax.ppermute only.
A program may use at most 128 MiB of HBM per device.

```python
import math
import jax
import jax.numpy as jnp

BX = 32
BY = 64
NZ = 128
NEWTON = 3
SWEEPS = 8
CAP = 4
BLX = 4
BLY = 4
BLZ = 8
APER_DEV = 16
BLK = 128
PAN_DEV = 128
PANELS = 16384
ROWS = 65536
APERTURES = 2048
NX = 512
NY = 512
N_GY = 8
DEVICES = 128


def bricks_of(key):
    subkeys = jax.random.split(jax.random.fold_in(key, 11), DEVICES)
    return jax.vmap(lambda single: jax.random.permutation(single, DEVICES))(subkeys).astype(jnp.int32)


def draw_panel_brick(key, part):
    return bricks_of(key).reshape(-1)


def draw_row_counts(key, part):
    bricks = bricks_of(key)
    counts_drawn = jax.random.randint(jax.random.fold_in(key, 12), (DEVICES, PAN_DEV), 1, CAP + 1)
    crowded = jax.random.randint(jax.random.fold_in(key, 13), (DEVICES,), 0, 4) == 0
    filled = crowded[bricks] | (bricks == 0)
    return jnp.where(filled, CAP, counts_drawn).astype(jnp.int32).reshape(-1)


def draw_block_offset(key, part):
    total_rows = DEVICES * PAN_DEV * CAP
    along_x = jax.random.randint(jax.random.fold_in(key, 21), (total_rows,), 0, BX)
    along_y = jax.random.randint(jax.random.fold_in(key, 22), (total_rows,), 0, BY)
    along_z = jax.random.randint(jax.random.fold_in(key, 23), (total_rows,), 0, NZ - BLZ + 1)
    offsets = (along_x * BY + along_y) * NZ + along_z
    offsets = offsets.at[0].set(BX * BY * NZ - BLZ)
    offsets = offsets.at[1].set(0)
    return offsets.astype(jnp.int32)


def touch_ends(values, key, least, high):
    longest = values.shape.index(max(values.shape))
    spots = []
    for shift in (0, 1):
        where = [jax.random.randint(jax.random.fold_in(key, axis), (), 0, length) for axis, length in enumerate(values.shape)]
        where[longest] = (where[longest] + shift) % values.shape[longest]
        spots.append(tuple(where))
    return values.at[spots[0]].set(least).at[spots[1]].set(high)


def levels(rng, dims, cuts, smallest, high):
    def one(axis_at, parts):
        heights = jax.random.uniform(jax.random.fold_in(jax.random.fold_in(rng, 6), axis_at), (parts,), jnp.float32, smallest / len(cuts), high / len(cuts))
        return jnp.repeat(jnp.exp(heights), dims[axis_at] // parts).reshape((-1,) + (1,) * (len(dims) - axis_at - 1))

    gain = one(*cuts[0])
    for cut in cuts[1:]:
        gain = gain * one(*cut)
    return gain


def bell_draw(rng, extent, spread, most, cuts=(), kind=jnp.bfloat16):
    result = jax.random.normal(rng, extent, jnp.float32) * spread
    if len(cuts) > 0:
        result = levels(rng, extent, cuts, -0.22, 0.18) * result
    return jnp.clip(result, min=-most, max=most).astype(kind)


def setup_inputs(seed: int = 0) -> dict:
    streams_of = jax.random.split(jax.random.key(seed), 8)
    return {
        "ion_charge": bell_draw(streams_of[0], (NX, NY, NZ), 1.0, 6.0, ((0, 16), (1, 8)), jnp.float32),
        "density": jnp.clip(jnp.exp(math.log(2.0) - 3.6888794 * jax.random.uniform(streams_of[1], (NX, NY, NZ), jnp.float32) ** levels(streams_of[1], (NX, NY, NZ), ((0, 16), (1, 8)), -0.2, 0.2)), 0.05, 2.0),
        "charge_blocks": bell_draw(streams_of[2], (ROWS, BLK), 1.0, 6.0, ((0, 128),), jnp.float32),
        "panel_brick": draw_panel_brick(jax.random.fold_in(streams_of[7], 71), 0),
        "row_counts": draw_row_counts(jax.random.fold_in(streams_of[7], 71), 0),
        "block_offset": draw_block_offset(jax.random.fold_in(streams_of[7], 71), 0),
        "aperture_panel": touch_ends(jax.random.randint(streams_of[6], (APERTURES,), 0, PAN_DEV), jax.random.fold_in(streams_of[6], 1), 0, PAN_DEV - 1).astype(jnp.int32),
    }


def neighbours(field):
    padded = jnp.pad(field, 1)
    total = padded[2:, 1:-1, 1:-1] + padded[:-2, 1:-1, 1:-1]
    total = total + padded[1:-1, 2:, 1:-1] + padded[1:-1, :-2, 1:-1]
    total = total + padded[1:-1, 1:-1, 2:] + padded[1:-1, 1:-1, :-2]
    return total


def reference(ion_charge, density, charge_blocks, panel_brick, row_counts, block_offset, aperture_panel):
    slot_index = jnp.arange(CAP, dtype=jnp.int32)
    live_rows = (slot_index[None, :] < row_counts[:, None]).astype(jnp.float32).reshape(ROWS)
    charges = charge_blocks * live_rows[:, None]
    brick_rows = jnp.repeat(panel_brick, CAP)
    brick_x = brick_rows // N_GY
    brick_y = brick_rows % N_GY
    corner_z = block_offset % NZ
    remains = block_offset // NZ
    corner_y = remains % BY + brick_y * BY
    corner_x = remains // BY + brick_x * BX
    entry = jnp.arange(BLK, dtype=jnp.int32)
    entry_x = entry // (BLY * BLZ)
    entry_y = (entry // BLZ) % BLY
    entry_z = entry % BLZ
    wide_y = NY + BLY - 1
    cell_index = ((corner_x[:, None] + entry_x[None, :]) * wide_y + corner_y[:, None] + entry_y[None, :]) * NZ + corner_z[:, None] + entry_z[None, :]
    cell_index = cell_index.astype(jnp.int32)
    flat_size = (NX + BLX - 1) * wide_y * NZ
    deposit = jnp.zeros((flat_size,), jnp.float32).at[cell_index.reshape(-1)].add(charges.reshape(-1))
    deposit = deposit.reshape(NX + BLX - 1, wide_y, NZ)[:NX, :NY]
    source = ion_charge + deposit
    potential = jnp.zeros((NX, NY, NZ), jnp.float32)
    for newton_step in range(NEWTON):
        coef = density * jnp.exp(potential)
        rhs = source + coef * (potential - 1.0)
        diagonal = 6.0 + coef
        for sweep_step in range(SWEEPS):
            potential = (rhs + neighbours(potential)) / diagonal
    padded = jnp.pad(potential, ((0, BLX - 1), (0, BLY - 1), (0, 0))).reshape(-1)
    row_potential = jnp.sum(charges * padded[cell_index], axis=1)
    panel_potential = row_potential.reshape(PANELS, CAP).sum(axis=1) / row_counts.astype(jnp.float32)
    owners = (jnp.arange(APERTURES, dtype=jnp.int32) // APER_DEV) * PAN_DEV + aperture_panel
    return potential, panel_potential[owners.astype(jnp.int32)]
```

```python
import jax
import jax.numpy as jnp
from jax import lax
from jax.experimental import pallas as pl
from jax.experimental.pallas import tpu as pltpu
from jax.sharding import PartitionSpec as P

BX = 32
BY = 64
NZ = 128
NEWTON = 3
SWEEPS = 8
CAP = 4
BLX = 4
BLY = 4
BLZ = 8
N_GX = 16
N_GY = 8
PAN_DEV = 128
APER_DEV = 16
LOW = 8
HIGH = 11
WX = LOW + BX + HIGH
TILES = 11
WY = 8 * TILES
DEPX = BX + BLX - 1
DEPY = 72
UNROLL = 8

VMEM = pl.BlockSpec(memory_space=pltpu.VMEM)
SMEM = pl.BlockSpec(memory_space=pltpu.SMEM)
F32 = jnp.float32


def call(body, outs, ins, scratch=(), mib=24):
    return pl.pallas_call(
        body,
        out_shape=[jax.ShapeDtypeStruct(s, F32) for s in outs],
        in_specs=list(ins),
        out_specs=[VMEM] * len(outs),
        scratch_shapes=list(scratch),
        compiler_params=pltpu.CompilerParams(vmem_limit_bytes=mib << 20),
    )


def iota(shape, dim):
    return lax.broadcasted_iota(jnp.int32, shape, dim)


def pack_kernel(brick, counts, offsets, aper, rows, send, need):
    def clear(p, c):
        need[p] = 0
        return c

    lax.fori_loop(0, PAN_DEV, clear, 0)
    for a in range(APER_DEV):
        need[aper[a]] = 1
    sub = iota((8, 128), 0)
    group = (iota((8, 128), 1) >> 3) & 3
    j = sub & 3
    masks = {e: (group == j - e) for e in range(-3, 4)}
    lane1 = iota((1, 128), 1)

    def body(q, c):
        p = q * 2
        live = sub < jnp.where(sub < 4, counts[p], counts[p + 1] + 4)
        v = jnp.where(live, rows[pl.ds(pl.multiple_of(q * 8, 8), 8), :], 0.0)
        out = v
        for e in (-3, -2, -1, 1, 2, 3):
            moved = pltpu.roll(pltpu.roll(v, e % 8, 0), (-8 * e) % 128, 1)
            out = jnp.where(masks[e], moved, out)
        for h in range(2):
            b = brick[p + h]
            send[b, 0:4, :] = out[4 * h : 4 * h + 4]
            meta = jnp.zeros((1, 128), jnp.int32)
            for k in range(CAP):
                meta = jnp.where(lane1 == k, offsets[(p + h) * CAP + k], meta)
            meta = jnp.where(lane1 == CAP, need[p + h], meta)
            send[b, 4:5, :] = meta.astype(F32)
        return c

    lax.fori_loop(0, PAN_DEV // 2, body, 0, unroll=2)


def corner(meta, p, k):
    offset = meta[p, k].astype(jnp.int32)
    return offset >> 13, (offset >> 7) & 63, offset & 127


def block_rows(v, z, k, i, lane):
    moved = pltpu.roll(v, (z - 32 * i - 8 * k + 128) & 127, 1)
    return jnp.where((lane >= z) & (lane < z + BLZ), moved, 0.0)


def deposit_kernel(got, ion, out, low, high, meta, sem):
    copy = pltpu.make_async_copy(got.at[:, 4, :], meta, sem)
    copy.start()
    out[0:BX, 0:BY, :] = ion[...]
    out[0:BX, BY:DEPY, :] = jnp.zeros((BX, DEPY - BY, NZ), F32)
    out[BX:DEPX] = jnp.zeros((DEPX - BX, DEPY, NZ), F32)
    lane = iota((BLY, 128), 1)
    copy.wait()

    def body(p, c):
        v = got[p, 0:4, :]
        for k in range(CAP):
            x, y, z = corner(meta, p, k)
            for i in range(BLX):
                out[x + i, pl.ds(y, BLY), :] += block_rows(v, z, k, i, lane)
        return c

    lax.fori_loop(0, PAN_DEV, body, 0, unroll=4)
    low[...] = out[0:HIGH]
    high[...] = out[BX - LOW : DEPX]


def widen_kernel(own, below, above, out, low, high):
    inside = jnp.where(lax.axis_index("gx") > 0, 1.0, 0.0)
    spill = DEPX - BX
    out[0:LOW] = below[0:LOW]
    out[LOW : LOW + BX] = own[0:BX]
    out[LOW : LOW + spill] += below[LOW : LOW + spill] * inside
    out[LOW + BX : WX] = above[...]
    out[LOW + BX : LOW + BX + spill] += own[BX:DEPX]
    low[...] = out[:, 0:16]
    high[...] = out[:, BY - LOW : DEPY]


def bounds():
    gx, gy = lax.axis_index("gx"), lax.axis_index("gy")
    x_lo = jnp.where(gx == 0, LOW, 0)
    x_hi = jnp.where(gx == N_GX - 1, LOW + BX, WX)
    y_lo = jnp.where(gy == 0, LOW, 0)
    y_hi = jnp.where(gy == N_GY - 1, LOW + BY, WY)
    sub = iota((8, 128), 0)
    inside = []
    for t in range(TILES):
        y = sub * TILES + t
        inside.append((y >= y_lo) & (y < y_hi))
    return x_lo, x_hi, inside


def sweep(src, dst, rhs, inv, lo, hi):
    lane = iota((8, 128), 1)
    first, last = lane == 0, lane == NZ - 1

    def layer(x):
        return [src[x, t] for t in range(TILES)]

    def rows(x0, count):
        layers = [layer(x0 - 1 + u) for u in range(count + 2)]
        for u in range(count):
            prev, cur, nxt = layers[u : u + 3]
            before = [pltpu.roll(cur[-1], 1, 0)] + cur[:-1]
            after = cur[1:] + [pltpu.roll(cur[0], 7, 0)]
            for t in range(TILES):
                left = jnp.where(first, 0.0, pltpu.roll(cur[t], 1, 1))
                right = jnp.where(last, 0.0, pltpu.roll(cur[t], NZ - 1, 1))
                total = (prev[t] + nxt[t]) + (before[t] + after[t]) + (left + right)
                dst[x0 + u, t] = (rhs[x0 + u, t] + total) * inv[x0 + u, t]

    turns = (hi - lo) // UNROLL

    def body(i, c):
        rows(lo + i * UNROLL, UNROLL)
        return c

    lax.fori_loop(0, turns, body, 0)
    if (hi - lo) % UNROLL:
        rows(lo + turns * UNROLL, (hi - lo) % UNROLL)


def finish(pot, nat, out, low, high):
    def body(x, c):
        for t in range(TILES):
            nat[x, pl.ds(t, 8, stride=TILES), :] = pot[x + LOW, t]
        return c

    lax.fori_loop(0, DEPX, body, 0, unroll=5)
    out[...] = nat[0:BX, LOW : LOW + BY]
    if high is not None:
        low[...] = nat[0:HIGH, LOW : LOW + BY]
        high[...] = nat[BX - LOW : BX, LOW : LOW + BY]
    else:
        low[...] = nat[0:DEPX, LOW : LOW + DEPY]


def first_kernel(
    own, below, above, density, out, low, high, source, dens, nat, b0, b1, rhs, inv
):
    x_lo, x_hi, inside = bounds()
    spread = jnp.where(lax.axis_index("gy") > 0, 1.0, 0.0)
    nat[:, 0:LOW] = below[:, 0:LOW]
    nat[:, LOW : LOW + DEPY] = own[...]
    nat[:, LOW : LOW + 8] += below[:, 8:16] * spread
    nat[:, LOW + DEPY : WY] = above[:, 8:16]
    nat[:, LOW + BY : LOW + DEPY] += above[:, 0:8]

    def prep(x, c):
        f = jnp.where((x >= x_lo) & (x < x_hi), 1.0, 0.0)
        for t in range(TILES):
            s = nat[x, pl.ds(t, 8, stride=TILES), :]
            d = density[x, pl.ds(t, 8, stride=TILES), :]
            source[x, t] = s
            dens[x, t] = d
            scale = jnp.where(inside[t], f / (6.0 + d), 0.0)
            inv[x, t] = scale
            rhs[x, t] = s - d
            b1[x, t] = (s - d) * scale
        return c

    lax.fori_loop(0, WX, prep, 0, unroll=3)
    bufs = (b0, b1)
    for k in range(2, SWEEPS + 1):
        sweep(bufs[(k - 1) % 2], bufs[k % 2], rhs, inv, k, WX - k)
    finish(b0, nat, out, low, high)


def next_kernel(
    own, x_below, x_above, y_below, y_above, source, dens, out, low, high, nat, b0, b1, rhs, inv
):
    x_lo, x_hi, inside = bounds()
    nat[:, 0:LOW] = y_below[...]
    nat[0:LOW, LOW : LOW + BY] = x_below[...]
    nat[LOW : LOW + BX, LOW : LOW + BY] = own[...]
    nat[LOW + BX : WX, LOW : LOW + BY] = x_above[...]
    nat[:, LOW + BY : WY] = y_above[...]

    def prep(x, c):
        f = jnp.where((x >= x_lo) & (x < x_hi), 1.0, 0.0)
        for t in range(TILES):
            p = jnp.where(inside[t], nat[x, pl.ds(t, 8, stride=TILES), :] * f, 0.0)
            coef = dens[x, t] * jnp.exp(p)
            b0[x, t] = p
            rhs[x, t] = source[x, t] + coef * (p - 1.0)
            inv[x, t] = jnp.where(inside[t], f / (6.0 + coef), 0.0)
        return c

    lax.fori_loop(0, WX, prep, 0, unroll=3)
    bufs = (b0, b1)
    for k in range(1, SWEEPS + 1):
        sweep(bufs[(k - 1) % 2], bufs[k % 2], rhs, inv, k, WX - k)
    finish(b0, nat, out, low, high)


def last_kernel(*refs):
    next_kernel(*refs[:9], None, *refs[9:])


def read_kernel(got, field, out, meta, sem):
    copy = pltpu.make_async_copy(got.at[:, 4, :], meta, sem)
    copy.start()
    out[...] = jnp.zeros((PAN_DEV, 1, 128), F32)
    lane = iota((BLY, 128), 1)
    copy.wait()

    def body(p, c):
        @pl.when(meta[p, CAP].astype(jnp.int32) > 0)
        def _():
            v = got[p, 0:4, :]
            total = jnp.zeros((BLY, 128), F32)
            for k in range(CAP):
                x, y, z = corner(meta, p, k)
                for i in range(BLX):
                    total += block_rows(v, z, k, i, lane) * field[x + i, pl.ds(y, BLY), :]
            out[p] = jnp.sum(total, axis=0, keepdims=True)

        return c

    lax.fori_loop(0, PAN_DEV, body, 0)


def pick_kernel(brick, counts, aper, got, out, rows):
    sub = iota((APER_DEV, 1), 0)
    live = jnp.ones((APER_DEV, 1), F32)
    for a in range(APER_DEV):
        p = aper[a]
        rows[a : a + 1, :] = got[brick[p]]
        live = jnp.where(sub == a, counts[p].astype(F32), live)
    out[...] = jnp.sum(rows[...], axis=1, keepdims=True) / live


def ring(array, axis, by):
    size = lax.axis_size(axis)
    return lax.ppermute(array, axis, [(i, (i + by) % size) for i in range(size)])


def on_device(
    ion_charge, density, charge_blocks, panel_brick, row_counts, block_offset, aperture_panel
):
    everyone = ("gx", "gy")
    (send,) = call(
        pack_kernel,
        [(PAN_DEV, 8, 128)],
        [SMEM] * 4 + [VMEM],
        [pltpu.SMEM((PAN_DEV,), jnp.int32)],
    )(panel_brick, row_counts, block_offset, aperture_panel, charge_blocks)
    got = lax.all_to_all(send, everyone, split_axis=0, concat_axis=0, tiled=True)

    d_below = ring(density[BX - LOW :], "gx", 1)
    d_above = ring(density[:HIGH], "gx", -1)
    d_wide = jnp.concatenate([d_below, density, d_above], axis=0)
    d_left = ring(d_wide[:, BY - LOW :], "gy", 1)
    d_right = ring(d_wide[:, :16], "gy", -1)
    d_wide = jnp.concatenate([d_left, d_wide, d_right], axis=1)

    meta = [pltpu.SMEM((PAN_DEV, 128), F32), pltpu.SemaphoreType.DMA]
    own, low, high = call(
        deposit_kernel,
        [(DEPX, DEPY, NZ), (HIGH, DEPY, NZ), (HIGH, DEPY, NZ)],
        [VMEM] * 2,
        meta,
    )(got, ion_charge)
    below, above = ring(high, "gx", 1), ring(low, "gx", -1)
    wide, low, high = call(
        widen_kernel, [(WX, DEPY, NZ), (WX, 16, NZ), (WX, 16, NZ)], [VMEM] * 3
    )(own, below, above)
    below, above = ring(high, "gy", 1), ring(low, "gy", -1)

    tiles = (WX, TILES, 8, NZ)
    work = [pltpu.VMEM((WX, WY, NZ), F32)] + [pltpu.VMEM(tiles, F32)] * 4
    brick = [(BX, BY, NZ), (HIGH, BY, NZ), (LOW, BY, NZ)]
    pot, low, high, source, dens = call(
        first_kernel, brick + [tiles, tiles], [VMEM] * 4, work, 40
    )(wide, below, above, d_wide)
    for step in range(1, NEWTON):
        below, above = ring(high, "gx", 1), ring(low, "gx", -1)
        edge = jnp.concatenate(
            [below[:, BY - LOW :], pot[:, BY - LOW :], above[:, BY - LOW :]], axis=0
        )
        left = ring(edge, "gy", 1)
        edge = jnp.concatenate([below[:, :16], pot[:, :16], above[:, :16]], axis=0)
        right = ring(edge, "gy", -1)
        operands = (pot, below, above, left, right, source, dens)
        if step < NEWTON - 1:
            pot, low, high = call(next_kernel, brick, [VMEM] * 7, work, 40)(*operands)
        else:
            pot, grown = call(
                last_kernel, [brick[0], (DEPX, DEPY, NZ)], [VMEM] * 7, work, 40
            )(*operands)
    (sums,) = call(read_kernel, [(PAN_DEV, 1, 128)], [VMEM] * 2, meta)(got, grown)
    back = lax.all_to_all(sums, everyone, split_axis=0, concat_axis=0, tiled=True)
    (picked,) = call(
        pick_kernel,
        [(APER_DEV, 1)],
        [SMEM] * 3 + [VMEM],
        [pltpu.VMEM((APER_DEV, 128), F32)],
    )(panel_brick, row_counts, aperture_panel, back)
    return pot, picked.reshape(APER_DEV)


def solution(mesh):
    everyone = P(("gx", "gy"))
    grid = P("gx", "gy", None)
    return jax.shard_map(
        on_device,
        mesh=mesh,
        in_specs=(grid, grid, P(("gx", "gy"), None)) + (everyone,) * 4,
        out_specs=(grid, everyone),
        check_vma=False,
    )
```

```python
import functools

import jax
import jax.numpy as jnp
from jax import lax
from jax.experimental import pallas as pl
from jax.experimental.pallas import tpu as pltpu
from jax.sharding import PartitionSpec as P

BX = 32
BY = 64
NZ = 128
NEWTON = 3
SWEEPS = 8
CAP = 4
BLX = 4
BLY = 4
BLZ = 8
N_GX = 16
N_GY = 8
PAN_DEV = 128
APER_DEV = 16
LOW = 8
HIGH = 11
WX = LOW + BX + HIGH
TILES = 11
WY = 8 * TILES
DEPX = BX + BLX - 1
DEPY = 72
UNROLL = 8

VMEM = pl.BlockSpec(memory_space=pltpu.VMEM)
SMEM = pl.BlockSpec(memory_space=pltpu.SMEM)
F32 = jnp.float32


def call(body, outs, ins, scratch=(), mib=24, flops=None):
    cost = None
    if flops is not None:
        cost = pl.CostEstimate(flops=flops, bytes_accessed=1 << 20, transcendentals=0)
    return pl.pallas_call(
        body,
        out_shape=[jax.ShapeDtypeStruct(s, F32) for s in outs],
        in_specs=list(ins),
        out_specs=[VMEM] * len(outs),
        scratch_shapes=list(scratch),
        cost_estimate=cost,
        compiler_params=pltpu.CompilerParams(vmem_limit_bytes=mib << 20),
    )


def iota(shape, dim):
    return lax.broadcasted_iota(jnp.int32, shape, dim)


def pack_kernel(*refs):
    arrays, send, local, need, sems = refs[:5], refs[5], refs[6:11], refs[11], refs[12]
    copies = [pltpu.make_async_copy(a, b, sems.at[i]) for i, (a, b) in enumerate(zip(arrays, local))]
    for copy in copies:
        copy.start()
    brick, counts, offsets, aper, rows = local

    def clear(p, c):
        need[p] = 0
        return c

    lax.fori_loop(0, PAN_DEV, clear, 0, unroll=8)
    for copy in copies:
        copy.wait()
    for a in range(APER_DEV):
        need[aper[a]] = 1
    sub = iota((8, 128), 0)
    group = (iota((8, 128), 1) >> 3) & 3
    j = sub & 3
    masks = {e: (group == j - e) for e in range(-3, 4)}
    lane1 = iota((1, 128), 1)

    def body(q, c):
        p = q * 2
        live = sub < jnp.where(sub < 4, counts[p], counts[p + 1] + 4)
        v = jnp.where(live, rows[pl.ds(pl.multiple_of(q * 8, 8), 8), :], 0.0)
        out = v
        for e in (-3, -2, -1, 1, 2, 3):
            moved = pltpu.roll(pltpu.roll(v, e % 8, 0), (-8 * e) % 128, 1)
            out = jnp.where(masks[e], moved, out)
        for h in range(2):
            b = brick[p + h]
            send[b, 0:4, :] = out[4 * h : 4 * h + 4]
            meta = jnp.zeros((1, 128), jnp.int32)
            for k in range(CAP):
                meta = jnp.where(lane1 == k, offsets[(p + h) * CAP + k], meta)
            meta = jnp.where(lane1 == CAP, need[p + h], meta)
            send[b, 4:5, :] = meta.astype(F32)
        return c

    lax.fori_loop(0, PAN_DEV // 2, body, 0, unroll=2)


def corner(meta, p, k):
    offset = meta[p, k].astype(jnp.int32)
    return offset >> 13, (offset >> 7) & 63, offset & 127


def block_rows(v, z, k, i, lane):
    moved = pltpu.roll(v, (z - 32 * i - 8 * k + 128) & 127, 1)
    return jnp.where((lane >= z) & (lane < z + BLZ), moved, 0.0)


def deposit_kernel(got, ion, out, x_low, x_high, y_low, y_high, meta, sem):
    copy = pltpu.make_async_copy(got.at[:, 4, :], meta, sem)
    copy.start()
    out[0:BX, 0:BY, :] = ion[...]
    out[0:BX, BY:DEPY, :] = jnp.zeros((BX, DEPY - BY, NZ), F32)
    out[BX:DEPX] = jnp.zeros((DEPX - BX, DEPY, NZ), F32)
    lane = iota((BLY, 128), 1)
    copy.wait()

    def body(p, c):
        v = got[p, 0:4, :]
        for k in range(CAP):
            x, y, z = corner(meta, p, k)
            for i in range(BLX):
                out[x + i, pl.ds(y, BLY), :] += block_rows(v, z, k, i, lane)
        return c

    lax.fori_loop(0, PAN_DEV, body, 0, unroll=4)
    x_low[...] = out[0:HIGH]
    x_high[...] = out[BX - LOW : DEPX]
    y_low[...] = out[:, 0:16]
    y_high[...] = out[:, BY - LOW : DEPY]


def inside_y():
    gy = lax.axis_index("gy")
    lo = jnp.where(gy == 0, LOW, 0)
    hi = jnp.where(gy == N_GY - 1, LOW + BY, WY)
    sub = iota((8, 128), 0)
    ys = [sub * TILES + t for t in range(TILES)]
    return [(y >= lo) & (y < hi) for y in ys]


def lay(nat, at, count, own, below, above):
    nat[at : at + count, 0:LOW] = below
    nat[at : at + count, LOW : LOW + BY] = own
    nat[at : at + count, LOW + BY : WY] = above


def lay_charge(nat, at, count, own, below, above):
    spread = jnp.where(lax.axis_index("gy") > 0, 1.0, 0.0)
    nat[at : at + count, 0:LOW] = below[:, 0:LOW]
    nat[at : at + count, LOW : LOW + DEPY] = own
    nat[at : at + count, LOW : LOW + 8] += below[:, LOW : LOW + 8] * spread
    nat[at : at + count, LOW + BY : LOW + DEPY] += above[:, 0:8]
    nat[at : at + count, LOW + DEPY : WY] = above[:, 8:16]


def strided(nat, x, t):
    return nat[x, pl.ds(t, 8, stride=TILES), :]


def relax(layers, write):
    lane = iota((8, 128), 1)
    first, last = lane == 0, lane == NZ - 1
    for u in range(len(layers) - 2):
        prev, cur, nxt = layers[u : u + 3]
        before = [pltpu.roll(cur[-1], 1, 0)] + cur[:-1]
        after = cur[1:] + [pltpu.roll(cur[0], 7, 0)]
        for t in range(TILES):
            left = jnp.where(first, 0.0, pltpu.roll(cur[t], 1, 1))
            right = jnp.where(last, 0.0, pltpu.roll(cur[t], NZ - 1, 1))
            total = (prev[t] + nxt[t]) + (before[t] + after[t]) + (left + right)
            write(u, t, total)


def layer(buf, x):
    return [buf[x, t] for t in range(TILES)]


def sweep(src, dst, rhs, inv, lo, hi):
    def rows(x0, count):
        def write(u, t, total):
            dst[x0 + u, t] = (rhs[x0 + u, t] + total) * inv[x0 + u, t]

        relax([layer(src, x0 - 1 + u) for u in range(count + 2)], write)

    turns = (hi - lo) // UNROLL

    def body(i, c):
        rows(lo + i * UNROLL, UNROLL)
        return c

    lax.fori_loop(0, turns, body, 0)
    if (hi - lo) % UNROLL:
        rows(lo + turns * UNROLL, (hi - lo) % UNROLL)


def inner(b0, b1, rhs, inv, k0, a, h):
    bufs = (b0, b1)
    for k in range(k0, SWEEPS + 1):
        sweep(bufs[(k - 1) % 2], bufs[k % 2], rhs, inv, a + k, h - k)


def inner_first(charge, y_below, y_above, density, d_below, d_above, *refs):
    b0, b1, rhs, inv, source, dens, nat = refs
    inside = inside_y()
    lay(nat, 0, BX, density[...], d_below[...], d_above[...])

    def take(x, c):
        for t in range(TILES):
            dens[x, t] = strided(nat, x, t)
        return c

    lax.fori_loop(0, BX, take, 0, unroll=4)
    lay_charge(nat, 0, DEPX, charge[...], y_below, y_above)

    def prep(x, c):
        for t in range(TILES):
            s = strided(nat, x, t)
            d = dens[x, t]
            source[x, t] = s
            scale = jnp.where(inside[t], 1.0 / (6.0 + d), 0.0)
            inv[x, t] = scale
            rhs[x, t] = s - d
            b1[x, t] = (s - d) * scale
        return c

    lax.fori_loop(0, BX, prep, 0, unroll=4)
    for x in range(BX, DEPX):
        for t in range(TILES):
            source[x, t] = strided(nat, x, t)
    inner(b0, b1, rhs, inv, 2, BLX - 2, BX + 1)


def inner_next(own, y_below, y_above, source, s_low, dens, b0, b1, rhs, inv, nat):
    inside = inside_y()
    lay(nat, 0, BX, own[...], y_below[...], y_above[...])

    def prep_from(src, shift):
        def prep(x, c):
            for t in range(TILES):
                p = jnp.where(inside[t], strided(nat, x, t), 0.0)
                coef = dens[x, t] * jnp.exp(p)
                b0[x, t] = p
                rhs[x, t] = src[x + shift, t] + coef * (p - 1.0)
                inv[x, t] = jnp.where(inside[t], 1.0 / (6.0 + coef), 0.0)
            return c

        return prep

    for x in range(BLX - 1):
        prep_from(s_low, LOW)(x, 0)
    lax.fori_loop(BLX - 1, BX, prep_from(source, 0), 0)
    inner(b0, b1, rhs, inv, 1, 0, BX)


def flanks(b0, b1, lows, highs, rhs, inv, k0, a, h):
    (l0, l1, l_rhs, l_inv), (h0, h1, h_rhs, h_inv) = lows, highs
    n_low, n_high = LOW + a, BX + HIGH - h
    for i in range(LOW + a):
        if i + LOW >= len_low_halo(a):
            l_rhs[i + LOW], l_inv[i + LOW] = rhs[i], inv[i]
    for i in range(h - LOW, BX):
        h_rhs[i - (h - LOW)], h_inv[i - (h - LOW)] = rhs[i], inv[i]

    def one(k, near, l_src, l_dst, h_src, h_dst):
        def low_write(u, t, total):
            l_dst[k + u, t] = (l_rhs[k + u, t] + total) * l_inv[k + u, t]

        def high_write(u, t, total):
            r = LOW - k + u
            h_dst[r, t] = (h_rhs[r, t] + total) * h_inv[r, t]

        low = [layer(l_src, k - 1 + j) for j in range(n_low)]
        relax(low + [layer(near, a + k - 1), layer(near, a + k)], low_write)
        high = [layer(h_src, LOW + 1 - k + j) for j in range(n_high)]
        relax([layer(near, h - k - 1), layer(near, h - k)] + high, high_write)

    if k0 == 2:
        one(2, b1, l1, l0, h1, h0)

    def body(j, c):
        one(2 * j + 1, b0, l0, l1, h0, h1)
        one(2 * j + 2, b1, l1, l0, h1, h0)
        return c

    lax.fori_loop(k0 - 1, SWEEPS // 2, body, 0)


def len_low_halo(a):
    return LOW + (BLX - 1 if a else 0)


def finish(b0, l0, h0, nat, a, h):
    def take(src, shift):
        def body(x, c):
            for t in range(TILES):
                nat[x, pl.ds(t, 8, stride=TILES), :] = src[x + shift, t]
            return c

        return body

    lax.fori_loop(0, a + LOW, take(l0, LOW), 0, unroll=4)
    lax.fori_loop(a + LOW, h - LOW, take(b0, 0), 0, unroll=4)
    lax.fori_loop(h - LOW, DEPX, take(h0, LOW - h), 0, unroll=4)


def hand_on(nat, out, x_low, x_high, y_low, y_high):
    out[...] = nat[0:BX, LOW : LOW + BY]
    x_low[...] = nat[0:HIGH, LOW : LOW + BY]
    x_high[...] = nat[BX - LOW : BX, LOW : LOW + BY]
    y_low[...] = nat[0:BX, LOW : LOW + 16]
    y_high[...] = nat[0:BX, BY : LOW + BY]


def edges():
    gx = lax.axis_index("gx")
    return jnp.where(gx > 0, 1.0, 0.0), jnp.where(gx < N_GX - 1, 1.0, 0.0)


def flank_first(*refs):
    b0, b1, rhs, inv, source, dens, x_below, x_above, c_below, c_above = refs[:10]
    dx_below, dx_above, dc_below, dc_above = refs[10:14]
    outs, (s_low, s_high, d_low, d_high), nat, spare = refs[14:19], refs[19:23], refs[23], refs[24:]
    l0, l1, l_rhs, l_inv, h0, h1, h_rhs, h_inv = spare
    a, h = BLX - 2, BX + 1
    inside, (f_low, f_high) = inside_y(), edges()
    lay_charge(nat, 0, HIGH, x_below[...], c_below[:, 0:16], c_below[:, 16:32])
    lay_charge(nat, HIGH, HIGH, x_above[...], c_above[:, 0:16], c_above[:, 16:32])
    for r in range(HIGH):
        for t in range(TILES):
            s = strided(nat, r, t)
            if r >= LOW:
                s = source[r - LOW, t] + s * f_low
            s_low[r, t] = s
            s = strided(nat, HIGH + r, t)
            if r < DEPX - BX:
                s = s + source[BX + r, t]
            s_high[r, t] = s
    lay(nat, 0, LOW, dx_below[...], dc_below[:, 0:LOW], dc_below[:, LOW:24])
    lay(nat, LOW, HIGH, dx_above[...], dc_above[:, 0:LOW], dc_above[:, LOW:24])
    for r in range(LOW):
        for t in range(TILES):
            d_low[r, t] = strided(nat, r, t)
    for r in range(HIGH):
        for t in range(TILES):
            d_high[r, t] = strided(nat, LOW + r, t)
    for r in range(HIGH):
        for t in range(TILES):
            if r < LOW:
                d = d_low[r, t]
                scale = jnp.where(inside[t], f_low / (6.0 + d), 0.0)
            else:
                scale = inv[r - LOW, t]
                d = dens[r - LOW, t]
            value = s_low[r, t] - d
            l_rhs[r, t], l_inv[r, t], l1[r, t] = value, scale, value * scale
            d = d_high[r, t]
            scale = jnp.where(inside[t], f_high / (6.0 + d), 0.0)
            value = s_high[r, t] - d
            q = r + LOW - 1
            h_rhs[q, t], h_inv[q, t], h1[q, t] = value, scale, value * scale
    flanks(b0, b1, (l0, l1, l_rhs, l_inv), (h0, h1, h_rhs, h_inv), rhs, inv, 2, a, h)
    finish(b0, l0, h0, nat, a, h)
    hand_on(nat, *outs)


def flank_next(last, *refs):
    b0, b1, rhs, inv, x_below, x_above, c_below, c_above = refs[:8]
    s_low, s_high, d_low, d_high = refs[8:12]
    outs, rest = (refs[12:14], refs[14:]) if last else (refs[12:17], refs[17:])
    nat, l0, l1, l_rhs, l_inv, h0, h1, h_rhs, h_inv = rest
    a, h = 0, BX
    inside, (f_low, f_high) = inside_y(), edges()
    lay(nat, 0, LOW, x_below[...], c_below[:, 0:LOW], c_below[:, LOW:24])
    lay(nat, LOW, HIGH, x_above[...], c_above[:, 0:LOW], c_above[:, LOW:24])

    def prep(count, shift, at, f, d_ref, s_ref, p_out, rhs_out, inv_out):
        def body(r, c):
            for t in range(TILES):
                p = jnp.where(inside[t], strided(nat, r + shift, t) * f, 0.0)
                coef = d_ref[r, t] * jnp.exp(p)
                p_out[r + at, t] = p
                rhs_out[r + at, t] = s_ref[r, t] + coef * (p - 1.0)
                inv_out[r + at, t] = jnp.where(inside[t], f / (6.0 + coef), 0.0)
            return c

        lax.fori_loop(0, count, body, 0)

    prep(LOW, 0, 0, f_low, d_low, s_low, l0, l_rhs, l_inv)
    prep(HIGH, LOW, LOW, f_high, d_high, s_high, h0, h_rhs, h_inv)
    flanks(b0, b1, (l0, l1, l_rhs, l_inv), (h0, h1, h_rhs, h_inv), rhs, inv, 1, a, h)
    finish(b0, l0, h0, nat, a, h)
    if last:
        outs[0][...] = nat[0:BX, LOW : LOW + BY]
        outs[1][...] = nat[0:DEPX, LOW : LOW + DEPY]
    else:
        hand_on(nat, *outs)


def corner_kernel(below, above, low, high):
    n = below.shape[1]
    low[:, 0:n] = below[0:HIGH]
    low[:, n:] = above[0:HIGH]
    high[:, 0:n] = below[BX - LOW :]
    high[:, n:] = above[BX - LOW :]


def beside(x_low, x_high, y_low, y_high):
    y_below, y_above = ring(y_high, "gy", 1), ring(y_low, "gy", -1)
    x_below, x_above = ring(x_high, "gx", 1), ring(x_low, "gx", -1)
    rows, n = y_high.shape[0], y_high.shape[1] + y_low.shape[1]
    c_low, c_high = call(
        corner_kernel, [(HIGH, n, NZ), (rows - BX + LOW, n, NZ)], [VMEM] * 2
    )(y_below, y_above)
    c_below, c_above = ring(c_high, "gx", 1), ring(c_low, "gx", -1)
    return (y_below, y_above), (x_below, x_above, c_below, c_above)


def read_kernel(got, field, out, meta, sem):
    copy = pltpu.make_async_copy(got.at[:, 4, :], meta, sem)
    copy.start()
    out[...] = jnp.zeros((PAN_DEV, 1, 128), F32)
    lane = iota((BLY, 128), 1)
    copy.wait()

    def body(p, c):
        @pl.when(meta[p, CAP].astype(jnp.int32) > 0)
        def _():
            v = got[p, 0:4, :]
            total = jnp.zeros((BLY, 128), F32)
            for k in range(CAP):
                x, y, z = corner(meta, p, k)
                for i in range(BLX):
                    total += block_rows(v, z, k, i, lane) * field[x + i, pl.ds(y, BLY), :]
            out[p] = jnp.sum(total, axis=0, keepdims=True)

        return c

    lax.fori_loop(0, PAN_DEV, body, 0)


def pick_kernel(brick, counts, aper, got, out, rows):
    sub = iota((APER_DEV, 1), 0)
    live = jnp.ones((APER_DEV, 1), F32)
    for a in range(APER_DEV):
        p = aper[a]
        rows[a : a + 1, :] = got[brick[p]]
        live = jnp.where(sub == a, counts[p].astype(F32), live)
    out[...] = jnp.sum(rows[...], axis=1, keepdims=True) / live


def ring(array, axis, by):
    size = lax.axis_size(axis)
    return lax.ppermute(array, axis, [(i, (i + by) % size) for i in range(size)])


def on_device(
    ion_charge, density, charge_blocks, panel_brick, row_counts, block_offset, aperture_panel
):
    everyone = ("gx", "gy")
    ints = [pltpu.SMEM((n,), jnp.int32) for n in (PAN_DEV, PAN_DEV, PAN_DEV * CAP, APER_DEV)]
    (send,) = call(
        pack_kernel,
        [(PAN_DEV, 8, 128)],
        [pl.BlockSpec(memory_space=pl.ANY)] * 5,
        ints
        + [
            pltpu.VMEM((PAN_DEV * CAP, 128), F32),
            pltpu.SMEM((PAN_DEV,), jnp.int32),
            pltpu.SemaphoreType.DMA((5,)),
        ],
    )(panel_brick, row_counts, block_offset, aperture_panel, charge_blocks)
    got = lax.all_to_all(send, everyone, split_axis=0, concat_axis=0, tiled=True)
    dy, dx = beside(density[:HIGH], density[BX - LOW :], density[:, :16], density[:, BY - LOW :])

    meta = [pltpu.SMEM((PAN_DEV, 128), F32), pltpu.SemaphoreType.DMA]
    charge, *slabs = call(
        deposit_kernel,
        [(DEPX, DEPY, NZ)] + [(HIGH, DEPY, NZ)] * 2 + [(DEPX, 16, NZ)] * 2,
        [VMEM] * 2,
        meta,
    )(got, ion_charge)

    def tiles(n):
        return (n, TILES, 8, NZ)

    def nat(n):
        return [pltpu.VMEM((n, WY, NZ), F32)]

    spare = [pltpu.VMEM(tiles(LOW + LOW + BLX), F32)] * 8
    brick = [(BX, BY, NZ), (HIGH, BY, NZ), (LOW, BY, NZ), (BX, 16, NZ), (BX, LOW, NZ)]
    inner_out = [tiles(BX)] * 4
    work = 20_000_000_000

    cy, cx = beside(*slabs)
    *state, source, dens = call(
        inner_first, inner_out + [tiles(DEPX), tiles(BX)], [VMEM] * 6, nat(DEPX), 32, work
    )(charge, *cy, density, *dy)
    out = call(
        flank_first,
        brick + [tiles(HIGH), tiles(HIGH), tiles(LOW), tiles(HIGH)],
        [VMEM] * 14,
        nat(DEPX) + spare,
        32,
    )(*state, source, dens, *cx, *dx)
    pot, slabs, halo = out[0], out[1:5], out[5:]
    for step in range(1, NEWTON):
        py, px = beside(*slabs)
        state = call(inner_next, inner_out, [VMEM] * 6, nat(BX), 32, work)(
            pot, *py, source, halo[0], dens
        )
        last = step == NEWTON - 1
        outs = [brick[0], (DEPX, DEPY, NZ)] if last else brick
        out = call(functools.partial(flank_next, last), outs, [VMEM] * 12, nat(DEPX) + spare, 32)(
            *state, *px, *halo
        )
        pot, slabs = out[0], out[1:]
    (grown,) = slabs
    (sums,) = call(read_kernel, [(PAN_DEV, 1, 128)], [VMEM] * 2, meta)(got, grown)
    back = lax.all_to_all(sums, everyone, split_axis=0, concat_axis=0, tiled=True)
    (picked,) = call(
        pick_kernel,
        [(APER_DEV, 1)],
        [SMEM] * 3 + [VMEM],
        [pltpu.VMEM((APER_DEV, 128), F32)],
    )(panel_brick, row_counts, aperture_panel, back)
    return pot, picked.reshape(APER_DEV)


def solution(mesh):
    everyone = P(("gx", "gy"))
    grid = P("gx", "gy", None)
    return jax.shard_map(
        on_device,
        mesh=mesh,
        in_specs=(grid, grid, P(("gx", "gy"), None)) + (everyone,) * 4,
        out_specs=(grid, everyone),
        check_vma=False,
    )
```

```python
import functools

import jax
import jax.numpy as jnp
from jax import lax
from jax.experimental import pallas as pl
from jax.experimental.pallas import tpu as pltpu
from jax.sharding import PartitionSpec as P

BX = 32
BY = 64
NZ = 128
NEWTON = 3
SWEEPS = 8
CAP = 4
BLX = 4
BLY = 4
BLZ = 8
N_GX = 16
N_GY = 8
PAN_DEV = 128
APER_DEV = 16
LOW = 8
HIGH = 11
TILES = 11
WY = 8 * TILES
NEAR = (10, 8)
FAR = (TILES, HIGH)
DEPX = BX + BLX - 1
DEPY = 72

VMEM = pl.BlockSpec(memory_space=pltpu.VMEM)
SMEM = pl.BlockSpec(memory_space=pltpu.SMEM)
F32 = jnp.float32


def call(body, outs, ins, scratch=(), mib=24, flops=None):
    cost = None
    if flops is not None:
        cost = pl.CostEstimate(flops=flops, bytes_accessed=1 << 20, transcendentals=0)
    return pl.pallas_call(
        body,
        out_shape=[jax.ShapeDtypeStruct(s, F32) for s in outs],
        in_specs=list(ins),
        out_specs=[VMEM] * len(outs),
        scratch_shapes=list(scratch),
        cost_estimate=cost,
        compiler_params=pltpu.CompilerParams(vmem_limit_bytes=mib << 20),
    )


def iota(shape, dim):
    return lax.broadcasted_iota(jnp.int32, shape, dim)


def pack_kernel(*refs):
    arrays, send, local, need, sems = refs[:5], refs[5], refs[6:11], refs[11], refs[12]
    copies = [pltpu.make_async_copy(a, b, sems.at[i]) for i, (a, b) in enumerate(zip(arrays, local))]
    for copy in copies:
        copy.start()
    brick, counts, offsets, aper, rows = local

    def clear(p, c):
        need[p] = 0
        return c

    lax.fori_loop(0, PAN_DEV, clear, 0, unroll=8)
    for copy in copies:
        copy.wait()
    for a in range(APER_DEV):
        need[aper[a]] = 1
    sub = iota((8, 128), 0)
    group = (iota((8, 128), 1) >> 3) & 3
    j = sub & 3
    masks = {e: (group == j - e) for e in range(-3, 4)}
    lane1 = iota((1, 128), 1)

    def body(q, c):
        p = q * 2
        live = sub < jnp.where(sub < 4, counts[p], counts[p + 1] + 4)
        v = jnp.where(live, rows[pl.ds(pl.multiple_of(q * 8, 8), 8), :], 0.0)
        out = v
        for e in (-3, -2, -1, 1, 2, 3):
            moved = pltpu.roll(pltpu.roll(v, e % 8, 0), (-8 * e) % 128, 1)
            out = jnp.where(masks[e], moved, out)
        for h in range(2):
            b = brick[p + h]
            send[b, 0:4, :] = out[4 * h : 4 * h + 4]
            meta = jnp.zeros((1, 128), jnp.int32)
            for k in range(CAP):
                meta = jnp.where(lane1 == k, offsets[(p + h) * CAP + k], meta)
            meta = jnp.where(lane1 == CAP, need[p + h], meta)
            send[b, 4:5, :] = meta.astype(F32)
        return c

    lax.fori_loop(0, PAN_DEV // 2, body, 0, unroll=2)


def corner(meta, p, k):
    offset = meta[p, k].astype(jnp.int32)
    return offset >> 13, (offset >> 7) & 63, offset & 127


def block_rows(v, z, k, i, lane):
    moved = pltpu.roll(v, (z - 32 * i - 8 * k + 128) & 127, 1)
    return jnp.where((lane >= z) & (lane < z + BLZ), moved, 0.0)


def deposit_kernel(got, ion, out, x_low, x_high, y_low, y_high, meta, sem):
    copy = pltpu.make_async_copy(got.at[:, 4, :], meta, sem)
    copy.start()
    out[0:BX, 0:BY, :] = ion[...]
    out[0:BX, BY:DEPY, :] = jnp.zeros((BX, DEPY - BY, NZ), F32)
    out[BX:DEPX] = jnp.zeros((DEPX - BX, DEPY, NZ), F32)
    lane = iota((BLY, 128), 1)
    copy.wait()

    def body(p, c):
        v = got[p, 0:4, :]
        for k in range(CAP):
            x, y, z = corner(meta, p, k)
            add = [block_rows(v, z, k, i, lane) for i in range(BLX)]
            old = [out[x + i, pl.ds(y, BLY), :] for i in range(BLX)]
            for i in range(BLX):
                out[x + i, pl.ds(y, BLY), :] = old[i] + add[i]
        return c

    lax.fori_loop(0, PAN_DEV, body, 0, unroll=8)
    x_low[...] = out[0:HIGH]
    x_high[...] = out[BX - LOW : DEPX]
    y_low[...] = out[:, 0:16]
    y_high[...] = out[:, BY - LOW : DEPY]


def inside_y(tiles):
    gy = lax.axis_index("gy")
    lo = jnp.where(gy == 0, LOW, 0)
    hi = jnp.where(gy == N_GY - 1, LOW + BY, WY)
    sub = iota((8, 128), 0)
    ys = [sub * tiles + t for t in range(tiles)]
    return [(y >= lo) & (y < hi) for y in ys]


def lay(nat, at, count, own, below, above):
    nat[at : at + count, 0:LOW] = below
    nat[at : at + count, LOW : LOW + BY] = own
    nat[at : at + count, LOW + BY : LOW + BY + above.shape[1]] = above


def lay_charge(nat, at, count, own, below, above):
    spread = jnp.where(lax.axis_index("gy") > 0, 1.0, 0.0)
    nat[at : at + count, 0:LOW] = below[:, 0:LOW]
    nat[at : at + count, LOW : LOW + DEPY] = own
    nat[at : at + count, LOW : LOW + 8] += below[:, LOW : LOW + 8] * spread
    nat[at : at + count, LOW + BY : LOW + DEPY] += above[:, 0:8]
    nat[at : at + count, LOW + DEPY : WY] = above[:, 8:16]


def strided(nat, x, t, tiles):
    return nat[x, pl.ds(t, 8, stride=tiles), :]


def relax(layers, write):
    tiles = len(layers[0])
    lane = iota((8, 128), 1)
    first, last = lane == 0, lane == NZ - 1
    for u in range(len(layers) - 2):
        prev, cur, nxt = layers[u : u + 3]
        before = [pltpu.roll(cur[-1], 1, 0)] + cur[:-1]
        after = cur[1:] + [pltpu.roll(cur[0], 7, 0)]
        for t in range(tiles):
            left = jnp.where(first, 0.0, pltpu.roll(cur[t], 1, 1))
            right = jnp.where(last, 0.0, pltpu.roll(cur[t], NZ - 1, 1))
            total = (prev[t] + nxt[t]) + (before[t] + after[t]) + (left + right)
            write(u, t, total)


def layer(buf, x):
    return [buf[x, t] for t in range(buf.shape[1])]


def sweep(src, dst, rhs, inv, lo, hi):
    def rows(x0, count):
        def write(u, t, total):
            dst[x0 + u, t] = (rhs[x0 + u, t] + total) * inv[x0 + u, t]

        relax([layer(src, x0 - 1 + u) for u in range(count + 2)], write)

    count = (hi - lo + 1) // 2

    def body(i, c):
        rows(lo + i * count, count)
        return c

    lax.fori_loop(0, (hi - lo) // count, body, 0)
    if (hi - lo) % count:
        rows(lo + count, (hi - lo) % count)


def inner(b0, b1, rhs, inv, k0, a, h):
    bufs = (b0, b1)
    for k in range(k0, SWEEPS + 1):
        sweep(bufs[(k - 1) % 2], bufs[k % 2], rhs, inv, a + k, h - k)


def inner_first(charge, y_below, y_above, density, d_below, d_above, *refs):
    b0, b1, rhs, inv, source, dens = refs
    tiles = b0.shape[1]
    inside = inside_y(tiles)
    lay(dens, 0, BX, density[...], d_below[...], d_above[...])
    lay_charge(source, 0, DEPX, charge[...], y_below, y_above)

    def prep(x, c):
        for t in range(tiles):
            s = strided(source, x, t, tiles)
            d = strided(dens, x, t, tiles)
            scale = jnp.where(inside[t], 1.0 / (6.0 + d), 0.0)
            inv[x, t] = scale
            rhs[x, t] = s - d
            b1[x, t] = (s - d) * scale
        return c

    lax.fori_loop(0, BX, prep, 0, unroll=2)
    inner(b0, b1, rhs, inv, 2, BLX - 2, BX + 1)


def start(p_nat, s, s_at, d, inside, f, outs, to, x):
    p_out, rhs, inv = outs
    tiles = p_out.shape[1]
    for t in range(tiles):
        p = jnp.where(inside[t], strided(p_nat, x, t, tiles) * f, 0.0)
        coef = strided(d, x, t, tiles) * jnp.exp(p)
        p_out[x + to, t] = p
        rhs[x + to, t] = strided(s, x + s_at, t, tiles) + coef * (p - 1.0)
        inv[x + to, t] = jnp.where(inside[t], f / (6.0 + coef), 0.0)


def inner_next(own, y_below, y_above, source, s_low, dens, b0, b1, rhs, inv, nat):
    inside = inside_y(b0.shape[1])
    lay(nat, 0, BX, own[...], y_below[...], y_above[...])
    outs = (b0, rhs, inv)

    def prep_from(src, at):
        def prep(x, c):
            start(nat, src, at, dens, inside, 1.0, outs, 0, x)
            return c

        return prep

    lax.fori_loop(0, BLX - 1, prep_from(s_low, LOW), 0)
    lax.fori_loop(BLX - 1, BX, prep_from(source, 0), 0)
    inner(b0, b1, rhs, inv, 1, 0, BX)


def flanks(b0, b1, lows, highs, rhs, inv, k0, a, h, over):
    (l0, l1, l_rhs, l_inv), (h0, h1, h_rhs, h_inv) = lows, highs
    n_low, n_high = LOW + a, BX + over - h
    for i in range(LOW + a):
        if i + LOW >= len_low_halo(a):
            l_rhs[i + LOW], l_inv[i + LOW] = rhs[i], inv[i]
    for i in range(h - LOW, BX):
        h_rhs[i - (h - LOW)], h_inv[i - (h - LOW)] = rhs[i], inv[i]

    def one(k, near, l_src, l_dst, h_src, h_dst):
        def low_write(u, t, total):
            l_dst[k + u, t] = (l_rhs[k + u, t] + total) * l_inv[k + u, t]

        def high_write(u, t, total):
            r = LOW - k + u
            h_dst[r, t] = (h_rhs[r, t] + total) * h_inv[r, t]

        low = [layer(l_src, k - 1 + j) for j in range(n_low)]
        relax(low + [layer(near, a + k - 1), layer(near, a + k)], low_write)
        high = [layer(h_src, LOW + 1 - k + j) for j in range(n_high)]
        relax([layer(near, h - k - 1), layer(near, h - k)] + high, high_write)

    if k0 == 2:
        one(2, b1, l1, l0, h1, h0)

    def body(j, c):
        one(2 * j + 1, b0, l0, l1, h0, h1)
        one(2 * j + 2, b1, l1, l0, h1, h0)
        return c

    lax.fori_loop(k0 - 1, SWEEPS // 2, body, 0)


def len_low_halo(a):
    return LOW + (BLX - 1 if a else 0)


def finish(b0, l0, h0, nat, a, h, stop):
    tiles = b0.shape[1]

    def take(src, shift):
        def body(x, c):
            for t in range(tiles):
                nat[x, pl.ds(t, 8, stride=tiles), :] = src[x + shift, t]
            return c

        return body

    lax.fori_loop(0, a + LOW, take(l0, LOW), 0, unroll=2)
    lax.fori_loop(a + LOW, h - LOW, take(b0, 0), 0, unroll=2)
    lax.fori_loop(h - LOW, stop, take(h0, LOW - h), 0, unroll=2)


def hand_on(nat, out, x_low, x_high, y_low, y_high):
    out[...] = nat[0:BX, LOW : LOW + BY]
    x_low[...] = nat[0 : x_low.shape[0], LOW : LOW + BY]
    x_high[...] = nat[BX - LOW : BX, LOW : LOW + BY]
    y_low[...] = nat[0:BX, LOW : LOW + y_low.shape[1]]
    y_high[...] = nat[0:BX, BY : LOW + BY]


def edges():
    gx = lax.axis_index("gx")
    return jnp.where(gx > 0, 1.0, 0.0), jnp.where(gx < N_GX - 1, 1.0, 0.0)


def flank_first(*refs):
    b0, b1, rhs, inv, source, dens, x_below, x_above, d_below, d_above = refs[:10]
    outs, (s_low, s_high), nat, spare = refs[10:15], refs[15:17], refs[17], refs[18:]
    l0, l1, l_rhs, l_inv, h0, h1, h_rhs, h_inv = spare
    a, h = BLX - 2, BX + 1
    tiles, over = NEAR
    inside, (f_low, f_high) = inside_y(tiles), edges()
    s_low[...] = x_below[...]
    s_low[LOW:HIGH] = source[0 : HIGH - LOW] + x_below[LOW:HIGH] * f_low
    s_high[...] = x_above[...]
    s_high[0 : DEPX - BX] += source[BX:DEPX]

    def fill(count, s, s_at, d, d_at, f, at, p_out, rhs_out, inv_out):
        def body(r, c):
            for t in range(tiles):
                den = strided(d, r + d_at, t, tiles)
                scale = jnp.where(inside[t], f / (6.0 + den), 0.0)
                value = strided(s, r + s_at, t, tiles) - den
                rhs_out[r + at, t], inv_out[r + at, t] = value, scale
                p_out[r + at, t] = value * scale
            return c

        lax.fori_loop(0, count, body, 0)

    fill(LOW, s_low, 0, d_below, 0, f_low, 0, l1, l_rhs, l_inv)
    fill(BLX - 1, s_low, LOW, dens, 0, 1.0, LOW, l1, l_rhs, l_inv)
    fill(over, s_high, 0, d_above, 0, f_high, LOW - 1, h1, h_rhs, h_inv)
    lows, highs = (l0, l1, l_rhs, l_inv), (h0, h1, h_rhs, h_inv)
    flanks(b0, b1, lows, highs, rhs, inv, 2, a, h, over)
    finish(b0, l0, h0, nat, a, h, BX)
    hand_on(nat, *outs)


def next_flanks(refs, nat, spare, over):
    b0, b1, rhs, inv, x_below, x_above, s_low, s_high, d_low, d_high = refs
    l0, l1, l_rhs, l_inv, h0, h1, h_rhs, h_inv = spare
    inside, (f_low, f_high) = inside_y(b0.shape[1]), edges()

    def low_body(r, c):
        start(x_below, s_low, 0, d_low, inside, f_low, (l0, l_rhs, l_inv), 0, r)
        return c

    def high_body(r, c):
        start(x_above, s_high, 0, d_high, inside, f_high, (h0, h_rhs, h_inv), LOW, r)
        return c

    lax.fori_loop(0, LOW, low_body, 0)
    lax.fori_loop(0, over, high_body, 0)
    lows, highs = (l0, l1, l_rhs, l_inv), (h0, h1, h_rhs, h_inv)
    flanks(b0, b1, lows, highs, rhs, inv, 1, 0, BX, over)
    finish(b0, l0, h0, nat, 0, BX, BX + over - LOW)


def flank_next(*refs):
    outs, (nat, *spare) = refs[10:15], refs[15:]
    next_flanks(refs[:10], nat, spare, NEAR[1])
    hand_on(nat, *outs)


def flank_last(*refs):
    got, out, sums, nat, spare, (meta, sem, named) = refs[10], refs[11], refs[12], refs[13], refs[14:22], refs[22:]
    copy = pltpu.make_async_copy(got.at[:, 4, :], meta, sem)
    copy.start()
    next_flanks(refs[:10], nat, spare, HIGH)
    out[...] = nat[0:BX, LOW : LOW + BY]
    copy.wait()
    read(got, nat, sums, meta, named)


def slab_kernel(x_low, x_high, below, above, low, high):
    for own, at, slab in ((x_low, 0, low), (x_high, BX - LOW, high)):
        n, width = slab.shape[0], slab.shape[1]
        slab[:, 0:LOW] = below[at : at + n]
        slab[:, LOW : LOW + BY] = own[...]
        slab[:, LOW + BY : width] = above[at : at + n]


def charge_slab_kernel(x_low, x_high, below, above, low, high):
    for own, at, slab in ((x_low, 0, low), (x_high, BX - LOW, high)):
        lay_charge(slab, 0, HIGH, own[...], below[at : at + HIGH], above[at : at + HIGH])


def beside(body, width, x_low, x_high, y_low, y_high):
    y_below, y_above = ring(y_high, "gy", 1), ring(y_low, "gy", -1)
    low, high = call(
        body, [(x_low.shape[0], width, NZ), (x_high.shape[0], width, NZ)], [VMEM] * 4
    )(x_low, x_high, y_below, y_above)
    x_below, x_above = ring(high, "gx", 1), ring(low, "gx", -1)
    return (y_below, y_above), (x_below, x_above)


def read(got, field, out, meta, named):
    lane = iota((BLY, 128), 1)

    def note(p, n):
        named[n] = p
        return n + meta[p, CAP].astype(jnp.int32)

    count = lax.fori_loop(0, PAN_DEV, note, 0, unroll=8)
    named[count] = 0

    def body(j, c):
        for u in range(2):
            p = named[2 * j + u]
            v = got[p, 0:4, :]
            total = jnp.zeros((BLY, 128), F32)
            for k in range(CAP):
                x, y, z = corner(meta, p, k)
                for i in range(BLX):
                    piece = field[x + i, pl.ds(y + LOW, BLY), :]
                    total += block_rows(v, z, k, i, lane) * piece
            out[p] = jnp.sum(total, axis=0, keepdims=True)
        return c

    lax.fori_loop(0, (count + 1) // 2, body, 0)


def pick_kernel(brick, counts, aper, got, out, rows):
    sub = iota((1, APER_DEV), 1)
    live = jnp.ones((1, APER_DEV), F32)
    for a in range(APER_DEV):
        p = aper[a]
        rows[a : a + 1, :] = got[brick[p]]
        live = jnp.where(sub == a, counts[p].astype(F32), live)
    out[...] = jnp.sum(rows[...], axis=1) / live[0]


def ring(array, axis, by):
    size = lax.axis_size(axis)
    return lax.ppermute(array, axis, [(i, (i + by) % size) for i in range(size)])


def on_device(
    ion_charge, density, charge_blocks, panel_brick, row_counts, block_offset, aperture_panel
):
    everyone = ("gx", "gy")
    ints = [pltpu.SMEM((n,), jnp.int32) for n in (PAN_DEV, PAN_DEV, PAN_DEV * CAP, APER_DEV)]
    (send,) = call(
        pack_kernel,
        [(PAN_DEV, 8, 128)],
        [pl.BlockSpec(memory_space=pl.ANY)] * 5,
        ints
        + [
            pltpu.VMEM((PAN_DEV * CAP, 128), F32),
            pltpu.SMEM((PAN_DEV,), jnp.int32),
            pltpu.SemaphoreType.DMA((5,)),
        ],
    )(panel_brick, row_counts, block_offset, aperture_panel, charge_blocks)
    got = lax.all_to_all(send, everyone, split_axis=0, concat_axis=0, tiled=True)
    dy, dx = beside(
        slab_kernel, WY, density[:HIGH], density[BX - LOW :], density[:, :16], density[:, BY - LOW :]
    )

    meta = [pltpu.SMEM((PAN_DEV, 128), F32), pltpu.SemaphoreType.DMA]
    charge, *slabs = call(
        deposit_kernel,
        [(DEPX, DEPY, NZ)] + [(HIGH, DEPY, NZ)] * 2 + [(DEPX, 16, NZ)] * 2,
        [VMEM] * 2,
        meta,
    )(got, ion_charge)

    def tiles(n, width):
        return (n, width, 8, NZ)

    def layers(n):
        return pltpu.VMEM((n, WY, NZ), F32)

    def brick(over, width):
        return [(BX, BY, NZ), (over, BY, NZ), (LOW, BY, NZ), (BX, width, NZ), (BX, LOW, NZ)]

    def spare(width):
        return [pltpu.VMEM(tiles(LOW + LOW + BLX, width), F32)] * 8

    near, far = NEAR[0], FAR[0]
    work = 20_000_000_000
    cy, cx = beside(charge_slab_kernel, WY, *slabs)
    *state, source, dens = call(
        inner_first,
        [tiles(BX, near)] * 4 + [(DEPX, WY, NZ), (BX, WY, NZ)],
        [VMEM] * 6,
        (),
        32,
        work,
    )(charge, *cy, density, *dy)
    next_brick = brick(NEAR[1], 8)
    pot, *slabs, s_low, s_high = call(
        flank_first,
        next_brick + [(HIGH, WY, NZ)] * 2,
        [VMEM] * 10,
        [layers(DEPX)] + spare(near),
        32,
    )(*state, source, dens, *cx, *dx)
    for width, over in (NEAR, FAR):
        py, px = beside(slab_kernel, 8 * width, *slabs)
        state = call(inner_next, [tiles(BX, width)] * 4, [VMEM] * 6, [layers(BX)], 32, work)(
            pot, *py, source, s_low, dens
        )
        operands = (*state, *px, s_low, s_high, *dx)
        if over < HIGH:
            pot, *slabs = call(
                flank_next, brick(HIGH, 16), [VMEM] * 10, [layers(DEPX)] + spare(width), 32
            )(*operands)
    pot, sums = call(
        flank_last,
        [(BX, BY, NZ), (PAN_DEV, 1, 128)],
        [VMEM] * 11,
        [layers(DEPX)] + spare(far) + meta + [pltpu.SMEM((PAN_DEV + 8,), jnp.int32)],
        32,
    )(*operands, got)
    back = lax.all_to_all(sums, everyone, split_axis=0, concat_axis=0, tiled=True)
    (picked,) = call(
        pick_kernel,
        [(APER_DEV,)],
        [SMEM] * 3 + [VMEM],
        [pltpu.VMEM((APER_DEV, 128), F32)],
    )(panel_brick, row_counts, aperture_panel, back)
    return pot, picked


def solution(mesh):
    everyone = P(("gx", "gy"))
    grid = P("gx", "gy", None)
    return jax.shard_map(
        on_device,
        mesh=mesh,
        in_specs=(grid, grid, P(("gx", "gy"), None)) + (everyone,) * 4,
        out_specs=(grid, everyone),
        check_vma=False,
    )
```

```python
import functools

import jax
import jax.numpy as jnp
from jax import lax
from jax.experimental import pallas as pl
from jax.experimental.pallas import tpu as pltpu
from jax.sharding import PartitionSpec as P

BX = 32
BY = 64
NZ = 128
NEWTON = 3
SWEEPS = 8
CAP = 4
BLX = 4
BLY = 4
BLZ = 8
N_GX = 16
N_GY = 8
PAN_DEV = 128
APER_DEV = 16
LOW = 8
HIGH = 11
TILES = 11
WY = 8 * TILES
NEAR = (10, 8)
FAR = (TILES, HIGH)
DEPX = BX + BLX - 1
DEPY = 72

VMEM = pl.BlockSpec(memory_space=pltpu.VMEM)
SMEM = pl.BlockSpec(memory_space=pltpu.SMEM)
ANY = pl.BlockSpec(memory_space=pl.ANY)
F32 = jnp.float32


def call(body, outs, ins, scratch=(), mib=24, flops=None):
    cost = None
    if flops is not None:
        cost = pl.CostEstimate(flops=flops, bytes_accessed=1 << 20, transcendentals=0)
    return pl.pallas_call(
        body,
        out_shape=[jax.ShapeDtypeStruct(s, F32) for s in outs],
        in_specs=list(ins),
        out_specs=[VMEM] * len(outs),
        scratch_shapes=list(scratch),
        cost_estimate=cost,
        compiler_params=pltpu.CompilerParams(vmem_limit_bytes=mib << 20),
    )


def iota(shape, dim):
    return lax.broadcasted_iota(jnp.int32, shape, dim)


def pack_kernel(*refs):
    arrays, send, local, need, sems = refs[:5], refs[5], refs[6:11], refs[11], refs[12]
    copies = [pltpu.make_async_copy(a, b, sems.at[i]) for i, (a, b) in enumerate(zip(arrays, local))]
    for copy in copies:
        copy.start()
    brick, counts, offsets, aper, rows = local

    def clear(p, c):
        need[p] = 0
        return c

    lax.fori_loop(0, PAN_DEV, clear, 0, unroll=8)
    for copy in copies:
        copy.wait()
    for a in range(APER_DEV):
        need[aper[a]] = 1
    sub = iota((8, 128), 0)
    group = (iota((8, 128), 1) >> 3) & 3
    j = sub & 3
    masks = {e: (group == j - e) for e in range(-3, 4)}
    lane1 = iota((1, 128), 1)

    def body(q, c):
        p = q * 2
        live = sub < jnp.where(sub < 4, counts[p], counts[p + 1] + 4)
        v = jnp.where(live, rows[pl.ds(pl.multiple_of(q * 8, 8), 8), :], 0.0)
        out = v
        for e in (-3, -2, -1, 1, 2, 3):
            moved = pltpu.roll(pltpu.roll(v, e % 8, 0), (-8 * e) % 128, 1)
            out = jnp.where(masks[e], moved, out)
        for h in range(2):
            b = brick[p + h]
            send[b, 0:4, :] = out[4 * h : 4 * h + 4]
            meta = jnp.zeros((1, 128), jnp.int32)
            for k in range(CAP):
                meta = jnp.where(lane1 == k, offsets[(p + h) * CAP + k], meta)
            meta = jnp.where(lane1 == CAP, need[p + h], meta)
            send[b, 4:5, :] = meta.astype(F32)
        return c

    lax.fori_loop(0, PAN_DEV // 2, body, 0, unroll=4)


def corner(meta, p, k):
    offset = meta[p, k].astype(jnp.int32)
    return offset >> 13, (offset >> 7) & 63, offset & 127


def block_rows(v, z, k, i, lane):
    moved = pltpu.roll(v, (z - 32 * i - 8 * k + 128) & 127, 1)
    return jnp.where((lane >= z) & (lane < z + BLZ), moved, 0.0)


def deposit_kernel(got, ion, unused_low, unused_high, out, x_low, x_high, y_low, y_high, meta, sem):
    copy = pltpu.make_async_copy(got.at[:, 4, :], meta, sem)
    copy.start()
    out[0:BX, 0:BY, :] = ion[...]
    out[0:BX, BY:DEPY, :] = jnp.zeros((BX, DEPY - BY, NZ), F32)
    out[BX:DEPX] = jnp.zeros((DEPX - BX, DEPY, NZ), F32)
    lane = iota((BLY, 128), 1)
    copy.wait()

    def body(p, c):
        v = got[p, 0:4, :]
        for k in range(CAP):
            x, y, z = corner(meta, p, k)
            add = [block_rows(v, z, k, i, lane) for i in range(BLX)]
            old = [out[x + i, pl.ds(y, BLY), :] for i in range(BLX)]
            for i in range(BLX):
                out[x + i, pl.ds(y, BLY), :] = old[i] + add[i]
        return c

    lax.fori_loop(0, PAN_DEV, body, 0, unroll=8)
    x_low[...] = out[0:HIGH]
    x_high[...] = out[BX - LOW : DEPX]
    y_low[...] = out[:, 0:16]
    y_high[...] = out[:, BY - LOW : DEPY]


def inside_y(tiles):
    gy = lax.axis_index("gy")
    lo = jnp.where(gy == 0, LOW, 0)
    hi = jnp.where(gy == N_GY - 1, LOW + BY, WY)
    sub = iota((8, 128), 0)
    ys = [sub * tiles + t for t in range(tiles)]
    return [(y >= lo) & (y < hi) for y in ys]


def lay(nat, at, count, own, below, above):
    nat[at : at + count, 0:LOW] = below
    nat[at : at + count, LOW : LOW + BY] = own
    nat[at : at + count, LOW + BY : LOW + BY + above.shape[1]] = above


def lay_charge(nat, at, count, own, below, above):
    spread = jnp.where(lax.axis_index("gy") > 0, 1.0, 0.0)
    nat[at : at + count, 0:LOW] = below[:, 0:LOW]
    nat[at : at + count, LOW : LOW + DEPY] = own
    nat[at : at + count, LOW : LOW + 8] += below[:, LOW : LOW + 8] * spread
    nat[at : at + count, LOW + BY : LOW + DEPY] += above[:, 0:8]
    nat[at : at + count, LOW + DEPY : WY] = above[:, 8:16]


def strided(nat, x, t, tiles):
    return nat[x, pl.ds(t, 8, stride=tiles), :]


def relax(layers, write):
    tiles = len(layers[0])
    lane = iota((8, 128), 1)
    first, last = lane == 0, lane == NZ - 1
    for u in range(len(layers) - 2):
        prev, cur, nxt = layers[u : u + 3]
        before = [pltpu.roll(cur[-1], 1, 0)] + cur[:-1]
        after = cur[1:] + [pltpu.roll(cur[0], 7, 0)]
        for t in range(tiles):
            left = jnp.where(first, 0.0, pltpu.roll(cur[t], 1, 1))
            right = jnp.where(last, 0.0, pltpu.roll(cur[t], NZ - 1, 1))
            total = (prev[t] + nxt[t]) + (before[t] + after[t]) + (left + right)
            write(u, t, total)


def layer(buf, x):
    return [buf[x, t] for t in range(buf.shape[1])]


def sweep(src, dst, rhs, inv, lo, hi):
    def rows(x0, count):
        def write(u, t, total):
            dst[x0 + u, t] = (rhs[x0 + u, t] + total) * inv[x0 + u, t]

        relax([layer(src, x0 - 1 + u) for u in range(count + 2)], write)

    count = (hi - lo + 1) // 2

    def body(i, c):
        rows(lo + i * count, count)
        return c

    lax.fori_loop(0, (hi - lo) // count, body, 0)
    if (hi - lo) % count:
        rows(lo + count, (hi - lo) % count)


def inner(b0, b1, rhs, inv, k0, a, h):
    bufs = (b0, b1)
    for k in range(k0, SWEEPS + 1):
        sweep(bufs[(k - 1) % 2], bufs[k % 2], rhs, inv, a + k, h - k)


def inner_first(charge, y_below, y_above, density, d_below, d_above, *refs):
    b0, b1, rhs, inv, source, dens = refs
    tiles = b0.shape[1]
    inside = inside_y(tiles)
    lay(dens, 0, BX, density[...], d_below[...], d_above[...])
    lay_charge(source, 0, DEPX, charge[...], y_below, y_above)

    def prep(x, c):
        for t in range(tiles):
            s = strided(source, x, t, tiles)
            d = strided(dens, x, t, tiles)
            scale = jnp.where(inside[t], 1.0 / (6.0 + d), 0.0)
            inv[x, t] = scale
            rhs[x, t] = s - d
            b1[x, t] = (s - d) * scale
        return c

    lax.fori_loop(0, BX, prep, 0, unroll=2)
    inner(b0, b1, rhs, inv, 2, BLX - 2, BX + 1)


def start(p_nat, s, s_at, d, inside, f, outs, to, x):
    p_out, rhs, inv = outs
    tiles = p_out.shape[1]
    for t in range(tiles):
        p = jnp.where(inside[t], strided(p_nat, x, t, tiles) * f, 0.0)
        coef = strided(d, x, t, tiles) * jnp.exp(p)
        p_out[x + to, t] = p
        rhs[x + to, t] = strided(s, x + s_at, t, tiles) + coef * (p - 1.0)
        inv[x + to, t] = jnp.where(inside[t], f / (6.0 + coef), 0.0)


def inner_next(own, y_below, y_above, source, s_low, dens, b0, b1, rhs, inv, nat):
    inside = inside_y(b0.shape[1])
    lay(nat, 0, BX, own[...], y_below[...], y_above[...])
    outs = (b0, rhs, inv)

    def prep_from(src, at):
        def prep(x, c):
            start(nat, src, at, dens, inside, 1.0, outs, 0, x)
            return c

        return prep

    lax.fori_loop(0, BLX - 1, prep_from(s_low, LOW), 0)
    lax.fori_loop(BLX - 1, BX, prep_from(source, 0), 0)
    inner(b0, b1, rhs, inv, 1, 0, BX)


def flanks(b0, b1, lows, highs, rhs, inv, k0, a, h, over):
    (l0, l1, l_rhs, l_inv), (h0, h1, h_rhs, h_inv) = lows, highs
    n_low, n_high = LOW + a, BX + over - h
    for i in range(LOW + a):
        if i + LOW >= len_low_halo(a):
            l_rhs[i + LOW], l_inv[i + LOW] = rhs[i], inv[i]
    for i in range(h - LOW, BX):
        h_rhs[i - (h - LOW)], h_inv[i - (h - LOW)] = rhs[i], inv[i]

    def one(k, near, l_src, l_dst, h_src, h_dst):
        def low_write(u, t, total):
            l_dst[k + u, t] = (l_rhs[k + u, t] + total) * l_inv[k + u, t]

        def high_write(u, t, total):
            r = LOW - k + u
            h_dst[r, t] = (h_rhs[r, t] + total) * h_inv[r, t]

        low = [layer(l_src, k - 1 + j) for j in range(n_low)]
        relax(low + [layer(near, a + k - 1), layer(near, a + k)], low_write)
        high = [layer(h_src, LOW + 1 - k + j) for j in range(n_high)]
        relax([layer(near, h - k - 1), layer(near, h - k)] + high, high_write)

    if k0 == 2:
        one(2, b1, l1, l0, h1, h0)

    def body(j, c):
        one(2 * j + 1, b0, l0, l1, h0, h1)
        one(2 * j + 2, b1, l1, l0, h1, h0)
        return c

    lax.fori_loop(k0 - 1, SWEEPS // 2, body, 0)


def len_low_halo(a):
    return LOW + (BLX - 1 if a else 0)


def finish(b0, l0, h0, nat, a, h, stop):
    tiles = b0.shape[1]

    def take(src, shift):
        def body(x, c):
            for t in range(tiles):
                nat[x, pl.ds(t, 8, stride=tiles), :] = src[x + shift, t]
            return c

        return body

    lax.fori_loop(0, a + LOW, take(l0, LOW), 0, unroll=2)
    lax.fori_loop(a + LOW, h - LOW, take(b0, 0), 0, unroll=2)
    lax.fori_loop(h - LOW, stop, take(h0, LOW - h), 0, unroll=2)


def hand_on(nat, out, x_low, x_high, y_low, y_high):
    out[...] = nat[0:BX, LOW : LOW + BY]
    x_low[...] = nat[0 : x_low.shape[0], LOW : LOW + BY]
    x_high[...] = nat[BX - LOW : BX, LOW : LOW + BY]
    y_low[...] = nat[0:BX, LOW : LOW + y_low.shape[1]]
    y_high[...] = nat[0:BX, BY : LOW + BY]


def edges():
    gx = lax.axis_index("gx")
    return jnp.where(gx > 0, 1.0, 0.0), jnp.where(gx < N_GX - 1, 1.0, 0.0)


def flank_first(*refs):
    b0, b1, rhs, inv, source, dens, x_below, x_above, d_below, d_above = refs[:10]
    outs, (s_low, s_high), nat, spare = refs[10:15], refs[15:17], refs[17], refs[18:]
    l0, l1, l_rhs, l_inv, h0, h1, h_rhs, h_inv = spare
    a, h = BLX - 2, BX + 1
    tiles, over = NEAR
    inside, (f_low, f_high) = inside_y(tiles), edges()
    s_low[...] = x_below[...]
    s_low[LOW:HIGH] = source[0 : HIGH - LOW] + x_below[LOW:HIGH] * f_low
    s_high[...] = x_above[...]
    s_high[0 : DEPX - BX] += source[BX:DEPX]

    def fill(count, s, s_at, d, d_at, f, at, p_out, rhs_out, inv_out):
        def body(r, c):
            for t in range(tiles):
                den = strided(d, r + d_at, t, tiles)
                scale = jnp.where(inside[t], f / (6.0 + den), 0.0)
                value = strided(s, r + s_at, t, tiles) - den
                rhs_out[r + at, t], inv_out[r + at, t] = value, scale
                p_out[r + at, t] = value * scale
            return c

        lax.fori_loop(0, count, body, 0)

    fill(LOW, s_low, 0, d_below, 0, f_low, 0, l1, l_rhs, l_inv)
    fill(BLX - 1, s_low, LOW, dens, 0, 1.0, LOW, l1, l_rhs, l_inv)
    fill(over, s_high, 0, d_above, 0, f_high, LOW - 1, h1, h_rhs, h_inv)
    lows, highs = (l0, l1, l_rhs, l_inv), (h0, h1, h_rhs, h_inv)
    flanks(b0, b1, lows, highs, rhs, inv, 2, a, h, over)
    finish(b0, l0, h0, nat, a, h, BX)
    hand_on(nat, *outs)


def next_flanks(refs, nat, spare, over):
    b0, b1, rhs, inv, x_below, x_above, s_low, s_high, d_low, d_high = refs
    l0, l1, l_rhs, l_inv, h0, h1, h_rhs, h_inv = spare
    inside, (f_low, f_high) = inside_y(b0.shape[1]), edges()

    def low_body(r, c):
        start(x_below, s_low, 0, d_low, inside, f_low, (l0, l_rhs, l_inv), 0, r)
        return c

    def high_body(r, c):
        start(x_above, s_high, 0, d_high, inside, f_high, (h0, h_rhs, h_inv), LOW, r)
        return c

    lax.fori_loop(0, LOW, low_body, 0)
    lax.fori_loop(0, over, high_body, 0)
    lows, highs = (l0, l1, l_rhs, l_inv), (h0, h1, h_rhs, h_inv)
    flanks(b0, b1, lows, highs, rhs, inv, 1, 0, BX, over)
    finish(b0, l0, h0, nat, 0, BX, BX + over - LOW)


def flank_next(*refs):
    outs, (nat, *spare) = refs[10:15], refs[15:]
    next_flanks(refs[:10], nat, spare, NEAR[1])
    hand_on(nat, *outs)


def flank_last(*refs):
    got, out, sums, nat, spare, (meta, sem, named) = refs[10], refs[11], refs[12], refs[13], refs[14:22], refs[22:]
    copy = pltpu.make_async_copy(got.at[:, 4, :], meta, sem)
    copy.start()
    next_flanks(refs[:10], nat, spare, HIGH)
    out[...] = nat[0:BX, LOW : LOW + BY]
    copy.wait()
    read(got, nat, sums, meta, named)


def slab_kernel(x_low, x_high, below, above, low, high):
    for own, at, slab in ((x_low, 0, low), (x_high, BX - LOW, high)):
        n, width = slab.shape[0], slab.shape[1]
        slab[:, 0:LOW] = below[at : at + n]
        slab[:, LOW : LOW + BY] = own[...]
        slab[:, LOW + BY : width] = above[at : at + n]


def charge_slab_kernel(x_low, x_high, below, above, unused_low, unused_high, low, high):
    for own, at, slab in ((x_low, 0, low), (x_high, BX - LOW, high)):
        lay_charge(slab, 0, HIGH, own[...], below[at : at + HIGH], above[at : at + HIGH])


def beside(body, width, x_low, x_high, y_low, y_high, first=()):
    y_below, y_above = ring(y_high, "gy", 1), ring(y_low, "gy", -1)
    low, high = call(
        body, [(x_low.shape[0], width, NZ), (x_high.shape[0], width, NZ)], [VMEM] * 4 + [ANY] * len(first)
    )(x_low, x_high, y_below, y_above, *first)
    x_below, x_above = ring(high, "gx", 1), ring(low, "gx", -1)
    return (y_below, y_above), (x_below, x_above), (low, high)


def read(got, field, out, meta, named):
    lane = iota((BLY, 128), 1)

    def note(p, n):
        named[n] = p
        return n + meta[p, CAP].astype(jnp.int32)

    count = lax.fori_loop(0, PAN_DEV, note, 0, unroll=8)
    named[count] = 0

    def body(j, c):
        for u in range(2):
            p = named[2 * j + u]
            v = got[p, 0:4, :]
            total = jnp.zeros((BLY, 128), F32)
            for k in range(CAP):
                x, y, z = corner(meta, p, k)
                for i in range(BLX):
                    piece = field[x + i, pl.ds(y + LOW, BLY), :]
                    total += block_rows(v, z, k, i, lane) * piece
            out[p] = jnp.sum(total, axis=0, keepdims=True)
        return c

    lax.fori_loop(0, (count + 1) // 2, body, 0)


def pick_kernel(brick, counts, aper, got, out, rows):
    sub = iota((1, APER_DEV), 1)
    live = jnp.ones((1, APER_DEV), F32)
    for a in range(APER_DEV):
        p = aper[a]
        rows[a : a + 1, :] = got[brick[p]]
        live = jnp.where(sub == a, counts[p].astype(F32), live)
    out[...] = jnp.sum(rows[...], axis=1) / live[0]


def ring(array, axis, by):
    size = lax.axis_size(axis)
    return lax.ppermute(array, axis, [(i, (i + by) % size) for i in range(size)])


def on_device(
    ion_charge, density, charge_blocks, panel_brick, row_counts, block_offset, aperture_panel
):
    everyone = ("gx", "gy")
    ints = [pltpu.SMEM((n,), jnp.int32) for n in (PAN_DEV, PAN_DEV, PAN_DEV * CAP, APER_DEV)]
    (send,) = call(
        pack_kernel,
        [(PAN_DEV, 8, 128)],
        [ANY] * 5,
        ints
        + [
            pltpu.VMEM((PAN_DEV * CAP, 128), F32),
            pltpu.SMEM((PAN_DEV,), jnp.int32),
            pltpu.SemaphoreType.DMA((5,)),
        ],
        60,
    )(panel_brick, row_counts, block_offset, aperture_panel, charge_blocks)
    got = lax.all_to_all(send, everyone, split_axis=0, concat_axis=0, tiled=True)
    dy, dx, d_slabs = beside(
        slab_kernel, WY, density[:HIGH], density[BX - LOW :], density[:, :16], density[:, BY - LOW :]
    )

    meta = [pltpu.SMEM((PAN_DEV, 128), F32), pltpu.SemaphoreType.DMA]
    charge, *slabs = call(
        deposit_kernel,
        [(DEPX, DEPY, NZ)] + [(HIGH, DEPY, NZ)] * 2 + [(DEPX, 16, NZ)] * 2,
        [VMEM] * 2 + [ANY] * 2,
        meta,
    )(got, ion_charge, *d_slabs)

    def tiles(n, width):
        return (n, width, 8, NZ)

    def layers(n):
        return pltpu.VMEM((n, WY, NZ), F32)

    def brick(over, width):
        return [(BX, BY, NZ), (over, BY, NZ), (LOW, BY, NZ), (BX, width, NZ), (BX, LOW, NZ)]

    def spare(width):
        return [pltpu.VMEM(tiles(LOW + LOW + BLX, width), F32)] * 8

    near, far = NEAR[0], FAR[0]
    work = 20_000_000_000
    cy, cx, _ = beside(charge_slab_kernel, WY, *slabs, first=dx)
    *state, source, dens = call(
        inner_first,
        [tiles(BX, near)] * 4 + [(DEPX, WY, NZ), (BX, WY, NZ)],
        [VMEM] * 6,
        (),
        32,
        work,
    )(charge, *cy, density, *dy)
    next_brick = brick(NEAR[1], 8)
    pot, *slabs, s_low, s_high = call(
        flank_first,
        next_brick + [(HIGH, WY, NZ)] * 2,
        [VMEM] * 10,
        [layers(DEPX)] + spare(near),
        32,
    )(*state, source, dens, *cx, *dx)
    for width, over in (NEAR, FAR):
        py, px, _ = beside(slab_kernel, 8 * width, *slabs)
        state = call(inner_next, [tiles(BX, width)] * 4, [VMEM] * 6, [layers(BX)], 32, work)(
            pot, *py, source, s_low, dens
        )
        operands = (*state, *px, s_low, s_high, *dx)
        if over < HIGH:
            pot, *slabs = call(
                flank_next, brick(HIGH, 16), [VMEM] * 10, [layers(DEPX)] + spare(width), 32
            )(*operands)
    pot, sums = call(
        flank_last,
        [(BX, BY, NZ), (PAN_DEV, 1, 128)],
        [VMEM] * 11,
        [layers(DEPX)] + spare(far) + meta + [pltpu.SMEM((PAN_DEV + 8,), jnp.int32)],
        32,
    )(*operands, got)
    back = lax.all_to_all(sums, everyone, split_axis=0, concat_axis=0, tiled=True)
    (picked,) = call(
        pick_kernel,
        [(APER_DEV,)],
        [SMEM] * 3 + [VMEM],
        [pltpu.VMEM((APER_DEV, 128), F32)],
    )(panel_brick, row_counts, aperture_panel, back)
    return pot, picked


def solution(mesh):
    everyone = P(("gx", "gy"))
    grid = P("gx", "gy", None)
    return jax.shard_map(
        on_device,
        mesh=mesh,
        in_specs=(grid, grid, P(("gx", "gy"), None)) + (everyone,) * 4,
        out_specs=(grid, everyone),
        check_vma=False,
    )
```

```python
import functools

import jax
import jax.numpy as jnp
from jax import lax
from jax.experimental import pallas as pl
from jax.experimental.pallas import tpu as pltpu
from jax.sharding import PartitionSpec as P

BX = 32
BY = 64
NZ = 128
NEWTON = 3
SWEEPS = 8
CAP = 4
BLX = 4
BLY = 4
BLZ = 8
N_GX = 16
N_GY = 8
PAN_DEV = 128
APER_DEV = 16
READ = 4
LOW = 8
HIGH = 11
TILES = 11
WY = 8 * TILES
NEAR = 10
DEPX = BX + BLX - 1
DEPY = 72

VMEM = pl.BlockSpec(memory_space=pltpu.VMEM)
SMEM = pl.BlockSpec(memory_space=pltpu.SMEM)
ANY = pl.BlockSpec(memory_space=pl.ANY)
F32 = jnp.float32


def call(body, outs, ins, scratch=(), mib=24, flops=None):
    cost = None
    if flops is not None:
        cost = pl.CostEstimate(flops=flops, bytes_accessed=1 << 20, transcendentals=0)
    return pl.pallas_call(
        body,
        out_shape=[jax.ShapeDtypeStruct(s, F32) for s in outs],
        in_specs=list(ins),
        out_specs=[VMEM] * len(outs),
        scratch_shapes=list(scratch),
        cost_estimate=cost,
        compiler_params=pltpu.CompilerParams(vmem_limit_bytes=mib << 20),
    )


def iota(shape, dim):
    return lax.broadcasted_iota(jnp.int32, shape, dim)


def pack_kernel(*refs):
    arrays, send, local, need, sems = refs[:5], refs[5], refs[6:11], refs[11], refs[12]
    copies = [pltpu.make_async_copy(a, b, sems.at[i]) for i, (a, b) in enumerate(zip(arrays, local))]
    for copy in copies:
        copy.start()
    brick, counts, offsets, aper, rows = local

    def clear(p, c):
        need[p] = 0
        return c

    lax.fori_loop(0, PAN_DEV, clear, 0, unroll=8)
    for copy in copies:
        copy.wait()
    for a in range(APER_DEV):
        need[aper[a]] = 1
    sub = iota((8, 128), 0)
    group = (iota((8, 128), 1) >> 3) & 3
    j = sub & 3
    masks = {e: (group == j - e) for e in range(-3, 4)}
    lane1 = iota((1, 128), 1)

    def body(q, c):
        p = q * 2
        live = sub < jnp.where(sub < 4, counts[p], counts[p + 1] + 4)
        v = jnp.where(live, rows[pl.ds(pl.multiple_of(q * 8, 8), 8), :], 0.0)
        out = v
        for e in (-3, -2, -1, 1, 2, 3):
            moved = pltpu.roll(pltpu.roll(v, e % 8, 0), (-8 * e) % 128, 1)
            out = jnp.where(masks[e], moved, out)
        for h in range(2):
            b = brick[p + h]
            send[b, 0:4, :] = out[4 * h : 4 * h + 4]
            meta = jnp.zeros((1, 128), jnp.int32)
            for k in range(CAP):
                meta = jnp.where(lane1 == k, offsets[(p + h) * CAP + k], meta)
            meta = jnp.where(lane1 == CAP, need[p + h], meta)
            send[b, 4:5, :] = meta.astype(F32)
        return c

    lax.fori_loop(0, PAN_DEV // 2, body, 0, unroll=4)


def corner(meta, p, k):
    offset = meta[p, k].astype(jnp.int32)
    return offset >> 13, (offset >> 7) & 63, offset & 127


def block_rows(v, z, k, i, lane):
    moved = pltpu.roll(v, (z - 32 * i - 8 * k + 128) & 127, 1)
    return jnp.where((lane >= z) & (lane < z + BLZ), moved, 0.0)


def deposit_kernel(got, ion, unused_low, unused_high, out, x_low, x_high, y_low, y_high, meta, sem):
    copy = pltpu.make_async_copy(got.at[:, 4, :], meta, sem)
    copy.start()
    out[0:BX, 0:BY, :] = ion[...]
    out[0:BX, BY:DEPY, :] = jnp.zeros((BX, DEPY - BY, NZ), F32)
    out[BX:DEPX] = jnp.zeros((DEPX - BX, DEPY, NZ), F32)
    lane = iota((BLY, 128), 1)
    copy.wait()

    def body(p, c):
        v = got[p, 0:4, :]
        for k in range(CAP):
            x, y, z = corner(meta, p, k)
            add = [block_rows(v, z, k, i, lane) for i in range(BLX)]
            old = [out[x + i, pl.ds(y, BLY), :] for i in range(BLX)]
            for i in range(BLX):
                out[x + i, pl.ds(y, BLY), :] = old[i] + add[i]
        return c

    lax.fori_loop(0, PAN_DEV, body, 0, unroll=16)
    x_low[...] = out[0:HIGH]
    x_high[...] = out[BX - LOW : DEPX]
    y_low[...] = out[:, 0:16]
    y_high[...] = out[:, BY - LOW : DEPY]


def inside_y(tiles):
    gy = lax.axis_index("gy")
    lo = jnp.where(gy == 0, LOW, 0)
    hi = jnp.where(gy == N_GY - 1, LOW + BY, WY)
    sub = iota((8, 128), 0)
    ys = [sub * tiles + t for t in range(tiles)]
    return [(y >= lo) & (y < hi) for y in ys]


def lay(nat, at, count, own, below, above):
    nat[at : at + count, 0:LOW] = below
    nat[at : at + count, LOW : LOW + BY] = own
    nat[at : at + count, LOW + BY : LOW + BY + above.shape[1]] = above


def lay_charge(nat, at, count, own, below, above):
    spread = jnp.where(lax.axis_index("gy") > 0, 1.0, 0.0)
    nat[at : at + count, 0:LOW] = below[:, 0:LOW]
    nat[at : at + count, LOW : LOW + DEPY] = own
    nat[at : at + count, LOW : LOW + 8] += below[:, LOW : LOW + 8] * spread
    nat[at : at + count, LOW + BY : LOW + DEPY] += above[:, 0:8]
    nat[at : at + count, LOW + DEPY : WY] = above[:, 8:16]


def strided(nat, x, t, tiles):
    return nat[x, pl.ds(t, 8, stride=tiles), :]


def relax(layers, write):
    tiles = len(layers[0])
    lane = iota((8, 128), 1)
    first, last = lane == 0, lane == NZ - 1
    for u in range(len(layers) - 2):
        prev, cur, nxt = layers[u : u + 3]
        before = [pltpu.roll(cur[-1], 1, 0)] + cur[:-1]
        after = cur[1:] + [pltpu.roll(cur[0], 7, 0)]
        for t in range(tiles):
            left = jnp.where(first, 0.0, pltpu.roll(cur[t], 1, 1))
            right = jnp.where(last, 0.0, pltpu.roll(cur[t], NZ - 1, 1))
            total = (prev[t] + nxt[t]) + (before[t] + after[t]) + (left + right)
            write(u, t, total)


def layer(buf, x):
    return [buf[x, t] for t in range(buf.shape[1])]


def sweep(src, dst, rhs, inv, lo, hi):
    def rows(x0, count):
        def write(u, t, total):
            dst[x0 + u, t] = (rhs[x0 + u, t] + total) * inv[x0 + u, t]

        relax([layer(src, x0 - 1 + u) for u in range(count + 2)], write)

    count = (hi - lo + 1) // 2

    def body(i, c):
        rows(lo + i * count, count)
        return c

    lax.fori_loop(0, (hi - lo) // count, body, 0)
    if (hi - lo) % count:
        rows(lo + count, (hi - lo) % count)


def inner(b0, b1, rhs, inv, k0, a, h):
    bufs = (b0, b1)
    for k in range(k0, SWEEPS + 1):
        sweep(bufs[(k - 1) % 2], bufs[k % 2], rhs, inv, a + k, h - k)


def inner_first(charge, y_below, y_above, density, d_below, d_above, *refs):
    b0, b1, rhs, inv, source, dens = refs
    tiles = b0.shape[1]
    inside = inside_y(tiles)
    lay(dens, 0, BX, density[...], d_below[...], d_above[...])
    lay_charge(source, 0, DEPX, charge[...], y_below, y_above)

    def prep(x, c):
        for t in range(tiles):
            s = strided(source, x, t, tiles)
            d = strided(dens, x, t, tiles)
            scale = jnp.where(inside[t], 1.0 / (6.0 + d), 0.0)
            inv[x, t] = scale
            rhs[x, t] = s - d
            b1[x, t] = (s - d) * scale
        return c

    lax.fori_loop(0, BX, prep, 0, unroll=2)
    inner(b0, b1, rhs, inv, 2, BLX - 2, BX + 1)


def start(p_nat, s, s_at, d, inside, f, outs, to, x):
    p_out, rhs, inv = outs
    tiles = p_out.shape[1]
    for t in range(tiles):
        p = jnp.where(inside[t], strided(p_nat, x, t, tiles) * f, 0.0)
        coef = strided(d, x, t, tiles) * jnp.exp(p)
        p_out[x + to, t] = p
        rhs[x + to, t] = strided(s, x + s_at, t, tiles) + coef * (p - 1.0)
        inv[x + to, t] = jnp.where(inside[t], f / (6.0 + coef), 0.0)


def inner_next(own, y_below, y_above, source, s_low, dens, b0, b1, rhs, inv, nat):
    inside = inside_y(b0.shape[1])
    lay(nat, 0, BX, own[...], y_below[0:BX], y_above[0:BX])
    outs = (b0, rhs, inv)

    def prep_from(src, at):
        def prep(x, c):
            start(nat, src, at, dens, inside, 1.0, outs, 0, x)
            return c

        return prep

    lax.fori_loop(0, BLX - 1, prep_from(s_low, LOW), 0)
    lax.fori_loop(BLX - 1, BX, prep_from(source, 0), 0)
    inner(b0, b1, rhs, inv, 1, 0, BX)


def flanks(b0, b1, lows, highs, rhs, inv, k0, a, h):
    (l0, l1, l_rhs, l_inv), (h0, h1, h_rhs, h_inv) = lows, highs
    n_low, n_high = LOW + a, BX + HIGH - h
    for i in range(LOW + a):
        if i + LOW >= len_low_halo(a):
            l_rhs[i + LOW], l_inv[i + LOW] = rhs[i], inv[i]
    for i in range(h - LOW, BX):
        h_rhs[i - (h - LOW)], h_inv[i - (h - LOW)] = rhs[i], inv[i]

    def one(k, near, l_src, l_dst, h_src, h_dst):
        def low_write(u, t, total):
            l_dst[k + u, t] = (l_rhs[k + u, t] + total) * l_inv[k + u, t]

        def high_write(u, t, total):
            r = LOW - k + u
            h_dst[r, t] = (h_rhs[r, t] + total) * h_inv[r, t]

        low = [layer(l_src, k - 1 + j) for j in range(n_low)]
        relax(low + [layer(near, a + k - 1), layer(near, a + k)], low_write)
        high = [layer(h_src, LOW + 1 - k + j) for j in range(n_high)]
        relax([layer(near, h - k - 1), layer(near, h - k)] + high, high_write)

    if k0 == 2:
        one(2, b1, l1, l0, h1, h0)

    def body(j, c):
        one(2 * j + 1, b0, l0, l1, h0, h1)
        one(2 * j + 2, b1, l1, l0, h1, h0)
        return c

    lax.fori_loop(k0 - 1, SWEEPS // 2, body, 0)


def len_low_halo(a):
    return LOW + (BLX - 1 if a else 0)


def finish(b0, l0, h0, nat, a, h):
    tiles = b0.shape[1]

    def take(src, shift):
        def body(x, c):
            for t in range(tiles):
                nat[x, pl.ds(t, 8, stride=tiles), :] = src[x + shift, t]
            return c

        return body

    lax.fori_loop(0, a + LOW, take(l0, LOW), 0, unroll=2)
    lax.fori_loop(a + LOW, h - LOW, take(b0, 0), 0, unroll=2)
    lax.fori_loop(h - LOW, DEPX, take(h0, LOW - h), 0, unroll=2)


def hand_on(nat, out, ahead, x_low, x_high, y_low, y_high):
    out[...] = nat[0:BX, LOW : LOW + BY]
    x_low[...] = nat[HIGH - LOW : HIGH, LOW : LOW + BY]
    ahead[...] = nat[BX:DEPX, LOW : LOW + BY]
    x_high[...] = nat[BX - LOW : BX, LOW : LOW + BY]
    y_low[...] = nat[0:DEPX, LOW : LOW + y_low.shape[1]]
    y_high[...] = nat[0:DEPX, BY : LOW + BY]


def edges():
    gx = lax.axis_index("gx")
    return jnp.where(gx > 0, 1.0, 0.0), jnp.where(gx < N_GX - 1, 1.0, 0.0)


def flank_first(*refs):
    b0, b1, rhs, inv, source, dens, x_below, x_above, c_below, c_above, d_below, d_above = refs[:12]
    outs, (s_low, s_high), nat, spare = refs[12:18], refs[18:20], refs[20], refs[21:]
    l0, l1, l_rhs, l_inv, h0, h1, h_rhs, h_inv = spare
    a, h = BLX - 2, BX + 1
    tiles = NEAR
    inside, (f_low, f_high) = inside_y(tiles), edges()
    lay_charge(s_low, 0, HIGH, x_below[...], c_below[:, 0:16], c_below[:, 16:32])
    lay_charge(s_high, 0, HIGH, x_above[...], c_above[:, 0:16], c_above[:, 16:32])
    s_low[LOW:HIGH] = source[0 : HIGH - LOW] + s_low[LOW:HIGH] * f_low
    s_high[0 : DEPX - BX] += source[BX:DEPX]

    def fill(count, s, s_at, d, d_at, f, at, p_out, rhs_out, inv_out):
        def body(r, c):
            for t in range(tiles):
                den = strided(d, r + d_at, t, tiles)
                scale = jnp.where(inside[t], f / (6.0 + den), 0.0)
                value = strided(s, r + s_at, t, tiles) - den
                rhs_out[r + at, t], inv_out[r + at, t] = value, scale
                p_out[r + at, t] = value * scale
            return c

        lax.fori_loop(0, count, body, 0)

    fill(LOW, s_low, 0, d_below, 0, f_low, 0, l1, l_rhs, l_inv)
    fill(BLX - 1, s_low, LOW, dens, 0, 1.0, LOW, l1, l_rhs, l_inv)
    fill(HIGH, s_high, 0, d_above, 0, f_high, LOW - 1, h1, h_rhs, h_inv)
    lows, highs = (l0, l1, l_rhs, l_inv), (h0, h1, h_rhs, h_inv)
    flanks(b0, b1, lows, highs, rhs, inv, 2, a, h)
    finish(b0, l0, h0, nat, a, h)
    hand_on(nat, *outs)


def next_flanks(refs, nat, spare):
    b0, b1, rhs, inv, ahead, y_below, y_above, x_below, x_above, s_low, s_high, d_low, d_high = refs
    l0, l1, l_rhs, l_inv, h0, h1, h_rhs, h_inv = spare
    inside, (f_low, f_high) = inside_y(b0.shape[1]), edges()

    def low_body(r, c):
        start(x_below, s_low, 0, d_low, inside, f_low, (l0, l_rhs, l_inv), 0, r)
        return c

    more = HIGH - LOW
    lay(nat, 0, more, ahead[...], y_below[BX:DEPX], y_above[BX:DEPX])
    nat[more:HIGH, 0 : x_above.shape[1]] = x_above[...]

    def high_body(r, c):
        start(nat, s_high, 0, d_high, inside, f_high, (h0, h_rhs, h_inv), LOW, r)
        return c

    lax.fori_loop(0, LOW, low_body, 0)
    lax.fori_loop(0, HIGH, high_body, 0)
    lows, highs = (l0, l1, l_rhs, l_inv), (h0, h1, h_rhs, h_inv)
    flanks(b0, b1, lows, highs, rhs, inv, 1, 0, BX)
    finish(b0, l0, h0, nat, 0, BX)


def flank_next(*refs):
    outs, (nat, *spare) = refs[13:19], refs[19:]
    next_flanks(refs[:13], nat, spare)
    hand_on(nat, *outs)


def flank_last(*refs):
    (got, out, sums, nat), spare, (meta, sem, named) = refs[13:17], refs[17:25], refs[25:]
    copy = pltpu.make_async_copy(got.at[:, 4, :], meta, sem)
    copy.start()
    next_flanks(refs[:13], nat, spare)
    out[...] = nat[0:BX, LOW : LOW + BY]
    copy.wait()
    read(got, nat, sums, meta, named)


def slab_kernel(at_low, x_low, x_high, below, above, low, high):
    for own, at, slab in ((x_low, at_low, low), (x_high, BX - LOW, high)):
        n, width = slab.shape[0], slab.shape[1]
        slab[:, 0:LOW] = below[at : at + n]
        slab[:, LOW : LOW + BY] = own[...]
        slab[:, LOW + BY : width] = above[at : at + n]


def beside(at_low, width, x_low, x_high, y_low, y_high):
    y_below, y_above = ring(y_high, "gy", 1), ring(y_low, "gy", -1)
    low, high = call(
        functools.partial(slab_kernel, at_low),
        [(x_low.shape[0], width, NZ), (x_high.shape[0], width, NZ)],
        [VMEM] * 4,
    )(x_low, x_high, y_below, y_above)
    x_below, x_above = ring(high, "gx", 1), ring(low, "gx", -1)
    return (y_below, y_above), (x_below, x_above), (low, high)


def corner_kernel(below, above, unused_low, unused_high, low, high):
    for at, strip in ((0, low), (BX - LOW, high)):
        strip[:, 0:16] = below[at : at + HIGH]
        strip[:, 16:32] = above[at : at + HIGH]


def charge_beside(x_low, x_high, y_low, y_high, first):
    x_below, x_above = ring(x_high, "gx", 1), ring(x_low, "gx", -1)
    y_below, y_above = ring(y_high, "gy", 1), ring(y_low, "gy", -1)
    low, high = call(corner_kernel, [(HIGH, 32, NZ)] * 2, [VMEM] * 2 + [ANY] * 2)(
        y_below, y_above, *first
    )
    c_below, c_above = ring(high, "gx", 1), ring(low, "gx", -1)
    return (y_below, y_above), (x_below, x_above, c_below, c_above)


def read(got, field, out, meta, named):
    lane = iota((BLY, 128), 1)

    def note(p, n):
        named[n] = p
        return n + meta[p, CAP].astype(jnp.int32)

    count = lax.fori_loop(0, PAN_DEV, note, 0, unroll=8)
    for u in range(READ):
        named[count + u] = 0

    def body(j, c):
        for u in range(READ):
            p = named[READ * j + u]
            v = got[p, 0:4, :]
            total = jnp.zeros((BLY, 128), F32)
            for k in range(CAP):
                x, y, z = corner(meta, p, k)
                for i in range(BLX):
                    piece = field[x + i, pl.ds(y + LOW, BLY), :]
                    total += block_rows(v, z, k, i, lane) * piece
            out[p] = jnp.sum(total, axis=0, keepdims=True)
        return c

    lax.fori_loop(0, (count + READ - 1) // READ, body, 0)


def pick_kernel(brick, counts, aper, got, out, rows):
    sub = iota((1, APER_DEV), 1)
    live = jnp.ones((1, APER_DEV), F32)
    for a in range(APER_DEV):
        p = aper[a]
        rows[a : a + 1, :] = got[brick[p]]
        live = jnp.where(sub == a, counts[p].astype(F32), live)
    out[...] = jnp.sum(rows[...], axis=1) / live[0]


def ring(array, axis, by):
    size = lax.axis_size(axis)
    return lax.ppermute(array, axis, [(i, (i + by) % size) for i in range(size)])


def on_device(
    ion_charge, density, charge_blocks, panel_brick, row_counts, block_offset, aperture_panel
):
    everyone = ("gx", "gy")
    ints = [pltpu.SMEM((n,), jnp.int32) for n in (PAN_DEV, PAN_DEV, PAN_DEV * CAP, APER_DEV)]
    (send,) = call(
        pack_kernel,
        [(PAN_DEV, 8, 128)],
        [ANY] * 5,
        ints
        + [
            pltpu.VMEM((PAN_DEV * CAP, 128), F32),
            pltpu.SMEM((PAN_DEV,), jnp.int32),
            pltpu.SemaphoreType.DMA((5,)),
        ],
        60,
    )(panel_brick, row_counts, block_offset, aperture_panel, charge_blocks)
    got = lax.all_to_all(send, everyone, split_axis=0, concat_axis=0, tiled=True)
    dy, dx, d_slabs = beside(
        0, WY, density[:HIGH], density[BX - LOW :], density[:, :16], density[:, BY - LOW :]
    )

    meta = [pltpu.SMEM((PAN_DEV, 128), F32), pltpu.SemaphoreType.DMA]
    charge, *slabs = call(
        deposit_kernel,
        [(DEPX, DEPY, NZ)] + [(HIGH, DEPY, NZ)] * 2 + [(DEPX, 16, NZ)] * 2,
        [VMEM] * 2 + [ANY] * 2,
        meta,
    )(got, ion_charge, *d_slabs)

    def tiles(n, width):
        return (n, width, 8, NZ)

    def layers(n):
        return pltpu.VMEM((n, WY, NZ), F32)

    def brick(width):
        slabs = [(HIGH - LOW, BY, NZ), (LOW, BY, NZ), (LOW, BY, NZ), (DEPX, width, NZ), (DEPX, LOW, NZ)]
        return [(BX, BY, NZ)] + slabs

    def spare(width):
        return [pltpu.VMEM(tiles(LOW + LOW + BLX, width), F32)] * 8

    work = 20_000_000_000
    cy, cx = charge_beside(*slabs, first=dx)
    *state, source, dens = call(
        inner_first,
        [tiles(BX, NEAR)] * 4 + [(DEPX, WY, NZ), (BX, WY, NZ)],
        [VMEM] * 6,
        (),
        32,
        work,
    )(charge, *cy, density, *dy)
    pot, ahead, *slabs, s_low, s_high = call(
        flank_first,
        brick(8) + [(HIGH, WY, NZ)] * 2,
        [VMEM] * 12,
        [layers(DEPX)] + spare(NEAR),
        32,
    )(*state, source, dens, *cx, *dx)
    for step in range(1, NEWTON):
        width = NEAR if step < NEWTON - 1 else TILES
        py, px, _ = beside(HIGH - LOW, 8 * width, *slabs)
        state = call(inner_next, [tiles(BX, width)] * 4, [VMEM] * 6, [layers(BX)], 32, work)(
            pot, *py, source, s_low, dens
        )
        operands = (*state, ahead, *py, *px, s_low, s_high, *dx)
        if step < NEWTON - 1:
            pot, ahead, *slabs = call(
                flank_next, brick(16), [VMEM] * 13, [layers(DEPX)] + spare(width), 32
            )(*operands)
    pot, sums = call(
        flank_last,
        [(BX, BY, NZ), (PAN_DEV, 1, 128)],
        [VMEM] * 14,
        [layers(DEPX)] + spare(TILES) + meta + [pltpu.SMEM((PAN_DEV + 8,), jnp.int32)],
        32,
    )(*operands, got)
    back = lax.all_to_all(sums, everyone, split_axis=0, concat_axis=0, tiled=True)
    (picked,) = call(
        pick_kernel,
        [(APER_DEV,)],
        [SMEM] * 3 + [VMEM],
        [pltpu.VMEM((APER_DEV, 128), F32)],
    )(panel_brick, row_counts, aperture_panel, back)
    return pot, picked


def solution(mesh):
    everyone = P(("gx", "gy"))
    grid = P("gx", "gy", None)
    return jax.shard_map(
        on_device,
        mesh=mesh,
        in_specs=(grid, grid, P(("gx", "gy"), None)) + (everyone,) * 4,
        out_specs=(grid, everyone),
        check_vma=False,
    )
```

```python
import functools

import jax
import jax.numpy as jnp
from jax import lax
from jax.experimental import pallas as pl
from jax.experimental.pallas import tpu as pltpu
from jax.sharding import PartitionSpec as P

BX = 32
BY = 64
NZ = 128
NEWTON = 3
SWEEPS = 8
CAP = 4
BLX = 4
BLY = 4
BLZ = 8
N_GX = 16
N_GY = 8
PAN_DEV = 128
APER_DEV = 16
MSG = CAP + 1
READ = 4
LOW = 8
HIGH = 11
TILES = 11
WY = 8 * TILES
BY_PRODUCT = 4
NEAR = 10
DEPX = BX + BLX - 1
DEPY = 72

VMEM = pl.BlockSpec(memory_space=pltpu.VMEM)
SMEM = pl.BlockSpec(memory_space=pltpu.SMEM)
ANY = pl.BlockSpec(memory_space=pl.ANY)
F32 = jnp.float32


def call(body, outs, ins, scratch=(), mib=24, flops=None):
    cost = None
    if flops is not None:
        cost = pl.CostEstimate(flops=flops, bytes_accessed=1 << 20, transcendentals=0)
    return pl.pallas_call(
        body,
        out_shape=[jax.ShapeDtypeStruct(s, F32) for s in outs],
        in_specs=list(ins),
        out_specs=[VMEM] * len(outs),
        scratch_shapes=list(scratch),
        cost_estimate=cost,
        compiler_params=pltpu.CompilerParams(vmem_limit_bytes=mib << 20),
    )


def iota(shape, dim):
    return lax.broadcasted_iota(jnp.int32, shape, dim)


def pack_kernel(*refs):
    arrays, send, local, need, sems = refs[:5], refs[5], refs[6:11], refs[11], refs[12]
    copies = [pltpu.make_async_copy(a, b, sems.at[i]) for i, (a, b) in enumerate(zip(arrays, local))]
    for copy in copies:
        copy.start()
    brick, counts, offsets, aper, rows = local

    def clear(p, c):
        need[p] = 0
        return c

    lax.fori_loop(0, PAN_DEV, clear, 0, unroll=8)
    for copy in copies:
        copy.wait()
    for a in range(APER_DEV):
        need[aper[a]] = 1
    sub = iota((8, 128), 0)
    group = (iota((8, 128), 1) >> 3) & 3
    j = sub & 3
    masks = {e: (group == j - e) for e in range(-3, 4)}
    lane1 = iota((1, 128), 1)

    def body(q, c):
        p = q * 2
        live = sub < jnp.where(sub < 4, counts[p], counts[p + 1] + 4)
        v = jnp.where(live, rows[pl.ds(pl.multiple_of(q * 8, 8), 8), :], 0.0)
        out = v
        for e in (-3, -2, -1, 1, 2, 3):
            moved = pltpu.roll(pltpu.roll(v, e % 8, 0), (-8 * e) % 128, 1)
            out = jnp.where(masks[e], moved, out)
        for h in range(2):
            b = brick[p + h]
            send[pl.ds(b * MSG, 4), :] = out[4 * h : 4 * h + 4]
            meta = jnp.zeros((1, 128), jnp.int32)
            for k in range(CAP):
                meta = jnp.where(lane1 == k, offsets[(p + h) * CAP + k], meta)
            meta = jnp.where(lane1 == CAP, need[p + h], meta)
            send[pl.ds(b * MSG + 4, 1), :] = meta.astype(F32)
        return c

    lax.fori_loop(0, PAN_DEV // 2, body, 0, unroll=4)


def numbers(got, turned, meta, sem):
    rows = got[pl.ds(CAP, PAN_DEV, stride=MSG), :]
    turned[...] = jnp.transpose(rows)[0:8].astype(jnp.int32)
    copy = pltpu.make_async_copy(turned, meta, sem)
    copy.start()
    return copy


def corner(meta, p, k):
    offset = meta[k, p]
    return offset >> 13, (offset >> 7) & 63, offset & 127


def block_rows(v, z, k, i, lane):
    moved = pltpu.roll(v, (z - 32 * i - 8 * k + 128) & 127, 1)
    return jnp.where((lane >= z) & (lane < z + BLZ), moved, 0.0)


def deposit_kernel(got, ion, unused_low, unused_high, out, x_low, x_high, y_low, y_high, turned, meta, sem):
    copy = numbers(got, turned, meta, sem)
    out[0:BX, 0:BY, :] = ion[...]
    out[0:BX, BY:DEPY, :] = jnp.zeros((BX, DEPY - BY, NZ), F32)
    out[BX:DEPX] = jnp.zeros((DEPX - BX, DEPY, NZ), F32)
    lane = iota((BLY, 128), 1)
    copy.wait()

    def body(p, c):
        v = got[pl.ds(p * MSG, CAP), :]
        for k in range(CAP):
            x, y, z = corner(meta, p, k)
            add = [block_rows(v, z, k, i, lane) for i in range(BLX)]
            old = [out[x + i, pl.ds(y, BLY), :] for i in range(BLX)]
            for i in range(BLX):
                out[x + i, pl.ds(y, BLY), :] = old[i] + add[i]
        return c

    lax.fori_loop(0, PAN_DEV, body, 0, unroll=16)
    x_low[...] = out[0:HIGH]
    x_high[...] = out[BX - LOW : DEPX]
    y_low[...] = out[:, 0:16]
    y_high[...] = out[:, BY - LOW : DEPY]


def inside_y(tiles):
    gy = lax.axis_index("gy")
    lo = jnp.where(gy == 0, LOW, 0)
    hi = jnp.where(gy == N_GY - 1, LOW + BY, WY)
    sub = iota((8, 128), 0)
    ys = [sub * tiles + t for t in range(tiles)]
    return [(y >= lo) & (y < hi) for y in ys]


def lay(nat, at, count, own, below, above):
    nat[at : at + count, 0:LOW] = below
    nat[at : at + count, LOW : LOW + BY] = own
    nat[at : at + count, LOW + BY : LOW + BY + above.shape[1]] = above


def lay_charge(nat, at, count, own, below, spilled, above):
    spread = jnp.where(lax.axis_index("gy") > 0, 1.0, 0.0)
    nat[at : at + count, 0:LOW] = below
    nat[at : at + count, LOW : LOW + DEPY] = own
    nat[at : at + count, LOW : LOW + BLY - 1] += spilled * spread
    nat[at : at + count, LOW + BY : LOW + DEPY] += above[:, 0:8]
    nat[at : at + count, LOW + DEPY : LOW + DEPY + 3] = above[:, 8:HIGH]
    nat[at : at + count, LOW + DEPY + 3 : WY] = jnp.zeros((count, WY - LOW - DEPY - 3, NZ), F32)


def strided(nat, x, t, tiles):
    return nat[x, pl.ds(t, 8, stride=tiles), :]


def relax(layers, write):
    tiles = len(layers[0])
    rolled = tiles - BY_PRODUCT
    lane = iota((8, 128), 1)
    first, last = lane == 0, lane == NZ - 1
    inner_layers = layers[1:-1]
    flat = jnp.concatenate(sum([cur[rolled:] for cur in inner_layers], []), axis=0)
    high = flat.astype(jnp.bfloat16)
    low = (flat - high.astype(F32)).astype(jnp.bfloat16)
    from_z, to_z = iota((2 * NZ, NZ), 0) & (NZ - 1), iota((2 * NZ, NZ), 1)
    beside_z = jnp.where((from_z - to_z == 1) | (to_z - from_z == 1), 1.0, 0.0)
    product = jnp.dot(
        jnp.concatenate([high, low], axis=1),
        beside_z.astype(jnp.bfloat16),
        preferred_element_type=F32,
    )
    for u in range(len(inner_layers)):
        prev, cur, nxt = layers[u : u + 3]
        before = [pltpu.roll(cur[-1], 1, 0)] + cur[:-1]
        after = cur[1:] + [pltpu.roll(cur[0], 7, 0)]
        for t in range(tiles):
            if t < rolled:
                left = jnp.where(first, 0.0, pltpu.roll(cur[t], 1, 1))
                along_z = left + jnp.where(last, 0.0, pltpu.roll(cur[t], NZ - 1, 1))
            else:
                at = (u * BY_PRODUCT + t - rolled) * 8
                along_z = product[at : at + 8]
            total = (prev[t] + nxt[t]) + (before[t] + after[t]) + along_z
            write(u, t, total)


def layer(buf, x):
    return [buf[x, t] for t in range(buf.shape[1])]


def sweep(src, dst, rhs, inv, lo, hi):
    def rows(x0, count):
        def write(u, t, total):
            dst[x0 + u, t] = (rhs[x0 + u, t] + total) * inv[x0 + u, t]

        relax([layer(src, x0 - 1 + u) for u in range(count + 2)], write)

    count = (hi - lo + 1) // 2

    def body(i, c):
        rows(lo + i * count, count)
        return c

    lax.fori_loop(0, (hi - lo) // count, body, 0)
    if (hi - lo) % count:
        rows(lo + count, (hi - lo) % count)


def inner(b0, b1, rhs, inv, k0, a, h):
    bufs = (b0, b1)
    for k in range(k0, SWEEPS + 1):
        sweep(bufs[(k - 1) % 2], bufs[k % 2], rhs, inv, a + k, h - k)


def inner_first(charge, y_below, y_above, density, d_below, d_above, *refs):
    b0, b1, rhs, inv, source, dens = refs
    tiles = b0.shape[1]
    inside = inside_y(tiles)
    lay(dens, 0, BX, density[...], d_below[...], d_above[...])
    lay_charge(source, 0, DEPX, charge[...], y_below[:, 0:8], y_below[:, 8:HIGH], y_above)

    def prep(x, c):
        for t in range(tiles):
            s = strided(source, x, t, tiles)
            d = strided(dens, x, t, tiles)
            scale = jnp.where(inside[t], 1.0 / (6.0 + d), 0.0)
            inv[x, t] = scale
            rhs[x, t] = s - d
            b1[x, t] = (s - d) * scale
        return c

    lax.fori_loop(0, BX, prep, 0, unroll=2)
    inner(b0, b1, rhs, inv, 2, BLX - 2, BX + 1)


def start(p_nat, s, s_at, d, inside, f, outs, to, x):
    p_out, rhs, inv = outs
    tiles = p_out.shape[1]
    for t in range(tiles):
        p = jnp.where(inside[t], strided(p_nat, x, t, tiles) * f, 0.0)
        coef = strided(d, x, t, tiles) * jnp.exp(p)
        p_out[x + to, t] = p
        rhs[x + to, t] = strided(s, x + s_at, t, tiles) + coef * (p - 1.0)
        inv[x + to, t] = jnp.where(inside[t], f / (6.0 + coef), 0.0)


def inner_next(own, y_below, y_above, source, s_low, dens, b0, b1, rhs, inv, nat):
    inside = inside_y(b0.shape[1])
    lay(nat, 0, BX, own[...], y_below[0:BX], y_above[0:BX])
    outs = (b0, rhs, inv)

    def prep_from(src, at):
        def prep(x, c):
            start(nat, src, at, dens, inside, 1.0, outs, 0, x)
            return c

        return prep

    lax.fori_loop(0, BLX - 1, prep_from(s_low, LOW), 0)
    lax.fori_loop(BLX - 1, BX, prep_from(source, 0), 0)
    inner(b0, b1, rhs, inv, 1, 0, BX)


def flanks(b0, b1, lows, highs, rhs, inv, k0, a, h):
    (l0, l1, l_rhs, l_inv), (h0, h1, h_rhs, h_inv) = lows, highs
    n_low, n_high = LOW + a, BX + HIGH - h
    for i in range(LOW + a):
        if i + LOW >= len_low_halo(a):
            l_rhs[i + LOW], l_inv[i + LOW] = rhs[i], inv[i]
    for i in range(h - LOW, BX):
        h_rhs[i - (h - LOW)], h_inv[i - (h - LOW)] = rhs[i], inv[i]

    def one(k, near, l_src, l_dst, h_src, h_dst):
        def low_write(u, t, total):
            l_dst[k + u, t] = (l_rhs[k + u, t] + total) * l_inv[k + u, t]

        def high_write(u, t, total):
            r = LOW - k + u
            h_dst[r, t] = (h_rhs[r, t] + total) * h_inv[r, t]

        low = [layer(l_src, k - 1 + j) for j in range(n_low)]
        relax(low + [layer(near, a + k - 1), layer(near, a + k)], low_write)
        high = [layer(h_src, LOW + 1 - k + j) for j in range(n_high)]
        relax([layer(near, h - k - 1), layer(near, h - k)] + high, high_write)

    if k0 == 2:
        one(2, b1, l1, l0, h1, h0)

    def body(j, c):
        one(2 * j + 1, b0, l0, l1, h0, h1)
        one(2 * j + 2, b1, l1, l0, h1, h0)
        return c

    lax.fori_loop(k0 - 1, SWEEPS // 2, body, 0)


def len_low_halo(a):
    return LOW + (BLX - 1 if a else 0)


def finish(b0, l0, h0, nat, a, h):
    tiles = b0.shape[1]

    def take(src, shift):
        def body(x, c):
            for t in range(tiles):
                nat[x, pl.ds(t, 8, stride=tiles), :] = src[x + shift, t]
            return c

        return body

    lax.fori_loop(0, a + LOW, take(l0, LOW), 0, unroll=2)
    lax.fori_loop(a + LOW, h - LOW, take(b0, 0), 0, unroll=2)
    lax.fori_loop(h - LOW, DEPX, take(h0, LOW - h), 0, unroll=2)


def hand_on(nat, out, ahead, x_low, x_high, y_low, y_high):
    out[...] = nat[0:BX, LOW : LOW + BY]
    x_low[...] = nat[HIGH - LOW : HIGH, LOW : LOW + BY]
    ahead[...] = nat[BX:DEPX, LOW : LOW + BY]
    x_high[...] = nat[BX - LOW : BX, LOW : LOW + BY]
    y_low[...] = nat[0:DEPX, LOW : LOW + y_low.shape[1]]
    y_high[...] = nat[0:DEPX, BY : LOW + BY]


def edges():
    gx = lax.axis_index("gx")
    return jnp.where(gx > 0, 1.0, 0.0), jnp.where(gx < N_GX - 1, 1.0, 0.0)


def flank_first(*refs):
    b0, b1, rhs, inv, source, dens, x_below, x_above, c_below, c_above, d_below, d_above = refs[:12]
    outs, (s_low, s_high), nat, spare = refs[12:18], refs[18:20], refs[20], refs[21:]
    l0, l1, l_rhs, l_inv, h0, h1, h_rhs, h_inv = spare
    a, h = BLX - 2, BX + 1
    tiles = NEAR
    inside, (f_low, f_high) = inside_y(tiles), edges()
    for c, s, x in ((c_below, s_low, x_below), (c_above, s_high, x_above)):
        lay_charge(s, 0, HIGH, x[...], c[:, 0:8], c[:, 19:22], c[:, 8:19])
    s_low[LOW:HIGH] = source[0 : HIGH - LOW] + s_low[LOW:HIGH] * f_low
    s_high[0 : DEPX - BX] += source[BX:DEPX]

    def fill(count, s, s_at, d, d_at, f, at, p_out, rhs_out, inv_out):
        def body(r, c):
            for t in range(tiles):
                den = strided(d, r + d_at, t, tiles)
                scale = jnp.where(inside[t], f / (6.0 + den), 0.0)
                value = strided(s, r + s_at, t, tiles) - den
                rhs_out[r + at, t], inv_out[r + at, t] = value, scale
                p_out[r + at, t] = value * scale
            return c

        lax.fori_loop(0, count, body, 0)

    fill(LOW, s_low, 0, d_below, 0, f_low, 0, l1, l_rhs, l_inv)
    fill(BLX - 1, s_low, LOW, dens, 0, 1.0, LOW, l1, l_rhs, l_inv)
    fill(HIGH, s_high, 0, d_above, 0, f_high, LOW - 1, h1, h_rhs, h_inv)
    lows, highs = (l0, l1, l_rhs, l_inv), (h0, h1, h_rhs, h_inv)
    flanks(b0, b1, lows, highs, rhs, inv, 2, a, h)
    finish(b0, l0, h0, nat, a, h)
    hand_on(nat, *outs)


def next_flanks(refs, nat, spare):
    b0, b1, rhs, inv, ahead, y_below, y_above, x_below, x_above, s_low, s_high, d_low, d_high = refs
    l0, l1, l_rhs, l_inv, h0, h1, h_rhs, h_inv = spare
    inside, (f_low, f_high) = inside_y(b0.shape[1]), edges()

    def low_body(r, c):
        start(x_below, s_low, 0, d_low, inside, f_low, (l0, l_rhs, l_inv), 0, r)
        return c

    more = HIGH - LOW
    lay(nat, 0, more, ahead[...], y_below[BX:DEPX], y_above[BX:DEPX])
    nat[more:HIGH, 0 : x_above.shape[1]] = x_above[...]

    def high_body(r, c):
        start(nat, s_high, 0, d_high, inside, f_high, (h0, h_rhs, h_inv), LOW, r)
        return c

    lax.fori_loop(0, LOW, low_body, 0)
    lax.fori_loop(0, HIGH, high_body, 0)
    lows, highs = (l0, l1, l_rhs, l_inv), (h0, h1, h_rhs, h_inv)
    flanks(b0, b1, lows, highs, rhs, inv, 1, 0, BX)
    finish(b0, l0, h0, nat, 0, BX)


def flank_next(*refs):
    outs, (nat, *spare) = refs[13:19], refs[19:]
    next_flanks(refs[:13], nat, spare)
    hand_on(nat, *outs)


def flank_last(*refs):
    (got, out, sums, nat), spare, (turned, meta, sem, named) = refs[13:17], refs[17:25], refs[25:]
    copy = numbers(got, turned, meta, sem)
    next_flanks(refs[:13], nat, spare)
    out[...] = nat[0:BX, LOW : LOW + BY]
    copy.wait()
    read(got, nat, sums, meta, named)


def slab_kernel(at_low, x_low, x_high, below, above, low, high):
    for own, at, slab in ((x_low, at_low, low), (x_high, BX - LOW, high)):
        n, width = slab.shape[0], slab.shape[1]
        slab[:, 0:LOW] = below[at : at + n]
        slab[:, LOW : LOW + BY] = own[...]
        slab[:, LOW + BY : width] = above[at : at + n]


def beside(at_low, width, x_low, x_high, y_low, y_high):
    y_below, y_above = ring(y_high, "gy", 1), ring(y_low, "gy", -1)
    low, high = call(
        functools.partial(slab_kernel, at_low),
        [(x_low.shape[0], width, NZ), (x_high.shape[0], width, NZ)],
        [VMEM] * 4,
    )(x_low, x_high, y_below, y_above)
    x_below, x_above = ring(high, "gx", 1), ring(low, "gx", -1)
    return (y_below, y_above), (x_below, x_above), (low, high)


def corner_kernel(below, above, unused_low, unused_high, low, high):
    for at, strip in ((0, low), (BX - LOW, high)):
        strip[:, 0:8] = below[at : at + HIGH, 0:8]
        strip[:, 8:16] = above[at : at + HIGH, 0:8]
        strip[:, 16:19] = above[at : at + HIGH, 8:HIGH]
        strip[:, 19:22] = below[at : at + HIGH, 8:HIGH]
        strip[:, 22:24] = jnp.zeros((HIGH, 2, NZ), F32)


def charge_beside(x_low, x_high, y_low, y_high, first):
    x_below, x_above = ring(x_high, "gx", 1), ring(x_low, "gx", -1)
    y_below, y_above = ring(y_high, "gy", 1), ring(y_low, "gy", -1)
    low, high = call(corner_kernel, [(HIGH, 24, NZ)] * 2, [VMEM] * 2 + [ANY] * 2)(
        y_below, y_above, *first
    )
    c_below, c_above = ring(high, "gx", 1), ring(low, "gx", -1)
    return (y_below, y_above), (x_below, x_above, c_below, c_above)


def read(got, field, out, meta, named):
    lane = iota((BLY, 128), 1)

    def note(p, n):
        named[n] = p
        return n + meta[CAP, p]

    count = lax.fori_loop(0, PAN_DEV, note, 0, unroll=8)
    for u in range(READ):
        named[count + u] = 0

    def body(j, c):
        for u in range(READ):
            p = named[READ * j + u]
            v = got[pl.ds(p * MSG, CAP), :]
            total = jnp.zeros((BLY, 128), F32)
            for k in range(CAP):
                x, y, z = corner(meta, p, k)
                for i in range(BLX):
                    piece = field[x + i, pl.ds(y + LOW, BLY), :]
                    total += block_rows(v, z, k, i, lane) * piece
            out[p] = jnp.sum(total, axis=0, keepdims=True)
        return c

    lax.fori_loop(0, (count + READ - 1) // READ, body, 0)


def pick_kernel(brick, counts, aper, got, out, rows):
    sub = iota((1, APER_DEV), 1)
    live = jnp.ones((1, APER_DEV), F32)
    for a in range(APER_DEV):
        p = aper[a]
        rows[a : a + 1, :] = got[brick[p]]
        live = jnp.where(sub == a, counts[p].astype(F32), live)
    out[...] = jnp.sum(rows[...], axis=1) / live[0]


def ring(array, axis, by):
    size = lax.axis_size(axis)
    return lax.ppermute(array, axis, [(i, (i + by) % size) for i in range(size)])


def on_device(
    ion_charge, density, charge_blocks, panel_brick, row_counts, block_offset, aperture_panel
):
    everyone = ("gx", "gy")
    ints = [pltpu.SMEM((n,), jnp.int32) for n in (PAN_DEV, PAN_DEV, PAN_DEV * CAP, APER_DEV)]
    (send,) = call(
        pack_kernel,
        [(PAN_DEV * MSG, 128)],
        [ANY] * 5,
        ints
        + [
            pltpu.VMEM((PAN_DEV * CAP, 128), F32),
            pltpu.SMEM((PAN_DEV,), jnp.int32),
            pltpu.SemaphoreType.DMA((5,)),
        ],
        60,
    )(panel_brick, row_counts, block_offset, aperture_panel, charge_blocks)
    send = send.reshape(PAN_DEV, 1, MSG * 128)
    got = lax.all_to_all(send, everyone, split_axis=0, concat_axis=0, tiled=True)
    got = got.reshape(PAN_DEV * MSG, 128)
    dy, dx, d_slabs = beside(
        0, WY, density[:HIGH], density[BX - LOW :], density[:, :16], density[:, BY - LOW :]
    )

    meta = [
        pltpu.VMEM((8, 128), jnp.int32),
        pltpu.SMEM((8, 128), jnp.int32),
        pltpu.SemaphoreType.DMA,
    ]
    charge, *slabs = call(
        deposit_kernel,
        [(DEPX, DEPY, NZ)] + [(HIGH, DEPY, NZ)] * 2 + [(DEPX, 16, NZ)] * 2,
        [VMEM] * 2 + [ANY] * 2,
        meta,
    )(got, ion_charge, *d_slabs)

    def tiles(n, width):
        return (n, width, 8, NZ)

    def layers(n):
        return pltpu.VMEM((n, WY, NZ), F32)

    def brick(width):
        slabs = [(HIGH - LOW, BY, NZ), (LOW, BY, NZ), (LOW, BY, NZ), (DEPX, width, NZ), (DEPX, LOW, NZ)]
        return [(BX, BY, NZ)] + slabs

    def spare(width):
        return [pltpu.VMEM(tiles(LOW + LOW + BLX, width), F32)] * 8

    work = 20_000_000_000
    cy, cx = charge_beside(*slabs, first=dx)
    *state, source, dens = call(
        inner_first,
        [tiles(BX, NEAR)] * 4 + [(DEPX, WY, NZ), (BX, WY, NZ)],
        [VMEM] * 6,
        (),
        32,
        work,
    )(charge, *cy, density, *dy)
    pot, ahead, *slabs, s_low, s_high = call(
        flank_first,
        brick(8) + [(HIGH, WY, NZ)] * 2,
        [VMEM] * 12,
        [layers(DEPX)] + spare(NEAR),
        32,
    )(*state, source, dens, *cx, *dx)
    for step in range(1, NEWTON):
        width = NEAR if step < NEWTON - 1 else TILES
        py, px, _ = beside(HIGH - LOW, 8 * width, *slabs)
        state = call(inner_next, [tiles(BX, width)] * 4, [VMEM] * 6, [layers(BX)], 32, work)(
            pot, *py, source, s_low, dens
        )
        operands = (*state, ahead, *py, *px, s_low, s_high, *dx)
        if step < NEWTON - 1:
            pot, ahead, *slabs = call(
                flank_next, brick(16), [VMEM] * 13, [layers(DEPX)] + spare(width), 32
            )(*operands)
    pot, sums = call(
        flank_last,
        [(BX, BY, NZ), (PAN_DEV, 1, 128)],
        [VMEM] * 14,
        [layers(DEPX)] + spare(TILES) + meta + [pltpu.SMEM((PAN_DEV + 8,), jnp.int32)],
        32,
    )(*operands, got)
    back = lax.all_to_all(sums, everyone, split_axis=0, concat_axis=0, tiled=True)
    (picked,) = call(
        pick_kernel,
        [(APER_DEV,)],
        [SMEM] * 3 + [VMEM],
        [pltpu.VMEM((APER_DEV, 128), F32)],
    )(panel_brick, row_counts, aperture_panel, back)
    return pot, picked


def solution(mesh):
    everyone = P(("gx", "gy"))
    grid = P("gx", "gy", None)
    return jax.shard_map(
        on_device,
        mesh=mesh,
        in_specs=(grid, grid, P(("gx", "gy"), None)) + (everyone,) * 4,
        out_specs=(grid, everyone),
        check_vma=False,
    )
```

```python
import functools

import jax
import jax.numpy as jnp
from jax import lax
from jax.experimental import pallas as pl
from jax.experimental.pallas import tpu as pltpu
from jax.sharding import PartitionSpec as P

BX = 32
BY = 64
NZ = 128
NEWTON = 3
SWEEPS = 8
CAP = 4
BLX = 4
BLY = 4
BLZ = 8
N_GX = 16
N_GY = 8
PAN_DEV = 128
APER_DEV = 16
MSG = CAP + 1
READ = 4
LOW = 8
HIGH = 11
TILES = 11
WY = 8 * TILES
BY_PRODUCT = 4
NEAR = 10
DEPX = BX + BLX - 1
DEPY = 72

VMEM = pl.BlockSpec(memory_space=pltpu.VMEM)
SMEM = pl.BlockSpec(memory_space=pltpu.SMEM)
ANY = pl.BlockSpec(memory_space=pl.ANY)
F32 = jnp.float32


def call(body, outs, ins, scratch=(), mib=24, flops=None):
    cost = None
    if flops is not None:
        cost = pl.CostEstimate(flops=flops, bytes_accessed=1 << 20, transcendentals=0)
    return pl.pallas_call(
        body,
        out_shape=[jax.ShapeDtypeStruct(s, F32) for s in outs],
        in_specs=list(ins),
        out_specs=[VMEM] * len(outs),
        scratch_shapes=list(scratch),
        cost_estimate=cost,
        compiler_params=pltpu.CompilerParams(vmem_limit_bytes=mib << 20),
    )


def iota(shape, dim):
    return lax.broadcasted_iota(jnp.int32, shape, dim)


def pack_kernel(*refs):
    arrays, density, (send, y_low, y_high) = refs[:5], refs[5], refs[6:9]
    local, need, sems = refs[9:14], refs[14], refs[15]
    copies = [pltpu.make_async_copy(a, b, sems.at[i]) for i, (a, b) in enumerate(zip(arrays, local))]
    cuts = [
        pltpu.make_async_copy(density.at[:, 0:16, :], y_low, sems.at[5]),
        pltpu.make_async_copy(density.at[:, BY - LOW : BY, :], y_high, sems.at[6]),
    ]
    for copy in copies + cuts:
        copy.start()
    brick, counts, offsets, aper, rows = local

    def clear(p, c):
        need[p] = 0
        return c

    lax.fori_loop(0, PAN_DEV, clear, 0, unroll=8)
    for copy in copies:
        copy.wait()
    for a in range(APER_DEV):
        need[aper[a]] = 1
    sub = iota((8, 128), 0)
    group = (iota((8, 128), 1) >> 3) & 3
    j = sub & 3
    masks = {e: (group == j - e) for e in range(-3, 4)}
    lane1 = iota((1, 128), 1)

    def body(q, c):
        p = q * 2
        live = sub < jnp.where(sub < 4, counts[p], counts[p + 1] + 4)
        v = jnp.where(live, rows[pl.ds(pl.multiple_of(q * 8, 8), 8), :], 0.0)
        out = v
        for e in (-3, -2, -1, 1, 2, 3):
            moved = pltpu.roll(pltpu.roll(v, e % 8, 0), (-8 * e) % 128, 1)
            out = jnp.where(masks[e], moved, out)
        for h in range(2):
            b = brick[p + h]
            send[pl.ds(b * MSG, 4), :] = out[4 * h : 4 * h + 4]
            meta = jnp.zeros((1, 128), jnp.int32)
            for k in range(CAP):
                meta = jnp.where(lane1 == k, offsets[(p + h) * CAP + k], meta)
            meta = jnp.where(lane1 == CAP, need[p + h], meta)
            send[pl.ds(b * MSG + 4, 1), :] = meta.astype(F32)
        return c

    lax.fori_loop(0, PAN_DEV // 2, body, 0, unroll=4)
    for copy in cuts:
        copy.wait()


def numbers(got, turned, meta, sem):
    rows = got[pl.ds(CAP, PAN_DEV, stride=MSG), :]
    turned[...] = jnp.transpose(rows)[0:8].astype(jnp.int32)
    copy = pltpu.make_async_copy(turned, meta, sem)
    copy.start()
    return copy


def corner(meta, p, k):
    offset = meta[k, p]
    return offset >> 13, (offset >> 7) & 63, offset & 127


def block_rows(v, z, k, i, lane):
    moved = pltpu.roll(v, (z - 32 * i - 8 * k + 128) & 127, 1)
    return jnp.where((lane >= z) & (lane < z + BLZ), moved, 0.0)


def deposit_kernel(got, ion, unused_low, unused_high, out, x_low, x_high, y_low, y_high, turned, meta, sem):
    copy = numbers(got, turned, meta, sem)
    out[0:BX, 0:BY, :] = ion[...]
    out[0:BX, BY:DEPY, :] = jnp.zeros((BX, DEPY - BY, NZ), F32)
    out[BX:DEPX] = jnp.zeros((DEPX - BX, DEPY, NZ), F32)
    lane = iota((BLY, 128), 1)
    copy.wait()

    def body(p, c):
        v = got[pl.ds(p * MSG, CAP), :]
        for k in range(CAP):
            x, y, z = corner(meta, p, k)
            add = [block_rows(v, z, k, i, lane) for i in range(BLX)]
            old = [out[x + i, pl.ds(y, BLY), :] for i in range(BLX)]
            for i in range(BLX):
                out[x + i, pl.ds(y, BLY), :] = old[i] + add[i]
        return c

    lax.fori_loop(0, PAN_DEV, body, 0, unroll=16)
    x_low[...] = out[0:HIGH]
    x_high[...] = out[BX - LOW : DEPX]
    y_low[...] = out[:, 0:16]
    y_high[...] = out[:, BY - LOW : DEPY]


def inside_y(tiles):
    gy = lax.axis_index("gy")
    lo = jnp.where(gy == 0, LOW, 0)
    hi = jnp.where(gy == N_GY - 1, LOW + BY, WY)
    sub = iota((8, 128), 0)
    ys = [sub * tiles + t for t in range(tiles)]
    return [(y >= lo) & (y < hi) for y in ys]


def lay(nat, at, count, own, below, above):
    nat[at : at + count, 0:LOW] = below
    nat[at : at + count, LOW : LOW + BY] = own
    nat[at : at + count, LOW + BY : LOW + BY + above.shape[1]] = above


def lay_charge(nat, at, count, own, below, spilled, above):
    spread = jnp.where(lax.axis_index("gy") > 0, 1.0, 0.0)
    nat[at : at + count, 0:LOW] = below
    nat[at : at + count, LOW : LOW + DEPY] = own
    nat[at : at + count, LOW : LOW + BLY - 1] += spilled * spread
    nat[at : at + count, LOW + BY : LOW + DEPY] += above[:, 0:8]
    nat[at : at + count, LOW + DEPY : LOW + DEPY + 3] = above[:, 8:HIGH]
    nat[at : at + count, LOW + DEPY + 3 : WY] = jnp.zeros((count, WY - LOW - DEPY - 3, NZ), F32)


def strided(nat, x, t, tiles):
    return nat[x, pl.ds(t, 8, stride=tiles), :]


def relax(layers, write):
    tiles = len(layers[0])
    rolled = tiles - BY_PRODUCT
    lane = iota((8, 128), 1)
    first, last = lane == 0, lane == NZ - 1
    inner_layers = layers[1:-1]
    flat = jnp.concatenate(sum([cur[rolled:] for cur in inner_layers], []), axis=0)
    high = flat.astype(jnp.bfloat16)
    low = (flat - high.astype(F32)).astype(jnp.bfloat16)
    from_z, to_z = iota((2 * NZ, NZ), 0) & (NZ - 1), iota((2 * NZ, NZ), 1)
    beside_z = jnp.where((from_z - to_z == 1) | (to_z - from_z == 1), 1.0, 0.0)
    product = jnp.dot(
        jnp.concatenate([high, low], axis=1),
        beside_z.astype(jnp.bfloat16),
        preferred_element_type=F32,
    )
    for u in range(len(inner_layers)):
        prev, cur, nxt = layers[u : u + 3]
        before = [pltpu.roll(cur[-1], 1, 0)] + cur[:-1]
        after = cur[1:] + [pltpu.roll(cur[0], 7, 0)]
        for t in range(tiles):
            if t < rolled:
                left = jnp.where(first, 0.0, pltpu.roll(cur[t], 1, 1))
                along_z = left + jnp.where(last, 0.0, pltpu.roll(cur[t], NZ - 1, 1))
            else:
                at = (u * BY_PRODUCT + t - rolled) * 8
                along_z = product[at : at + 8]
            total = (prev[t] + nxt[t]) + (before[t] + after[t]) + along_z
            write(u, t, total)


def layer(buf, x):
    return [buf[x, t] for t in range(buf.shape[1])]


def sweep(src, dst, rhs, inv, lo, hi):
    def rows(x0, count):
        def write(u, t, total):
            dst[x0 + u, t] = (rhs[x0 + u, t] + total) * inv[x0 + u, t]

        relax([layer(src, x0 - 1 + u) for u in range(count + 2)], write)

    count = (hi - lo + 1) // 2

    def body(i, c):
        rows(lo + i * count, count)
        return c

    lax.fori_loop(0, (hi - lo) // count, body, 0)
    if (hi - lo) % count:
        rows(lo + count, (hi - lo) % count)


def inner(b0, b1, rhs, inv, k0, a, h):
    bufs = (b0, b1)
    for k in range(k0, SWEEPS + 1):
        sweep(bufs[(k - 1) % 2], bufs[k % 2], rhs, inv, a + k, h - k)


def inner_first(charge, y_below, y_above, density, d_below, d_above, *refs):
    b0, b1, rhs, inv, source, dens = refs
    tiles = b0.shape[1]
    inside = inside_y(tiles)
    lay(dens, 0, BX, density[...], d_below[...], d_above[...])
    lay_charge(source, 0, DEPX, charge[...], y_below[:, 0:8], y_below[:, 8:HIGH], y_above)

    def prep(x, c):
        for t in range(tiles):
            s = strided(source, x, t, tiles)
            d = strided(dens, x, t, tiles)
            scale = jnp.where(inside[t], 1.0 / (6.0 + d), 0.0)
            inv[x, t] = scale
            rhs[x, t] = s - d
            b1[x, t] = (s - d) * scale
        return c

    lax.fori_loop(0, BX, prep, 0, unroll=2)
    inner(b0, b1, rhs, inv, 2, BLX - 2, BX + 1)


def start(p_nat, p_at, s, s_at, d, inside, f, outs, to, x):
    p_out, rhs, inv = outs
    tiles = p_out.shape[1]
    for t in range(tiles):
        p = jnp.where(inside[t], strided(p_nat, x + p_at, t, tiles) * f, 0.0)
        coef = strided(d, x, t, tiles) * jnp.exp(p)
        p_out[x + to, t] = p
        rhs[x + to, t] = strided(s, x + s_at, t, tiles) + coef * (p - 1.0)
        inv[x + to, t] = jnp.where(inside[t], f / (6.0 + coef), 0.0)


def inner_next(own, y_below, y_above, source, s_low, dens, b0, b1, rhs, inv, nat):
    inside = inside_y(b0.shape[1])
    lay(nat, 0, BX, own[...], y_below[0:BX], y_above[0:BX])
    outs = (b0, rhs, inv)

    def prep_from(src, at):
        def prep(x, c):
            start(nat, 0, src, at, dens, inside, 1.0, outs, 0, x)
            return c

        return prep

    lax.fori_loop(0, BLX - 1, prep_from(s_low, LOW), 0)
    lax.fori_loop(BLX - 1, BX, prep_from(source, 0), 0)
    inner(b0, b1, rhs, inv, 1, 0, BX)


def flanks(b0, b1, lows, highs, rhs, inv, k0, a, h):
    (l0, l1, l_rhs, l_inv), (h0, h1, h_rhs, h_inv) = lows, highs
    n_low, n_high = LOW + a, BX + HIGH - h
    for i in range(LOW + a):
        if i + LOW >= len_low_halo(a):
            l_rhs[i + LOW], l_inv[i + LOW] = rhs[i], inv[i]
    for i in range(h - LOW, BX):
        h_rhs[i - (h - LOW)], h_inv[i - (h - LOW)] = rhs[i], inv[i]

    def one(k, near, l_src, l_dst, h_src, h_dst):
        def low_write(u, t, total):
            l_dst[k + u, t] = (l_rhs[k + u, t] + total) * l_inv[k + u, t]

        def high_write(u, t, total):
            r = LOW - k + u
            h_dst[r, t] = (h_rhs[r, t] + total) * h_inv[r, t]

        low = [layer(l_src, k - 1 + j) for j in range(n_low)]
        relax(low + [layer(near, a + k - 1), layer(near, a + k)], low_write)
        high = [layer(h_src, LOW + 1 - k + j) for j in range(n_high)]
        relax([layer(near, h - k - 1), layer(near, h - k)] + high, high_write)

    if k0 == 2:
        one(2, b1, l1, l0, h1, h0)

    def body(j, c):
        one(2 * j + 1, b0, l0, l1, h0, h1)
        one(2 * j + 2, b1, l1, l0, h1, h0)
        return c

    lax.fori_loop(k0 - 1, SWEEPS // 2, body, 0)


def len_low_halo(a):
    return LOW + (BLX - 1 if a else 0)


def finish(b0, l0, h0, nat, a, h):
    tiles = b0.shape[1]

    def take(src, shift):
        def body(x, c):
            for t in range(tiles):
                nat[x, pl.ds(t, 8, stride=tiles), :] = src[x + shift, t]
            return c

        return body

    lax.fori_loop(0, a + LOW, take(l0, LOW), 0, unroll=2)
    lax.fori_loop(a + LOW, h - LOW, take(b0, 0), 0, unroll=2)
    lax.fori_loop(h - LOW, DEPX, take(h0, LOW - h), 0, unroll=2)


def hand_on(nat, out, ahead, x_low, x_high, y_low, y_high):
    out[...] = nat[0:BX, LOW : LOW + BY]
    x_low[...] = nat[HIGH - LOW : HIGH, LOW : LOW + BY]
    ahead[...] = nat[BX:DEPX, LOW : LOW + BY]
    x_high[...] = nat[BX - LOW : BX, LOW : LOW + BY]
    y_low[...] = nat[0:DEPX, LOW : LOW + y_low.shape[1]]
    y_high[...] = nat[0:DEPX, BY : LOW + BY]


def edges():
    gx = lax.axis_index("gx")
    return jnp.where(gx > 0, 1.0, 0.0), jnp.where(gx < N_GX - 1, 1.0, 0.0)


def flank_first(*refs):
    b0, b1, rhs, inv, source, dens, x_below, x_above, c_below, c_above, d_below, d_above = refs[:12]
    outs, (s_low, s_high), nat, spare = refs[12:18], refs[18:20], refs[20], refs[21:]
    l0, l1, l_rhs, l_inv, h0, h1, h_rhs, h_inv = spare
    a, h = BLX - 2, BX + 1
    tiles = NEAR
    inside, (f_low, f_high) = inside_y(tiles), edges()
    for c, s, x in ((c_below, s_low, x_below), (c_above, s_high, x_above)):
        lay_charge(s, 0, HIGH, x[...], c[:, 0:8], c[:, 19:22], c[:, 8:19])
    s_low[LOW:HIGH] = source[0 : HIGH - LOW] + s_low[LOW:HIGH] * f_low
    s_high[0 : DEPX - BX] += source[BX:DEPX]

    def fill(count, s, s_at, d, d_at, f, at, p_out, rhs_out, inv_out):
        def body(r, c):
            for t in range(tiles):
                den = strided(d, r + d_at, t, tiles)
                scale = jnp.where(inside[t], f / (6.0 + den), 0.0)
                value = strided(s, r + s_at, t, tiles) - den
                rhs_out[r + at, t], inv_out[r + at, t] = value, scale
                p_out[r + at, t] = value * scale
            return c

        lax.fori_loop(0, count, body, 0)

    fill(LOW, s_low, 0, d_below, 0, f_low, 0, l1, l_rhs, l_inv)
    fill(BLX - 1, s_low, LOW, dens, 0, 1.0, LOW, l1, l_rhs, l_inv)
    fill(HIGH, s_high, 0, d_above, 0, f_high, LOW - 1, h1, h_rhs, h_inv)
    lows, highs = (l0, l1, l_rhs, l_inv), (h0, h1, h_rhs, h_inv)
    flanks(b0, b1, lows, highs, rhs, inv, 2, a, h)
    finish(b0, l0, h0, nat, a, h)
    hand_on(nat, *outs)


def next_flanks(refs, nat, spare):
    b0, b1, rhs, inv, ahead, y_below, y_above, x_below, x_above, c_below, c_above = refs[:11]
    s_low, s_high, d_low, d_high = refs[11:]
    l0, l1, l_rhs, l_inv, h0, h1, h_rhs, h_inv = spare
    inside, (f_low, f_high) = inside_y(b0.shape[1]), edges()

    def low_body(r, c):
        start(nat, HIGH, s_low, 0, d_low, inside, f_low, (l0, l_rhs, l_inv), 0, r)
        return c

    more = HIGH - LOW
    lay(nat, 0, more, ahead[...], y_below[BX:DEPX], y_above[BX:DEPX])
    lay(nat, more, LOW, x_above[...], c_above[:, 0:LOW], c_above[:, LOW:])
    lay(nat, HIGH, LOW, x_below[...], c_below[:, 0:LOW], c_below[:, LOW:])

    def high_body(r, c):
        start(nat, 0, s_high, 0, d_high, inside, f_high, (h0, h_rhs, h_inv), LOW, r)
        return c

    lax.fori_loop(0, LOW, low_body, 0)
    lax.fori_loop(0, HIGH, high_body, 0)
    lows, highs = (l0, l1, l_rhs, l_inv), (h0, h1, h_rhs, h_inv)
    flanks(b0, b1, lows, highs, rhs, inv, 1, 0, BX)
    finish(b0, l0, h0, nat, 0, BX)


def flank_next(*refs):
    outs, (nat, *spare) = refs[15:21], refs[21:]
    next_flanks(refs[:15], nat, spare)
    hand_on(nat, *outs)


def flank_last(*refs):
    (got, out, sums, nat), spare, (turned, meta, sem, named) = refs[15:19], refs[19:27], refs[27:]
    copy = numbers(got, turned, meta, sem)
    next_flanks(refs[:15], nat, spare)
    out[...] = nat[0:BX, LOW : LOW + BY]
    copy.wait()
    read(got, nat, sums, meta, named)


def slab_kernel(x_low, x_high, below, above, low, high):
    lay(low, 0, HIGH, x_low[...], below[0:HIGH], above[0:HIGH])
    lay(high, 0, LOW, x_high[...], below[BX - LOW :], above[BX - LOW :])


def beside(x_low, x_high, y_low, y_high):
    y_below, y_above = ring(y_high, "gy", 1), ring(y_low, "gy", -1)
    low, high = call(slab_kernel, [(HIGH, WY, NZ), (LOW, WY, NZ)], [VMEM] * 4)(
        x_low, x_high, y_below, y_above
    )
    x_below, x_above = ring(high, "gx", 1), ring(low, "gx", -1)
    return (y_below, y_above), (x_below, x_above), (low, high)


def strip_kernel(below, above, low, high):
    for at, strip in ((HIGH - LOW, low), (BX - LOW, high)):
        strip[:, 0:LOW] = below[at : at + LOW]
        strip[:, LOW:] = above[at : at + LOW]


def corner_kernel(below, above, unused_low, unused_high, low, high):
    for at, strip in ((0, low), (BX - LOW, high)):
        strip[:, 0:8] = below[at : at + HIGH, 0:8]
        strip[:, 8:16] = above[at : at + HIGH, 0:8]
        strip[:, 16:19] = above[at : at + HIGH, 8:HIGH]
        strip[:, 19:22] = below[at : at + HIGH, 8:HIGH]
        strip[:, 22:24] = jnp.zeros((HIGH, 2, NZ), F32)


def around(x_low, x_high, y_low, y_high, body, strip, first=()):
    x_below, x_above = ring(x_high, "gx", 1), ring(x_low, "gx", -1)
    y_below, y_above = ring(y_high, "gy", 1), ring(y_low, "gy", -1)
    low, high = call(body, [strip] * 2, [VMEM] * 2 + [ANY] * len(first))(y_below, y_above, *first)
    c_below, c_above = ring(high, "gx", 1), ring(low, "gx", -1)
    return (y_below, y_above), (x_below, x_above, c_below, c_above)


def read(got, field, out, meta, named):
    lane = iota((BLY, 128), 1)

    def note(p, n):
        named[n] = p
        return n + meta[CAP, p]

    count = lax.fori_loop(0, PAN_DEV, note, 0, unroll=8)
    for u in range(READ):
        named[count + u] = 0

    def body(j, c):
        for u in range(READ):
            p = named[READ * j + u]
            v = got[pl.ds(p * MSG, CAP), :]
            total = jnp.zeros((BLY, 128), F32)
            for k in range(CAP):
                x, y, z = corner(meta, p, k)
                for i in range(BLX):
                    piece = field[x + i, pl.ds(y + LOW, BLY), :]
                    total += block_rows(v, z, k, i, lane) * piece
            out[p] = jnp.sum(total, axis=0, keepdims=True)
        return c

    lax.fori_loop(0, (count + READ - 1) // READ, body, 0)


def pick_kernel(brick, counts, aper, got, out, rows):
    sub = iota((1, APER_DEV), 1)
    live = jnp.ones((1, APER_DEV), F32)
    for a in range(APER_DEV):
        p = aper[a]
        rows[a : a + 1, :] = got[brick[p]]
        live = jnp.where(sub == a, counts[p].astype(F32), live)
    out[...] = jnp.sum(rows[...], axis=1) / live[0]


def ring(array, axis, by):
    size = lax.axis_size(axis)
    return lax.ppermute(array, axis, [(i, (i + by) % size) for i in range(size)])


def on_device(
    ion_charge, density, charge_blocks, panel_brick, row_counts, block_offset, aperture_panel
):
    everyone = ("gx", "gy")
    ints = [pltpu.SMEM((n,), jnp.int32) for n in (PAN_DEV, PAN_DEV, PAN_DEV * CAP, APER_DEV)]
    send, *d_slabs = call(
        pack_kernel,
        [(PAN_DEV * MSG, 128), (BX, 16, NZ), (BX, LOW, NZ)],
        [ANY] * 6,
        ints
        + [
            pltpu.VMEM((PAN_DEV * CAP, 128), F32),
            pltpu.SMEM((PAN_DEV,), jnp.int32),
            pltpu.SemaphoreType.DMA((7,)),
        ],
        60,
    )(panel_brick, row_counts, block_offset, aperture_panel, charge_blocks, density)
    send = send.reshape(PAN_DEV, 1, MSG * 128)
    got = lax.all_to_all(send, everyone, split_axis=0, concat_axis=0, tiled=True)
    got = got.reshape(PAN_DEV * MSG, 128)
    dy, dx, d_slabs = beside(density[:HIGH], density[BX - LOW :], *d_slabs)

    meta = [
        pltpu.VMEM((8, 128), jnp.int32),
        pltpu.SMEM((8, 128), jnp.int32),
        pltpu.SemaphoreType.DMA,
    ]
    charge, *slabs = call(
        deposit_kernel,
        [(DEPX, DEPY, NZ)] + [(HIGH, DEPY, NZ)] * 2 + [(DEPX, 16, NZ)] * 2,
        [VMEM] * 2 + [ANY] * 2,
        meta,
    )(got, ion_charge, *d_slabs)

    def tiles(n, width):
        return (n, width, 8, NZ)

    def layers(n):
        return pltpu.VMEM((n, WY, NZ), F32)

    def brick(width):
        slabs = [(HIGH - LOW, BY, NZ), (LOW, BY, NZ), (LOW, BY, NZ), (DEPX, width, NZ), (DEPX, LOW, NZ)]
        return [(BX, BY, NZ)] + slabs

    def spare(width):
        return [pltpu.VMEM(tiles(LOW + LOW + BLX, width), F32)] * 8

    work = 20_000_000_000
    cy, cx = around(*slabs, corner_kernel, (HIGH, 24, NZ), dx)
    *state, source, dens = call(
        inner_first,
        [tiles(BX, NEAR)] * 4 + [(DEPX, WY, NZ), (BX, WY, NZ)],
        [VMEM] * 6,
        (),
        32,
        work,
    )(charge, *cy, density, *dy)
    pot, ahead, *slabs, s_low, s_high = call(
        flank_first,
        brick(8) + [(HIGH, WY, NZ)] * 2,
        [VMEM] * 12,
        [layers(DEPX)] + spare(NEAR),
        32,
    )(*state, source, dens, *cx, *dx)
    for step in range(1, NEWTON):
        width = NEAR if step < NEWTON - 1 else TILES
        py, px = around(*slabs, strip_kernel, (LOW, 8 * width - BY, NZ))
        state = call(inner_next, [tiles(BX, width)] * 4, [VMEM] * 6, [layers(BX)], 32, work)(
            pot, *py, source, s_low, dens
        )
        operands = (*state, ahead, *py, *px, s_low, s_high, *dx)
        if step < NEWTON - 1:
            pot, ahead, *slabs = call(
                flank_next, brick(16), [VMEM] * 15, [layers(DEPX)] + spare(width), 32
            )(*operands)
    pot, sums = call(
        flank_last,
        [(BX, BY, NZ), (PAN_DEV, 1, 128)],
        [VMEM] * 16,
        [layers(DEPX)] + spare(TILES) + meta + [pltpu.SMEM((PAN_DEV + 8,), jnp.int32)],
        32,
    )(*operands, got)
    back = lax.all_to_all(sums, everyone, split_axis=0, concat_axis=0, tiled=True)
    (picked,) = call(
        pick_kernel,
        [(APER_DEV,)],
        [SMEM] * 3 + [VMEM],
        [pltpu.VMEM((APER_DEV, 128), F32)],
    )(panel_brick, row_counts, aperture_panel, back)
    return pot, picked


def solution(mesh):
    everyone = P(("gx", "gy"))
    grid = P("gx", "gy", None)
    return jax.shard_map(
        on_device,
        mesh=mesh,
        in_specs=(grid, grid, P(("gx", "gy"), None)) + (everyone,) * 4,
        out_specs=(grid, everyone),
        check_vma=False,
    )
```

```python
import functools

import jax
import jax.numpy as jnp
from jax import lax
from jax.experimental import pallas as pl
from jax.experimental.pallas import tpu as pltpu
from jax.sharding import PartitionSpec as P

BX = 32
BY = 64
NZ = 128
NEWTON = 3
SWEEPS = 8
CAP = 4
BLX = 4
BLY = 4
BLZ = 8
N_GX = 16
N_GY = 8
PAN_DEV = 128
APER_DEV = 16
MSG = CAP + 1
READ = 4
LOW = 8
HIGH = 11
TILES = 11
SRC = HIGH - 1
WY = 8 * TILES
BY_PRODUCT = 4
NEAR = 10
DEPX = BX + BLX - 1
DEPY = 72

VMEM = pl.BlockSpec(memory_space=pltpu.VMEM)
SMEM = pl.BlockSpec(memory_space=pltpu.SMEM)
ANY = pl.BlockSpec(memory_space=pl.ANY)
F32 = jnp.float32


def call(body, outs, ins, scratch=(), mib=24, flops=None):
    cost = None
    if flops is not None:
        cost = pl.CostEstimate(flops=flops, bytes_accessed=1 << 20, transcendentals=0)
    return pl.pallas_call(
        body,
        out_shape=[jax.ShapeDtypeStruct(s, F32) for s in outs],
        in_specs=list(ins),
        out_specs=[VMEM] * len(outs),
        scratch_shapes=list(scratch),
        cost_estimate=cost,
        compiler_params=pltpu.CompilerParams(vmem_limit_bytes=mib << 20),
    )


def iota(shape, dim):
    return lax.broadcasted_iota(jnp.int32, shape, dim)


def pack_kernel(*refs):
    arrays, density, (send, y_low, y_high) = refs[:5], refs[5], refs[6:9]
    local, need, sems = refs[9:14], refs[14], refs[15]
    copies = [pltpu.make_async_copy(a, b, sems.at[i]) for i, (a, b) in enumerate(zip(arrays, local))]
    cuts = [
        pltpu.make_async_copy(density.at[:, 0:16, :], y_low, sems.at[5]),
        pltpu.make_async_copy(density.at[:, BY - LOW : BY, :], y_high, sems.at[6]),
    ]
    for copy in copies + cuts:
        copy.start()
    brick, counts, offsets, aper, rows = local

    def clear(p, c):
        need[p] = 0
        return c

    lax.fori_loop(0, PAN_DEV, clear, 0, unroll=8)
    for copy in copies:
        copy.wait()
    for a in range(APER_DEV):
        need[aper[a]] = 1
    sub = iota((8, 128), 0)
    group = (iota((8, 128), 1) >> 3) & 3
    j = sub & 3
    masks = {e: (group == j - e) for e in range(-3, 4)}
    lane1 = iota((1, 128), 1)

    def body(q, c):
        p = q * 2
        live = sub < jnp.where(sub < 4, counts[p], counts[p + 1] + 4)
        v = jnp.where(live, rows[pl.ds(pl.multiple_of(q * 8, 8), 8), :], 0.0)
        out = v
        for e in (-3, -2, -1, 1, 2, 3):
            moved = pltpu.roll(pltpu.roll(v, e % 8, 0), (-8 * e) % 128, 1)
            out = jnp.where(masks[e], moved, out)
        for h in range(2):
            b = brick[p + h]
            send[pl.ds(b * MSG, 4), :] = out[4 * h : 4 * h + 4]
            meta = jnp.zeros((1, 128), jnp.int32)
            for k in range(CAP):
                meta = jnp.where(lane1 == k, offsets[(p + h) * CAP + k], meta)
            meta = jnp.where(lane1 == CAP, need[p + h], meta)
            send[pl.ds(b * MSG + 4, 1), :] = meta.astype(F32)
        return c

    lax.fori_loop(0, PAN_DEV // 2, body, 0, unroll=4)
    for copy in cuts:
        copy.wait()


def numbers(got, turned, meta, sem):
    rows = got[pl.ds(CAP, PAN_DEV, stride=MSG), :]
    turned[...] = jnp.transpose(rows)[0:8].astype(jnp.int32)
    copy = pltpu.make_async_copy(turned, meta, sem)
    copy.start()
    return copy


def corner(meta, p, k):
    offset = meta[k, p]
    return offset >> 13, (offset >> 7) & 63, offset & 127


def block_rows(v, z, k, i, lane):
    moved = pltpu.roll(v, (z - 32 * i - 8 * k + 128) & 127, 1)
    return jnp.where((lane >= z) & (lane < z + BLZ), moved, 0.0)


def deposit_kernel(got, ion, unused_low, unused_high, out, x_low, x_high, y_low, y_high, turned, meta, sem):
    copy = numbers(got, turned, meta, sem)
    out[0:BX, 0:BY, :] = ion[...]
    out[0:BX, BY:DEPY, :] = jnp.zeros((BX, DEPY - BY, NZ), F32)
    out[BX:DEPX] = jnp.zeros((DEPX - BX, DEPY, NZ), F32)
    lane = iota((BLY, 128), 1)
    copy.wait()

    def body(p, c):
        v = got[pl.ds(p * MSG, CAP), :]
        for k in range(CAP):
            x, y, z = corner(meta, p, k)
            add = [block_rows(v, z, k, i, lane) for i in range(BLX)]
            old = [out[x + i, pl.ds(y, BLY), :] for i in range(BLX)]
            for i in range(BLX):
                out[x + i, pl.ds(y, BLY), :] = old[i] + add[i]
        return c

    lax.fori_loop(0, PAN_DEV, body, 0, unroll=16)
    x_low[...] = out[0:SRC]
    x_high[...] = out[DEPX - SRC : DEPX]
    y_low[...] = out[:, 0:16]
    y_high[...] = out[:, BY - LOW : DEPY]


def inside_y(tiles):
    gy = lax.axis_index("gy")
    lo = jnp.where(gy == 0, LOW, 0)
    hi = jnp.where(gy == N_GY - 1, LOW + BY, WY)
    sub = iota((8, 128), 0)
    ys = [sub * tiles + t for t in range(tiles)]
    return [(y >= lo) & (y < hi) for y in ys]


def lay(nat, at, count, own, below, above):
    nat[at : at + count, 0:LOW] = below
    nat[at : at + count, LOW : LOW + BY] = own
    nat[at : at + count, LOW + BY : LOW + BY + above.shape[1]] = above


def lay_charge(nat, at, count, own, below, spilled, above):
    spread = jnp.where(lax.axis_index("gy") > 0, 1.0, 0.0)
    nat[at : at + count, 0:LOW] = below
    nat[at : at + count, LOW : LOW + DEPY] = own
    nat[at : at + count, LOW : LOW + BLY - 1] += spilled * spread
    nat[at : at + count, LOW + BY : LOW + DEPY] += above[:, 0:8]
    nat[at : at + count, LOW + DEPY : LOW + DEPY + 3] = above[:, 8:HIGH]
    nat[at : at + count, LOW + DEPY + 3 : WY] = jnp.zeros((count, WY - LOW - DEPY - 3, NZ), F32)


def strided(nat, x, t, tiles):
    return nat[x, pl.ds(t, 8, stride=tiles), :]


def relax(layers, write):
    tiles = len(layers[0])
    rolled = tiles - BY_PRODUCT
    lane = iota((8, 128), 1)
    first, last = lane == 0, lane == NZ - 1
    inner_layers = layers[1:-1]
    flat = jnp.concatenate(sum([cur[rolled:] for cur in inner_layers], []), axis=0)
    high = flat.astype(jnp.bfloat16)
    low = (flat - high.astype(F32)).astype(jnp.bfloat16)
    from_z, to_z = iota((2 * NZ, NZ), 0) & (NZ - 1), iota((2 * NZ, NZ), 1)
    beside_z = jnp.where((from_z - to_z == 1) | (to_z - from_z == 1), 1.0, 0.0)
    product = jnp.dot(
        jnp.concatenate([high, low], axis=1),
        beside_z.astype(jnp.bfloat16),
        preferred_element_type=F32,
    )
    for u in range(len(inner_layers)):
        prev, cur, nxt = layers[u : u + 3]
        before = [pltpu.roll(cur[-1], 1, 0)] + cur[:-1]
        after = cur[1:] + [pltpu.roll(cur[0], 7, 0)]
        for t in range(tiles):
            if t < rolled:
                left = jnp.where(first, 0.0, pltpu.roll(cur[t], 1, 1))
                along_z = left + jnp.where(last, 0.0, pltpu.roll(cur[t], NZ - 1, 1))
            else:
                at = (u * BY_PRODUCT + t - rolled) * 8
                along_z = product[at : at + 8]
            total = (prev[t] + nxt[t]) + (before[t] + after[t]) + along_z
            write(u, t, total)


def layer(buf, x):
    return [buf[x, t] for t in range(buf.shape[1])]


def sweep(src, dst, rhs, inv, lo, hi):
    def write(u, t, total):
        dst[lo + u, t] = (rhs[lo + u, t] + total) * inv[lo + u, t]

    relax([layer(src, x) for x in range(lo - 1, hi + 1)], write)


def inner(b0, b1, rhs, inv, k0, a, h):
    bufs = (b0, b1)
    for k in range(k0, SWEEPS + 1):
        sweep(bufs[(k - 1) % 2], bufs[k % 2], rhs, inv, a + k, h - k)


def inner_first(charge, y_below, y_above, density, d_below, d_above, *refs):
    b0, b1, rhs, inv, source, dens = refs
    tiles = b0.shape[1]
    inside = inside_y(tiles)
    lay(dens, 0, BX, density[...], d_below[...], d_above[...])
    lay_charge(source, 0, DEPX, charge[...], y_below[:, 0:8], y_below[:, 8:HIGH], y_above)

    def prep(x, c):
        for t in range(tiles):
            s = strided(source, x, t, tiles)
            d = strided(dens, x, t, tiles)
            scale = jnp.where(inside[t], 1.0 / (6.0 + d), 0.0)
            inv[x, t] = scale
            rhs[x, t] = s - d
            b1[x, t] = (s - d) * scale
        return c

    lax.fori_loop(0, BX, prep, 0, unroll=8)
    inner(b0, b1, rhs, inv, 2, BLX - 2, BX + 1)


def start(p_nat, p_at, s, s_at, d, inside, f, outs, to, x):
    p_out, rhs, inv = outs
    tiles = p_out.shape[1]
    for t in range(tiles):
        p = jnp.where(inside[t], strided(p_nat, x + p_at, t, tiles) * f, 0.0)
        coef = strided(d, x, t, tiles) * jnp.exp(p)
        p_out[x + to, t] = p
        rhs[x + to, t] = strided(s, x + s_at, t, tiles) + coef * (p - 1.0)
        inv[x + to, t] = jnp.where(inside[t], f / (6.0 + coef), 0.0)


def inner_next(own, y_below, y_above, source, s_low, dens, b0, b1, rhs, inv, nat):
    inside = inside_y(b0.shape[1])
    lay(nat, 0, BX, own[...], y_below[0:BX], y_above[0:BX])
    outs = (b0, rhs, inv)

    def prep_from(src, at):
        def prep(x, c):
            start(nat, 0, src, at, dens, inside, 1.0, outs, 0, x)
            return c

        return prep

    lax.fori_loop(0, BLX - 1, prep_from(s_low, LOW), 0, unroll=BLX - 1)
    lax.fori_loop(BLX - 1, BX, prep_from(source, 0), 0, unroll=8)
    inner(b0, b1, rhs, inv, 1, 0, BX)


def flanks(b0, b1, lows, highs, rhs, inv, k0, a, h):
    (l0, l1, l_rhs, l_inv), (h0, h1, h_rhs, h_inv) = lows, highs
    n_low, n_high = LOW + a, BX + HIGH - h
    for i in range(LOW + a):
        if i + LOW >= len_low_halo(a):
            l_rhs[i + LOW], l_inv[i + LOW] = rhs[i], inv[i]
    for i in range(h - LOW, BX):
        h_rhs[i - (h - LOW)], h_inv[i - (h - LOW)] = rhs[i], inv[i]

    def one(k, near, l_src, l_dst, h_src, h_dst):
        def low_write(u, t, total):
            l_dst[k + u, t] = (l_rhs[k + u, t] + total) * l_inv[k + u, t]

        def high_write(u, t, total):
            r = LOW - k + u
            h_dst[r, t] = (h_rhs[r, t] + total) * h_inv[r, t]

        low = [layer(l_src, k - 1 + j) for j in range(n_low)]
        relax(low + [layer(near, a + k - 1), layer(near, a + k)], low_write)
        high = [layer(h_src, LOW + 1 - k + j) for j in range(n_high)]
        relax([layer(near, h - k - 1), layer(near, h - k)] + high, high_write)

    if k0 == 2:
        one(2, b1, l1, l0, h1, h0)

    def body(j, c):
        one(2 * j + 1, b0, l0, l1, h0, h1)
        one(2 * j + 2, b1, l1, l0, h1, h0)
        return c

    lax.fori_loop(k0 - 1, SWEEPS // 2, body, 0)


def len_low_halo(a):
    return LOW + (BLX - 1 if a else 0)


def finish(b0, l0, h0, nat, a, h):
    tiles = b0.shape[1]

    def take(src, shift):
        def body(x, c):
            for t in range(tiles):
                nat[x, pl.ds(t, 8, stride=tiles), :] = src[x + shift, t]
            return c

        return body

    lax.fori_loop(0, a + LOW, take(l0, LOW), 0, unroll=8)
    lax.fori_loop(a + LOW, h - LOW, take(b0, 0), 0, unroll=8)
    lax.fori_loop(h - LOW, DEPX, take(h0, LOW - h), 0, unroll=11)


def hand_on(nat, out, ahead, x_low, x_high, y_low, y_high):
    out[...] = nat[0:BX, LOW : LOW + BY]
    x_low[...] = nat[HIGH - LOW : HIGH, LOW : LOW + BY]
    ahead[...] = nat[BX:DEPX, LOW : LOW + BY]
    x_high[...] = nat[BX - LOW : BX, LOW : LOW + BY]
    y_low[...] = nat[0:DEPX, LOW : LOW + y_low.shape[1]]
    y_high[...] = nat[0:DEPX, BY : LOW + BY]


def edges():
    gx = lax.axis_index("gx")
    return jnp.where(gx > 0, 1.0, 0.0), jnp.where(gx < N_GX - 1, 1.0, 0.0)


def flank_first(*refs):
    b0, b1, rhs, inv, source, dens, x_below, x_above, c_below, c_above, d_below, d_above = refs[:12]
    outs, (s_low, s_high), nat, spare = refs[12:18], refs[18:20], refs[20], refs[21:]
    l0, l1, l_rhs, l_inv, h0, h1, h_rhs, h_inv = spare
    a, h = BLX - 2, BX + 1
    tiles = NEAR
    inside, (f_low, f_high) = inside_y(tiles), edges()
    s_low[0] = jnp.zeros((WY, NZ), F32)
    s_high[SRC] = jnp.zeros((WY, NZ), F32)
    for c, s, x, at in ((c_below, s_low, x_below, 1), (c_above, s_high, x_above, 0)):
        lay_charge(s, at, SRC, x[...], c[:, 0:8], c[:, 19:22], c[:, 8:19])
    s_low[LOW:HIGH] = source[0 : HIGH - LOW] + s_low[LOW:HIGH] * f_low
    s_high[0 : DEPX - BX] += source[BX:DEPX]

    def fill(count, s, s_at, d, d_at, f, at, p_out, rhs_out, inv_out):
        def body(r, c):
            for t in range(tiles):
                den = strided(d, r + d_at, t, tiles)
                scale = jnp.where(inside[t], f / (6.0 + den), 0.0)
                value = strided(s, r + s_at, t, tiles) - den
                rhs_out[r + at, t], inv_out[r + at, t] = value, scale
                p_out[r + at, t] = value * scale
            return c

        lax.fori_loop(0, count, body, 0, unroll=count)

    fill(LOW, s_low, 0, d_below, 0, f_low, 0, l1, l_rhs, l_inv)
    fill(BLX - 1, s_low, LOW, dens, 0, 1.0, LOW, l1, l_rhs, l_inv)
    fill(HIGH, s_high, 0, d_above, 0, f_high, LOW - 1, h1, h_rhs, h_inv)
    lows, highs = (l0, l1, l_rhs, l_inv), (h0, h1, h_rhs, h_inv)
    flanks(b0, b1, lows, highs, rhs, inv, 2, a, h)
    finish(b0, l0, h0, nat, a, h)
    hand_on(nat, *outs)


def next_flanks(refs, nat, spare):
    b0, b1, rhs, inv, ahead, y_below, y_above, x_below, x_above, c_below, c_above = refs[:11]
    s_low, s_high, d_low, d_high = refs[11:]
    l0, l1, l_rhs, l_inv, h0, h1, h_rhs, h_inv = spare
    inside, (f_low, f_high) = inside_y(b0.shape[1]), edges()

    def low_body(r, c):
        start(nat, HIGH, s_low, 0, d_low, inside, f_low, (l0, l_rhs, l_inv), 0, r)
        return c

    more = HIGH - LOW
    lay(nat, 0, more, ahead[...], y_below[BX:DEPX], y_above[BX:DEPX])
    lay(nat, more, LOW, x_above[...], c_above[:, 0:LOW], c_above[:, LOW:])
    lay(nat, HIGH, LOW, x_below[...], c_below[:, 0:LOW], c_below[:, LOW:])

    def high_body(r, c):
        start(nat, 0, s_high, 0, d_high, inside, f_high, (h0, h_rhs, h_inv), LOW, r)
        return c

    lax.fori_loop(0, LOW, low_body, 0, unroll=LOW)
    lax.fori_loop(0, HIGH, high_body, 0, unroll=HIGH)
    lows, highs = (l0, l1, l_rhs, l_inv), (h0, h1, h_rhs, h_inv)
    flanks(b0, b1, lows, highs, rhs, inv, 1, 0, BX)
    finish(b0, l0, h0, nat, 0, BX)


def flank_next(*refs):
    outs, (nat, *spare) = refs[15:21], refs[21:]
    next_flanks(refs[:15], nat, spare)
    hand_on(nat, *outs)


def flank_last(*refs):
    (got, out, sums, nat), spare, (turned, meta, sem, named) = refs[15:19], refs[19:27], refs[27:]
    copy = numbers(got, turned, meta, sem)
    next_flanks(refs[:15], nat, spare)
    out[...] = nat[0:BX, LOW : LOW + BY]
    copy.wait()
    read(got, nat, sums, meta, named)


def slab_kernel(x_low, x_high, below, above, low, high):
    lay(low, 0, HIGH, x_low[...], below[0:HIGH], above[0:HIGH])
    lay(high, 0, LOW, x_high[...], below[BX - LOW :], above[BX - LOW :])


def beside(x_low, x_high, y_low, y_high):
    y_below, y_above = ring(y_high, "gy", 1), ring(y_low, "gy", -1)
    low, high = call(slab_kernel, [(HIGH, WY, NZ), (LOW, WY, NZ)], [VMEM] * 4)(
        x_low, x_high, y_below, y_above
    )
    x_below, x_above = ring(high, "gx", 1), ring(low, "gx", -1)
    return (y_below, y_above), (x_below, x_above), (low, high)


def strip_kernel(below, above, low, high):
    for at, strip in ((HIGH - LOW, low), (BX - LOW, high)):
        strip[:, 0:LOW] = below[at : at + LOW]
        strip[:, LOW:] = above[at : at + LOW]


def corner_kernel(below, above, unused_low, unused_high, low, high):
    for at, strip in ((0, low), (DEPX - SRC, high)):
        strip[:, 0:8] = below[at : at + SRC, 0:8]
        strip[:, 8:16] = above[at : at + SRC, 0:8]
        strip[:, 16:19] = above[at : at + SRC, 8:HIGH]
        strip[:, 19:22] = below[at : at + SRC, 8:HIGH]
        strip[:, 22:24] = jnp.zeros((SRC, 2, NZ), F32)


def around(x_low, x_high, y_low, y_high, body, strip, first=()):
    x_below, x_above = ring(x_high, "gx", 1), ring(x_low, "gx", -1)
    y_below, y_above = ring(y_high, "gy", 1), ring(y_low, "gy", -1)
    low, high = call(body, [strip] * 2, [VMEM] * 2 + [ANY] * len(first))(y_below, y_above, *first)
    c_below, c_above = ring(high, "gx", 1), ring(low, "gx", -1)
    return (y_below, y_above), (x_below, x_above, c_below, c_above)


def read(got, field, out, meta, named):
    lane = iota((BLY, 128), 1)

    def note(p, n):
        named[n] = p
        return n + meta[CAP, p]

    count = lax.fori_loop(0, PAN_DEV, note, 0, unroll=8)
    for u in range(READ):
        named[count + u] = 0

    def body(j, c):
        for u in range(READ):
            p = named[READ * j + u]
            v = got[pl.ds(p * MSG, CAP), :]
            total = jnp.zeros((BLY, 128), F32)
            for k in range(CAP):
                x, y, z = corner(meta, p, k)
                for i in range(BLX):
                    piece = field[x + i, pl.ds(y + LOW, BLY), :]
                    total += block_rows(v, z, k, i, lane) * piece
            out[p] = jnp.sum(total, axis=0, keepdims=True)
        return c

    lax.fori_loop(0, (count + READ - 1) // READ, body, 0)


def pick_kernel(brick, counts, aper, got, out, rows):
    sub = iota((1, APER_DEV), 1)
    live = jnp.ones((1, APER_DEV), F32)
    for a in range(APER_DEV):
        p = aper[a]
        rows[a : a + 1, :] = got[brick[p]]
        live = jnp.where(sub == a, counts[p].astype(F32), live)
    out[...] = jnp.sum(rows[...], axis=1) / live[0]


def ring(array, axis, by):
    size = lax.axis_size(axis)
    return lax.ppermute(array, axis, [(i, (i + by) % size) for i in range(size)])


def on_device(
    ion_charge, density, charge_blocks, panel_brick, row_counts, block_offset, aperture_panel
):
    everyone = ("gx", "gy")
    ints = [pltpu.SMEM((n,), jnp.int32) for n in (PAN_DEV, PAN_DEV, PAN_DEV * CAP, APER_DEV)]
    send, *d_slabs = call(
        pack_kernel,
        [(PAN_DEV * MSG, 128), (BX, 16, NZ), (BX, LOW, NZ)],
        [ANY] * 6,
        ints
        + [
            pltpu.VMEM((PAN_DEV * CAP, 128), F32),
            pltpu.SMEM((PAN_DEV,), jnp.int32),
            pltpu.SemaphoreType.DMA((7,)),
        ],
        60,
    )(panel_brick, row_counts, block_offset, aperture_panel, charge_blocks, density)
    send = send.reshape(PAN_DEV, 1, MSG * 128)
    got = lax.all_to_all(send, everyone, split_axis=0, concat_axis=0, tiled=True)
    got = got.reshape(PAN_DEV * MSG, 128)
    dy, dx, d_slabs = beside(density[:HIGH], density[BX - LOW :], *d_slabs)

    meta = [
        pltpu.VMEM((8, 128), jnp.int32),
        pltpu.SMEM((8, 128), jnp.int32),
        pltpu.SemaphoreType.DMA,
    ]
    charge, *slabs = call(
        deposit_kernel,
        [(DEPX, DEPY, NZ)] + [(SRC, DEPY, NZ)] * 2 + [(DEPX, 16, NZ)] * 2,
        [VMEM] * 2 + [ANY] * 2,
        meta,
    )(got, ion_charge, *d_slabs)

    def tiles(n, width):
        return (n, width, 8, NZ)

    def layers(n):
        return pltpu.VMEM((n, WY, NZ), F32)

    def brick(width):
        slabs = [(HIGH - LOW, BY, NZ), (LOW, BY, NZ), (LOW, BY, NZ), (DEPX, width, NZ), (DEPX, LOW, NZ)]
        return [(BX, BY, NZ)] + slabs

    def spare(width):
        return [pltpu.VMEM(tiles(LOW + LOW + BLX, width), F32)] * 8

    work = 20_000_000_000
    cy, cx = around(*slabs, corner_kernel, (SRC, 24, NZ), dx)
    *state, source, dens = call(
        inner_first,
        [tiles(BX, NEAR)] * 4 + [(DEPX, WY, NZ), (BX, WY, NZ)],
        [VMEM] * 6,
        (),
        32,
        work,
    )(charge, *cy, density, *dy)
    pot, ahead, *slabs, s_low, s_high = call(
        flank_first,
        brick(8) + [(HIGH, WY, NZ)] * 2,
        [VMEM] * 12,
        [layers(DEPX)] + spare(NEAR),
        32,
    )(*state, source, dens, *cx, *dx)
    for step in range(1, NEWTON):
        width = NEAR if step < NEWTON - 1 else TILES
        py, px = around(*slabs, strip_kernel, (LOW, 8 * width - BY, NZ))
        state = call(inner_next, [tiles(BX, width)] * 4, [VMEM] * 6, [layers(BX)], 32, work)(
            pot, *py, source, s_low, dens
        )
        operands = (*state, ahead, *py, *px, s_low, s_high, *dx)
        if step < NEWTON - 1:
            pot, ahead, *slabs = call(
                flank_next, brick(16), [VMEM] * 15, [layers(DEPX)] + spare(width), 32
            )(*operands)
    pot, sums = call(
        flank_last,
        [(BX, BY, NZ), (PAN_DEV, 1, 128)],
        [VMEM] * 16,
        [layers(DEPX)] + spare(TILES) + meta + [pltpu.SMEM((PAN_DEV + 8,), jnp.int32)],
        32,
    )(*operands, got)
    back = lax.all_to_all(sums, everyone, split_axis=0, concat_axis=0, tiled=True)
    (picked,) = call(
        pick_kernel,
        [(APER_DEV,)],
        [SMEM] * 3 + [VMEM],
        [pltpu.VMEM((APER_DEV, 128), F32)],
    )(panel_brick, row_counts, aperture_panel, back)
    return pot, picked


def solution(mesh):
    everyone = P(("gx", "gy"))
    grid = P("gx", "gy", None)
    return jax.shard_map(
        on_device,
        mesh=mesh,
        in_specs=(grid, grid, P(("gx", "gy"), None)) + (everyone,) * 4,
        out_specs=(grid, everyone),
        check_vma=False,
    )
```

```python
import functools

import jax
import jax.numpy as jnp
from jax import lax
from jax.experimental import pallas as pl
from jax.experimental.pallas import tpu as pltpu
from jax.sharding import PartitionSpec as P

BX = 32
BY = 64
NZ = 128
NEWTON = 3
SWEEPS = 8
CAP = 4
BLX = 4
BLY = 4
BLZ = 8
N_GX = 16
N_GY = 8
PAN_DEV = 128
APER_DEV = 16
MSG = CAP + 1
READ = 8
LOW = 8
HIGH = 11
TILES = 11
SRC = HIGH - 1
WY = 8 * TILES
BY_PRODUCT = 4
NEAR = 10
DEPX = BX + BLX - 1
DEPY = 72

VMEM = pl.BlockSpec(memory_space=pltpu.VMEM)
SMEM = pl.BlockSpec(memory_space=pltpu.SMEM)
ANY = pl.BlockSpec(memory_space=pl.ANY)
F32 = jnp.float32


def call(body, outs, ins, scratch=(), mib=24, flops=None, out_specs=None):
    cost = None
    if flops is not None:
        cost = pl.CostEstimate(flops=flops, bytes_accessed=1 << 20, transcendentals=0)
    return pl.pallas_call(
        body,
        out_shape=[jax.ShapeDtypeStruct(s, F32) for s in outs],
        in_specs=list(ins),
        out_specs=out_specs or [VMEM] * len(outs),
        scratch_shapes=list(scratch),
        cost_estimate=cost,
        compiler_params=pltpu.CompilerParams(vmem_limit_bytes=mib << 20),
    )


def iota(shape, dim):
    return lax.broadcasted_iota(jnp.int32, shape, dim)


def pack_kernel(*refs):
    arrays, density, (send, y_low, y_high, table) = refs[:5], refs[5], refs[6:10]
    local, need, sems = refs[10:15], refs[15], refs[16]
    copies = [pltpu.make_async_copy(a, b, sems.at[i]) for i, (a, b) in enumerate(zip(arrays, local))]
    cuts = [
        pltpu.make_async_copy(density.at[:, 0:16, :], y_low, sems.at[5]),
        pltpu.make_async_copy(density.at[:, BY - LOW : BY, :], y_high, sems.at[6]),
    ]
    for copy in copies + cuts:
        copy.start()
    brick, counts, offsets, aper, rows = local

    def clear(p, c):
        need[p] = 0
        return c

    lax.fori_loop(0, PAN_DEV, clear, 0, unroll=8)
    for copy in copies:
        copy.wait()
    lane1 = iota((1, 128), 1)
    picks = jnp.zeros((1, 128), jnp.int32)
    for a in range(APER_DEV):
        p = aper[a]
        need[p] = 1
        picks = jnp.where(lane1 == a, brick[p], picks)
        picks = jnp.where(lane1 == APER_DEV + a, counts[p], picks)
    table[...] = picks.astype(F32)
    sub = iota((8, 128), 0)
    group = (iota((8, 128), 1) >> 3) & 3
    j = sub & 3
    masks = {e: (group == j - e) for e in range(-3, 4)}

    def body(q, c):
        p = q * 2
        live = sub < jnp.where(sub < 4, counts[p], counts[p + 1] + 4)
        v = jnp.where(live, rows[pl.ds(pl.multiple_of(q * 8, 8), 8), :], 0.0)
        out = v
        for e in (-3, -2, -1, 1, 2, 3):
            moved = pltpu.roll(pltpu.roll(v, e % 8, 0), (-8 * e) % 128, 1)
            out = jnp.where(masks[e], moved, out)
        for h in range(2):
            b = brick[p + h]
            send[pl.ds(b * MSG, 4), :] = out[4 * h : 4 * h + 4]
            meta = jnp.zeros((1, 128), jnp.int32)
            for k in range(CAP):
                meta = jnp.where(lane1 == k, offsets[(p + h) * CAP + k], meta)
            meta = jnp.where(lane1 == CAP, need[p + h], meta)
            send[pl.ds(b * MSG + 4, 1), :] = meta.astype(F32)
        return c

    lax.fori_loop(0, PAN_DEV // 2, body, 0, unroll=8)
    for copy in cuts:
        copy.wait()


def numbers(got, turned, meta, sem):
    rows = got[pl.ds(CAP, PAN_DEV, stride=MSG), :]
    turned[...] = jnp.transpose(rows)[0:8].astype(jnp.int32)
    copy = pltpu.make_async_copy(turned, meta, sem)
    copy.start()
    return copy


def corner(meta, p, k):
    offset = meta[k, p]
    return offset >> 13, (offset >> 7) & 63, offset & 127


def block_rows(v, z, k, i, lane):
    moved = pltpu.roll(v, (z - 32 * i - 8 * k + 128) & 127, 1)
    return jnp.where((lane >= z) & (lane < z + BLZ), moved, 0.0)


def deposit_kernel(got, ion, unused_low, unused_high, out, x_low, x_high, y_low, y_high, turned, meta, sem):
    copy = numbers(got, turned, meta, sem)
    out[0:BX, 0:BY, :] = ion[...]
    out[0:BX, BY:DEPY, :] = jnp.zeros((BX, DEPY - BY, NZ), F32)
    out[BX:DEPX] = jnp.zeros((DEPX - BX, DEPY, NZ), F32)
    lane = iota((BLY, 128), 1)
    copy.wait()

    def body(p, c):
        v = got[pl.ds(p * MSG, CAP), :]
        for k in range(CAP):
            x, y, z = corner(meta, p, k)
            add = [block_rows(v, z, k, i, lane) for i in range(BLX)]
            old = [out[x + i, pl.ds(y, BLY), :] for i in range(BLX)]
            for i in range(BLX):
                out[x + i, pl.ds(y, BLY), :] = old[i] + add[i]
        return c

    lax.fori_loop(0, PAN_DEV, body, 0, unroll=16)
    x_low[...] = out[0:SRC]
    x_high[...] = out[DEPX - SRC : DEPX]
    y_low[...] = out[:, 0:16]
    y_high[...] = out[:, BY - LOW : DEPY]


def inside_y(tiles):
    gy = lax.axis_index("gy")
    lo = jnp.where(gy == 0, LOW, 0)
    hi = jnp.where(gy == N_GY - 1, LOW + BY, WY)
    sub = iota((8, 128), 0)
    ys = [sub * tiles + t for t in range(tiles)]
    return [(y >= lo) & (y < hi) for y in ys]


def lay(nat, at, count, own, below, above):
    nat[at : at + count, 0:LOW] = below
    nat[at : at + count, LOW : LOW + BY] = own
    nat[at : at + count, LOW + BY : LOW + BY + above.shape[1]] = above


def lay_charge(nat, at, count, own, below, spilled, above):
    spread = jnp.where(lax.axis_index("gy") > 0, 1.0, 0.0)
    nat[at : at + count, 0:LOW] = below
    nat[at : at + count, LOW : LOW + DEPY] = own
    nat[at : at + count, LOW : LOW + BLY - 1] += spilled * spread
    nat[at : at + count, LOW + BY : LOW + DEPY] += above[:, 0:8]
    nat[at : at + count, LOW + DEPY : LOW + DEPY + 3] = above[:, 8:HIGH]
    nat[at : at + count, LOW + DEPY + 3 : WY] = jnp.zeros((count, WY - LOW - DEPY - 3, NZ), F32)


def strided(nat, x, t, tiles):
    return nat[x, pl.ds(t, 8, stride=tiles), :]


def relax(layers, write):
    tiles = len(layers[0])
    rolled = tiles - BY_PRODUCT
    lane = iota((8, 128), 1)
    first, last = lane == 0, lane == NZ - 1
    inner_layers = layers[1:-1]
    flat = jnp.concatenate(sum([cur[rolled:] for cur in inner_layers], []), axis=0)
    high = flat.astype(jnp.bfloat16)
    low = (flat - high.astype(F32)).astype(jnp.bfloat16)
    from_z, to_z = iota((2 * NZ, NZ), 0) & (NZ - 1), iota((2 * NZ, NZ), 1)
    beside_z = jnp.where((from_z - to_z == 1) | (to_z - from_z == 1), 1.0, 0.0)
    product = jnp.dot(
        jnp.concatenate([high, low], axis=1),
        beside_z.astype(jnp.bfloat16),
        preferred_element_type=F32,
    )
    for u in range(len(inner_layers)):
        prev, cur, nxt = layers[u : u + 3]
        before = [pltpu.roll(cur[-1], 1, 0)] + cur[:-1]
        after = cur[1:] + [pltpu.roll(cur[0], 7, 0)]
        for t in range(tiles):
            if t < rolled:
                left = jnp.where(first, 0.0, pltpu.roll(cur[t], 1, 1))
                along_z = left + jnp.where(last, 0.0, pltpu.roll(cur[t], NZ - 1, 1))
            else:
                at = (u * BY_PRODUCT + t - rolled) * 8
                along_z = product[at : at + 8]
            total = (prev[t] + nxt[t]) + (before[t] + after[t]) + along_z
            write(u, t, total)


def layer(buf, x):
    return [buf[x, t] for t in range(buf.shape[1])]


def sweep(src, dst, rhs, inv, lo, hi):
    def write(u, t, total):
        dst[lo + u, t] = (rhs[lo + u, t] + total) * inv[lo + u, t]

    relax([layer(src, x) for x in range(lo - 1, hi + 1)], write)


def inner(b0, b1, rhs, inv, k0, a, h):
    bufs = (b0, b1)
    for k in range(k0, SWEEPS + 1):
        sweep(bufs[(k - 1) % 2], bufs[k % 2], rhs, inv, a + k, h - k)


def inner_first(charge, y_below, y_above, density, d_below, d_above, *refs):
    b0, b1, rhs, inv, source, dens = refs
    tiles = b0.shape[1]
    inside = inside_y(tiles)
    lay(dens, 0, BX, density[...], d_below[...], d_above[...])
    lay_charge(source, 0, DEPX, charge[...], y_below[:, 0:8], y_below[:, 8:HIGH], y_above)

    def prep(x, c):
        for t in range(tiles):
            s = strided(source, x, t, tiles)
            d = strided(dens, x, t, tiles)
            scale = jnp.where(inside[t], 1.0 / (6.0 + d), 0.0)
            inv[x, t] = scale
            rhs[x, t] = s - d
            b1[x, t] = (s - d) * scale
        return c

    lax.fori_loop(0, BX, prep, 0, unroll=8)
    inner(b0, b1, rhs, inv, 2, BLX - 2, BX + 1)


def start(p_nat, p_at, s, s_at, d, inside, f, outs, to, x):
    p_out, rhs, inv = outs
    tiles = p_out.shape[1]
    for t in range(tiles):
        p = jnp.where(inside[t], strided(p_nat, x + p_at, t, tiles) * f, 0.0)
        coef = strided(d, x, t, tiles) * jnp.exp(p)
        p_out[x + to, t] = p
        rhs[x + to, t] = strided(s, x + s_at, t, tiles) + coef * (p - 1.0)
        inv[x + to, t] = jnp.where(inside[t], f / (6.0 + coef), 0.0)


def inner_next(own, y_below, y_above, source, s_low, dens, b0, b1, rhs, inv, nat):
    inside = inside_y(b0.shape[1])
    lay(nat, 0, BX, own[...], y_below[0:BX], y_above[0:BX])
    outs = (b0, rhs, inv)

    def prep_from(src, at):
        def prep(x, c):
            start(nat, 0, src, at, dens, inside, 1.0, outs, 0, x)
            return c

        return prep

    lax.fori_loop(0, BLX - 1, prep_from(s_low, LOW), 0, unroll=BLX - 1)
    lax.fori_loop(BLX - 1, BX, prep_from(source, 0), 0, unroll=8)
    inner(b0, b1, rhs, inv, 1, 0, BX)


def flanks(b0, b1, lows, highs, rhs, inv, k0, a, h):
    (l0, l1, l_rhs, l_inv), (h0, h1, h_rhs, h_inv) = lows, highs
    n_low, n_high = LOW + a, BX + HIGH - h
    for i in range(LOW + a):
        if i + LOW >= len_low_halo(a):
            l_rhs[i + LOW], l_inv[i + LOW] = rhs[i], inv[i]
    for i in range(h - LOW, BX):
        h_rhs[i - (h - LOW)], h_inv[i - (h - LOW)] = rhs[i], inv[i]

    def one(k, near, l_src, l_dst, h_src, h_dst):
        def low_write(u, t, total):
            l_dst[k + u, t] = (l_rhs[k + u, t] + total) * l_inv[k + u, t]

        def high_write(u, t, total):
            r = LOW - k + u
            h_dst[r, t] = (h_rhs[r, t] + total) * h_inv[r, t]

        low = [layer(l_src, k - 1 + j) for j in range(n_low)]
        relax(low + [layer(near, a + k - 1), layer(near, a + k)], low_write)
        high = [layer(h_src, LOW + 1 - k + j) for j in range(n_high)]
        relax([layer(near, h - k - 1), layer(near, h - k)] + high, high_write)

    if k0 == 2:
        one(2, b1, l1, l0, h1, h0)

    def body(j, c):
        one(2 * j + 1, b0, l0, l1, h0, h1)
        one(2 * j + 2, b1, l1, l0, h1, h0)
        return c

    lax.fori_loop(k0 - 1, SWEEPS // 2, body, 0)


def len_low_halo(a):
    return LOW + (BLX - 1 if a else 0)


def finish(b0, l0, h0, nat, a, h):
    tiles = b0.shape[1]

    def take(src, shift):
        def body(x, c):
            for t in range(tiles):
                nat[x, pl.ds(t, 8, stride=tiles), :] = src[x + shift, t]
            return c

        return body

    lax.fori_loop(0, a + LOW, take(l0, LOW), 0, unroll=8)
    lax.fori_loop(a + LOW, h - LOW, take(b0, 0), 0, unroll=8)
    lax.fori_loop(h - LOW, DEPX, take(h0, LOW - h), 0, unroll=11)


def hand_on(nat, out, ahead, x_low, x_high, y_low, y_high):
    out[...] = nat[0:BX, LOW : LOW + BY]
    x_low[...] = nat[HIGH - LOW : HIGH, LOW : LOW + BY]
    ahead[...] = nat[BX:DEPX, LOW : LOW + BY]
    x_high[...] = nat[BX - LOW : BX, LOW : LOW + BY]
    y_low[...] = nat[0:DEPX, LOW : LOW + y_low.shape[1]]
    y_high[...] = nat[0:DEPX, BY : LOW + BY]


def edges():
    gx = lax.axis_index("gx")
    return jnp.where(gx > 0, 1.0, 0.0), jnp.where(gx < N_GX - 1, 1.0, 0.0)


def flank_first(*refs):
    b0, b1, rhs, inv, source, dens, x_below, x_above, c_below, c_above, d_below, d_above = refs[:12]
    outs, (s_low, s_high), nat, spare = refs[12:18], refs[18:20], refs[20], refs[21:]
    l0, l1, l_rhs, l_inv, h0, h1, h_rhs, h_inv = spare
    a, h = BLX - 2, BX + 1
    tiles = NEAR
    inside, (f_low, f_high) = inside_y(tiles), edges()
    s_low[0] = jnp.zeros((WY, NZ), F32)
    s_high[SRC] = jnp.zeros((WY, NZ), F32)
    for c, s, x, at in ((c_below, s_low, x_below, 1), (c_above, s_high, x_above, 0)):
        lay_charge(s, at, SRC, x[...], c[:, 0:8], c[:, 19:22], c[:, 8:19])
    s_low[LOW:HIGH] = source[0 : HIGH - LOW] + s_low[LOW:HIGH] * f_low
    s_high[0 : DEPX - BX] += source[BX:DEPX]

    def fill(count, s, s_at, d, d_at, f, at, p_out, rhs_out, inv_out):
        def body(r, c):
            for t in range(tiles):
                den = strided(d, r + d_at, t, tiles)
                scale = jnp.where(inside[t], f / (6.0 + den), 0.0)
                value = strided(s, r + s_at, t, tiles) - den
                rhs_out[r + at, t], inv_out[r + at, t] = value, scale
                p_out[r + at, t] = value * scale
            return c

        lax.fori_loop(0, count, body, 0, unroll=count)

    fill(LOW, s_low, 0, d_below, 0, f_low, 0, l1, l_rhs, l_inv)
    fill(BLX - 1, s_low, LOW, dens, 0, 1.0, LOW, l1, l_rhs, l_inv)
    fill(HIGH, s_high, 0, d_above, 0, f_high, LOW - 1, h1, h_rhs, h_inv)
    lows, highs = (l0, l1, l_rhs, l_inv), (h0, h1, h_rhs, h_inv)
    flanks(b0, b1, lows, highs, rhs, inv, 2, a, h)
    finish(b0, l0, h0, nat, a, h)
    hand_on(nat, *outs)


def next_flanks(refs, nat, spare):
    b0, b1, rhs, inv, ahead, y_below, y_above, x_below, x_above, c_below, c_above = refs[:11]
    s_low, s_high, d_low, d_high = refs[11:]
    l0, l1, l_rhs, l_inv, h0, h1, h_rhs, h_inv = spare
    inside, (f_low, f_high) = inside_y(b0.shape[1]), edges()

    def low_body(r, c):
        start(nat, HIGH, s_low, 0, d_low, inside, f_low, (l0, l_rhs, l_inv), 0, r)
        return c

    more = HIGH - LOW
    lay(nat, 0, more, ahead[...], y_below[BX:DEPX], y_above[BX:DEPX])
    lay(nat, more, LOW, x_above[...], c_above[:, 0:LOW], c_above[:, LOW:])
    lay(nat, HIGH, LOW, x_below[...], c_below[:, 0:LOW], c_below[:, LOW:])

    def high_body(r, c):
        start(nat, 0, s_high, 0, d_high, inside, f_high, (h0, h_rhs, h_inv), LOW, r)
        return c

    lax.fori_loop(0, LOW, low_body, 0, unroll=LOW)
    lax.fori_loop(0, HIGH, high_body, 0, unroll=HIGH)
    lows, highs = (l0, l1, l_rhs, l_inv), (h0, h1, h_rhs, h_inv)
    flanks(b0, b1, lows, highs, rhs, inv, 1, 0, BX)
    finish(b0, l0, h0, nat, 0, BX)


def flank_next(*refs):
    outs, (nat, *spare) = refs[15:21], refs[21:]
    next_flanks(refs[:15], nat, spare)
    hand_on(nat, *outs)


def flank_last(*refs):
    (got, out, sums, nat), spare, (turned, meta, sem, named, out_sem) = refs[15:19], refs[19:27], refs[27:]
    copy = numbers(got, turned, meta, sem)
    next_flanks(refs[:15], nat, spare)
    result = pltpu.make_async_copy(nat.at[0:BX, LOW : LOW + BY, :], out, out_sem)
    result.start()
    copy.wait()
    read(got, nat, sums, meta, named)
    result.wait()


def slab_kernel(x_low, x_high, below, above, low, high):
    lay(low, 0, HIGH, x_low[...], below[0:HIGH], above[0:HIGH])
    lay(high, 0, LOW, x_high[...], below[BX - LOW :], above[BX - LOW :])


def beside(x_low, x_high, y_low, y_high):
    y_below, y_above = ring(y_high, "gy", 1), ring(y_low, "gy", -1)
    low, high = call(slab_kernel, [(HIGH, WY, NZ), (LOW, WY, NZ)], [VMEM] * 4)(
        x_low, x_high, y_below, y_above
    )
    x_below, x_above = ring(high, "gx", 1), ring(low, "gx", -1)
    return (y_below, y_above), (x_below, x_above), (low, high)


def strip_kernel(below, above, low, high):
    for at, strip in ((HIGH - LOW, low), (BX - LOW, high)):
        strip[:, 0:LOW] = below[at : at + LOW]
        strip[:, LOW:] = above[at : at + LOW]


def corner_kernel(below, above, unused_low, unused_high, low, high):
    for at, strip in ((0, low), (DEPX - SRC, high)):
        strip[:, 0:8] = below[at : at + SRC, 0:8]
        strip[:, 8:16] = above[at : at + SRC, 0:8]
        strip[:, 16:19] = above[at : at + SRC, 8:HIGH]
        strip[:, 19:22] = below[at : at + SRC, 8:HIGH]
        strip[:, 22:24] = jnp.zeros((SRC, 2, NZ), F32)


def around(x_low, x_high, y_low, y_high, body, strip, first=()):
    x_below, x_above = ring(x_high, "gx", 1), ring(x_low, "gx", -1)
    y_below, y_above = ring(y_high, "gy", 1), ring(y_low, "gy", -1)
    low, high = call(body, [strip] * 2, [VMEM] * 2 + [ANY] * len(first))(y_below, y_above, *first)
    c_below, c_above = ring(high, "gx", 1), ring(low, "gx", -1)
    return (y_below, y_above), (x_below, x_above, c_below, c_above)


def read(got, field, out, meta, named):
    lane = iota((BLY, 128), 1)

    def note(p, n):
        named[n] = p
        return n + meta[CAP, p]

    count = lax.fori_loop(0, PAN_DEV, note, 0, unroll=8)
    for u in range(READ):
        named[count + u] = 0

    def body(j, c):
        for u in range(READ):
            p = named[READ * j + u]
            v = got[pl.ds(p * MSG, CAP), :]
            total = jnp.zeros((BLY, 128), F32)
            for k in range(CAP):
                x, y, z = corner(meta, p, k)
                for i in range(BLX):
                    piece = field[x + i, pl.ds(y + LOW, BLY), :]
                    total += block_rows(v, z, k, i, lane) * piece
            out[p] = jnp.sum(total, axis=0, keepdims=True)
        return c

    lax.fori_loop(0, (count + READ - 1) // READ, body, 0)


def pick_kernel(table, got, out, rows):
    lane = iota((1, APER_DEV), 1)
    live = jnp.ones((1, APER_DEV), F32)
    for a in range(APER_DEV):
        rows[a : a + 1, :] = got[table[0, a].astype(jnp.int32)]
        live = jnp.where(lane == a, table[0, APER_DEV + a], live)
    out[...] = jnp.sum(rows[...], axis=1) / live[0]


def ring(array, axis, by):
    size = lax.axis_size(axis)
    return lax.ppermute(array, axis, [(i, (i + by) % size) for i in range(size)])


def on_device(
    ion_charge, density, charge_blocks, panel_brick, row_counts, block_offset, aperture_panel
):
    everyone = ("gx", "gy")
    ints = [pltpu.SMEM((n,), jnp.int32) for n in (PAN_DEV, PAN_DEV, PAN_DEV * CAP, APER_DEV)]
    send, d_low, d_high, table = call(
        pack_kernel,
        [(PAN_DEV * MSG, 128), (BX, 16, NZ), (BX, LOW, NZ), (1, 128)],
        [ANY] * 6,
        ints
        + [
            pltpu.VMEM((PAN_DEV * CAP, 128), F32),
            pltpu.SMEM((PAN_DEV,), jnp.int32),
            pltpu.SemaphoreType.DMA((7,)),
        ],
        60,
    )(panel_brick, row_counts, block_offset, aperture_panel, charge_blocks, density)
    send = send.reshape(PAN_DEV, 1, MSG * 128)
    got = lax.all_to_all(send, everyone, split_axis=0, concat_axis=0, tiled=True)
    got = got.reshape(PAN_DEV * MSG, 128)
    dy, dx, d_slabs = beside(density[:HIGH], density[BX - LOW :], d_low, d_high)

    meta = [
        pltpu.VMEM((8, 128), jnp.int32),
        pltpu.SMEM((8, 128), jnp.int32),
        pltpu.SemaphoreType.DMA,
    ]
    charge, *slabs = call(
        deposit_kernel,
        [(DEPX, DEPY, NZ)] + [(SRC, DEPY, NZ)] * 2 + [(DEPX, 16, NZ)] * 2,
        [VMEM] * 2 + [ANY] * 2,
        meta,
    )(got, ion_charge, *d_slabs)

    def tiles(n, width):
        return (n, width, 8, NZ)

    def layers(n):
        return pltpu.VMEM((n, WY, NZ), F32)

    def brick(width):
        slabs = [(HIGH - LOW, BY, NZ), (LOW, BY, NZ), (LOW, BY, NZ), (DEPX, width, NZ), (DEPX, LOW, NZ)]
        return [(BX, BY, NZ)] + slabs

    def spare(width):
        return [pltpu.VMEM(tiles(LOW + LOW + BLX, width), F32)] * 8

    work = 20_000_000_000
    cy, cx = around(*slabs, corner_kernel, (SRC, 24, NZ), dx)
    *state, source, dens = call(
        inner_first,
        [tiles(BX, NEAR)] * 4 + [(DEPX, WY, NZ), (BX, WY, NZ)],
        [VMEM] * 6,
        (),
        32,
        work,
    )(charge, *cy, density, *dy)
    pot, ahead, *slabs, s_low, s_high = call(
        flank_first,
        brick(8) + [(HIGH, WY, NZ)] * 2,
        [VMEM] * 12,
        [layers(DEPX)] + spare(NEAR),
        32,
    )(*state, source, dens, *cx, *dx)
    for step in range(1, NEWTON):
        width = NEAR if step < NEWTON - 1 else TILES
        py, px = around(*slabs, strip_kernel, (LOW, 8 * width - BY, NZ))
        state = call(inner_next, [tiles(BX, width)] * 4, [VMEM] * 6, [layers(BX)], 32, work)(
            pot, *py, source, s_low, dens
        )
        operands = (*state, ahead, *py, *px, s_low, s_high, *dx)
        if step < NEWTON - 1:
            pot, ahead, *slabs = call(
                flank_next, brick(16), [VMEM] * 15, [layers(DEPX)] + spare(width), 32
            )(*operands)
    pot, sums = call(
        flank_last,
        [(BX, BY, NZ), (PAN_DEV, 1, 128)],
        [VMEM] * 16,
        [layers(DEPX)] + spare(TILES) + meta + [pltpu.SMEM((PAN_DEV + READ,), jnp.int32), pltpu.SemaphoreType.DMA],
        32,
        out_specs=[ANY, VMEM],
    )(*operands, got)
    back = lax.all_to_all(sums, everyone, split_axis=0, concat_axis=0, tiled=True)
    (picked,) = call(
        pick_kernel,
        [(APER_DEV,)],
        [SMEM, VMEM],
        [pltpu.VMEM((APER_DEV, 128), F32)],
    )(table, back)
    return pot, picked


def solution(mesh):
    everyone = P(("gx", "gy"))
    grid = P("gx", "gy", None)
    return jax.shard_map(
        on_device,
        mesh=mesh,
        in_specs=(grid, grid, P(("gx", "gy"), None)) + (everyone,) * 4,
        out_specs=(grid, everyone),
        check_vma=False,
    )
```

```python
import functools

import jax
import jax.numpy as jnp
from jax import lax
from jax.experimental import pallas as pl
from jax.experimental.pallas import tpu as pltpu
from jax.sharding import PartitionSpec as P

BX = 32
BY = 64
NZ = 128
NEWTON = 3
SWEEPS = 8
CAP = 4
BLX = 4
BLY = 4
BLZ = 8
N_GX = 16
N_GY = 8
PAN_DEV = 128
APER_DEV = 16
MSG = CAP + 1
READ = 8
LOW = 8
HIGH = 11
TILES = 11
SRC = HIGH - 1
WY = 8 * TILES
BY_PRODUCT = 4
NEAR = 10
DEPX = BX + BLX - 1
DEPY = 72

VMEM = pl.BlockSpec(memory_space=pltpu.VMEM)
SMEM = pl.BlockSpec(memory_space=pltpu.SMEM)
ANY = pl.BlockSpec(memory_space=pl.ANY)
F32 = jnp.float32


def call(body, outs, ins, scratch=(), mib=24, flops=None, out_specs=None):
    cost = None
    if flops is not None:
        cost = pl.CostEstimate(flops=flops, bytes_accessed=1 << 20, transcendentals=0)
    return pl.pallas_call(
        body,
        out_shape=[jax.ShapeDtypeStruct(s, F32) for s in outs],
        in_specs=list(ins),
        out_specs=out_specs or [VMEM] * len(outs),
        scratch_shapes=list(scratch),
        cost_estimate=cost,
        compiler_params=pltpu.CompilerParams(vmem_limit_bytes=mib << 20),
    )


def iota(shape, dim):
    return lax.broadcasted_iota(jnp.int32, shape, dim)


def pack_kernel(*refs):
    arrays, density, (send, y_low, y_high, table) = refs[:5], refs[5], refs[6:10]
    local, need, sems = refs[10:15], refs[15], refs[16]
    copies = [pltpu.make_async_copy(a, b, sems.at[i]) for i, (a, b) in enumerate(zip(arrays, local))]
    cuts = [
        pltpu.make_async_copy(density.at[:, 0:16, :], y_low, sems.at[5]),
        pltpu.make_async_copy(density.at[:, BY - LOW : BY, :], y_high, sems.at[6]),
    ]
    for copy in copies + cuts:
        copy.start()
    brick, counts, offsets, aper, rows = local

    def clear(p, c):
        need[p] = 0
        return c

    lax.fori_loop(0, PAN_DEV, clear, 0, unroll=8)
    for copy in copies:
        copy.wait()
    lane1 = iota((1, 128), 1)
    picks = jnp.zeros((1, 128), jnp.int32)
    for a in range(APER_DEV):
        p = aper[a]
        need[p] = 1
        picks = jnp.where(lane1 == a, brick[p], picks)
        picks = jnp.where(lane1 == APER_DEV + a, counts[p], picks)
    table[...] = picks.astype(F32)
    sub = iota((8, 128), 0)
    group = (iota((8, 128), 1) >> 3) & 3
    j = sub & 3
    masks = {e: (group == j - e) for e in range(-3, 4)}

    def body(q, c):
        p = q * 2
        live = sub < jnp.where(sub < 4, counts[p], counts[p + 1] + 4)
        v = jnp.where(live, rows[pl.ds(pl.multiple_of(q * 8, 8), 8), :], 0.0)
        out = v
        for e in (-3, -2, -1, 1, 2, 3):
            moved = pltpu.roll(pltpu.roll(v, e % 8, 0), (-8 * e) % 128, 1)
            out = jnp.where(masks[e], moved, out)
        for h in range(2):
            b = brick[p + h]
            send[pl.ds(b * MSG, 4), :] = out[4 * h : 4 * h + 4]
            meta = jnp.zeros((1, 128), jnp.int32)
            for k in range(CAP):
                meta = jnp.where(lane1 == k, offsets[(p + h) * CAP + k], meta)
            meta = jnp.where(lane1 == CAP, need[p + h], meta)
            send[pl.ds(b * MSG + 4, 1), :] = meta.astype(F32)
        return c

    lax.fori_loop(0, PAN_DEV // 2, body, 0, unroll=8)
    for copy in cuts:
        copy.wait()


def numbers(got, turned, meta, sem):
    rows = got[pl.ds(CAP, PAN_DEV, stride=MSG), :]
    turned[...] = jnp.transpose(rows)[0:8].astype(jnp.int32)
    copy = pltpu.make_async_copy(turned, meta, sem)
    copy.start()
    return copy


def corner(meta, p, k):
    offset = meta[k, p]
    return offset >> 13, (offset >> 7) & 63, offset & 127


def block_rows(v, z, k, i, lane):
    moved = pltpu.roll(v, (z - 32 * i - 8 * k + 128) & 127, 1)
    return jnp.where((lane >= z) & (lane < z + BLZ), moved, 0.0)


def deposit_kernel(got, ion, unused_low, unused_high, out, x_low, x_high, y_low, y_high, turned, meta, sem):
    copy = numbers(got, turned, meta, sem)
    out[0:BX, 0:BY, :] = ion[...]
    out[0:BX, BY:DEPY, :] = jnp.zeros((BX, DEPY - BY, NZ), F32)
    out[BX:DEPX] = jnp.zeros((DEPX - BX, DEPY, NZ), F32)
    lane = iota((BLY, 128), 1)
    copy.wait()

    def body(p, c):
        v = got[pl.ds(p * MSG, CAP), :]
        for k in range(CAP):
            x, y, z = corner(meta, p, k)
            add = [block_rows(v, z, k, i, lane) for i in range(BLX)]
            old = [out[x + i, pl.ds(y, BLY), :] for i in range(BLX)]
            for i in range(BLX):
                out[x + i, pl.ds(y, BLY), :] = old[i] + add[i]
        return c

    lax.fori_loop(0, PAN_DEV, body, 0, unroll=16)
    x_low[...] = out[0:SRC]
    x_high[...] = out[DEPX - SRC : DEPX]
    y_low[...] = out[:, 0:16]
    y_high[...] = out[:, BY - LOW : DEPY]


def inside_y(tiles):
    gy = lax.axis_index("gy")
    lo = jnp.where(gy == 0, LOW, 0)
    hi = jnp.where(gy == N_GY - 1, LOW + BY, WY)
    sub = iota((8, 128), 0)
    ys = [sub * tiles + t for t in range(tiles)]
    return [(y >= lo) & (y < hi) for y in ys]


def lay(nat, at, count, own, below, above):
    nat[at : at + count, 0:LOW] = below
    nat[at : at + count, LOW : LOW + BY] = own
    nat[at : at + count, LOW + BY : LOW + BY + above.shape[1]] = above


def lay_charge(nat, at, count, own, below, spilled, above):
    spread = jnp.where(lax.axis_index("gy") > 0, 1.0, 0.0)
    nat[at : at + count, 0:LOW] = below
    nat[at : at + count, LOW : LOW + DEPY] = own
    nat[at : at + count, LOW : LOW + BLY - 1] += spilled * spread
    nat[at : at + count, LOW + BY : LOW + DEPY] += above[:, 0:8]
    nat[at : at + count, LOW + DEPY : LOW + DEPY + 3] = above[:, 8:HIGH]
    nat[at : at + count, LOW + DEPY + 3 : WY] = jnp.zeros((count, WY - LOW - DEPY - 3, NZ), F32)


def strided(nat, x, t, tiles):
    return nat[x, pl.ds(t, 8, stride=tiles), :]


def relax(layers, write):
    tiles = len(layers[0])
    rolled = tiles - BY_PRODUCT
    lane = iota((8, 128), 1)
    first, last = lane == 0, lane == NZ - 1
    inner_layers = layers[1:-1]
    flat = jnp.concatenate(sum([cur[rolled:] for cur in inner_layers], []), axis=0)
    high = flat.astype(jnp.bfloat16)
    low = (flat - high.astype(F32)).astype(jnp.bfloat16)
    from_z, to_z = iota((2 * NZ, NZ), 0) & (NZ - 1), iota((2 * NZ, NZ), 1)
    beside_z = jnp.where((from_z - to_z == 1) | (to_z - from_z == 1), 1.0, 0.0)
    product = jnp.dot(
        jnp.concatenate([high, low], axis=1),
        beside_z.astype(jnp.bfloat16),
        preferred_element_type=F32,
    )
    for u in range(len(inner_layers)):
        prev, cur, nxt = layers[u : u + 3]
        before = [pltpu.roll(cur[-1], 1, 0)] + cur[:-1]
        after = cur[1:] + [pltpu.roll(cur[0], 7, 0)]
        for t in range(tiles):
            if t < rolled:
                left = jnp.where(first, 0.0, pltpu.roll(cur[t], 1, 1))
                along_z = left + jnp.where(last, 0.0, pltpu.roll(cur[t], NZ - 1, 1))
            else:
                at = (u * BY_PRODUCT + t - rolled) * 8
                along_z = product[at : at + 8]
            total = (prev[t] + nxt[t]) + (before[t] + after[t]) + along_z
            write(u, t, total)


def layer(buf, x):
    return [buf[x, t] for t in range(buf.shape[1])]


def sweep(src, dst, rhs, inv, lo, hi):
    def write(u, t, total):
        dst[lo + u, t] = (rhs[lo + u, t] + total) * inv[lo + u, t]

    relax([layer(src, x) for x in range(lo - 1, hi + 1)], write)


def inner(b0, b1, rhs, inv, k0, a, h):
    bufs = (b0, b1)
    for k in range(k0, SWEEPS + 1):
        sweep(bufs[(k - 1) % 2], bufs[k % 2], rhs, inv, a + k, h - k)


def inner_first(charge, y_below, y_above, density, d_below, d_above, *refs):
    b0, b1, rhs, inv, source, dens = refs
    tiles = b0.shape[1]
    inside = inside_y(tiles)
    lay(dens, 0, BX, density[...], d_below[...], d_above[...])
    lay_charge(source, 0, DEPX, charge[...], y_below[:, 0:8], y_below[:, 8:HIGH], y_above)

    def prep(x, c):
        for t in range(tiles):
            s = strided(source, x, t, tiles)
            d = strided(dens, x, t, tiles)
            scale = jnp.where(inside[t], 1.0 / (6.0 + d), 0.0)
            inv[x, t] = scale
            rhs[x, t] = s - d
            b1[x, t] = (s - d) * scale
        return c

    lax.fori_loop(0, BX, prep, 0, unroll=8)
    inner(b0, b1, rhs, inv, 2, BLX - 2, BX + 1)


def start(p_nat, p_at, s, s_at, d, inside, f, outs, to, x):
    p_out, rhs, inv = outs
    tiles = p_out.shape[1]
    for t in range(tiles):
        p = jnp.where(inside[t], strided(p_nat, x + p_at, t, tiles) * f, 0.0)
        coef = strided(d, x, t, tiles) * jnp.exp(p)
        p_out[x + to, t] = p
        rhs[x + to, t] = strided(s, x + s_at, t, tiles) + coef * (p - 1.0)
        inv[x + to, t] = jnp.where(inside[t], f / (6.0 + coef), 0.0)


def inner_next(own, y_below, y_above, source, s_low, dens, b0, b1, rhs, inv, nat):
    inside = inside_y(b0.shape[1])
    lay(nat, 0, BX, own[...], y_below[0:BX], y_above[0:BX])
    outs = (b0, rhs, inv)

    def prep_from(src, at):
        def prep(x, c):
            start(nat, 0, src, at, dens, inside, 1.0, outs, 0, x)
            return c

        return prep

    lax.fori_loop(0, BLX - 1, prep_from(s_low, LOW), 0, unroll=BLX - 1)
    lax.fori_loop(BLX - 1, BX, prep_from(source, 0), 0, unroll=8)
    inner(b0, b1, rhs, inv, 1, 0, BX)


def flanks(b0, b1, lows, highs, rhs, inv, k0, a, h):
    (l0, l1, l_rhs, l_inv), (h0, h1, h_rhs, h_inv) = lows, highs
    n_low, n_high = LOW + a, BX + HIGH - h
    for i in range(LOW + a):
        if i + LOW >= len_low_halo(a):
            l_rhs[i + LOW], l_inv[i + LOW] = rhs[i], inv[i]
    for i in range(h - LOW, BX):
        h_rhs[i - (h - LOW)], h_inv[i - (h - LOW)] = rhs[i], inv[i]

    def one(k, near, l_src, l_dst, h_src, h_dst):
        def low_write(u, t, total):
            l_dst[k + u, t] = (l_rhs[k + u, t] + total) * l_inv[k + u, t]

        def high_write(u, t, total):
            r = LOW - k + u
            h_dst[r, t] = (h_rhs[r, t] + total) * h_inv[r, t]

        low = [layer(l_src, k - 1 + j) for j in range(n_low)]
        relax(low + [layer(near, a + k - 1), layer(near, a + k)], low_write)
        high = [layer(h_src, LOW + 1 - k + j) for j in range(n_high)]
        relax([layer(near, h - k - 1), layer(near, h - k)] + high, high_write)

    if k0 == 2:
        one(2, b1, l1, l0, h1, h0)

    def body(j, c):
        one(2 * j + 1, b0, l0, l1, h0, h1)
        one(2 * j + 2, b1, l1, l0, h1, h0)
        return c

    for j in range(k0 - 1, SWEEPS // 2):
        body(j, 0)


def len_low_halo(a):
    return LOW + (BLX - 1 if a else 0)


def finish(b0, l0, h0, nat, a, h):
    tiles = b0.shape[1]

    def take(src, shift):
        def body(x, c):
            for t in range(tiles):
                nat[x, pl.ds(t, 8, stride=tiles), :] = src[x + shift, t]
            return c

        return body

    lax.fori_loop(0, a + LOW, take(l0, LOW), 0, unroll=8)
    lax.fori_loop(a + LOW, h - LOW, take(b0, 0), 0, unroll=8)
    lax.fori_loop(h - LOW, DEPX, take(h0, LOW - h), 0, unroll=11)


def hand_on(nat, out, ahead, x_low, x_high, y_low, y_high):
    out[...] = nat[0:BX, LOW : LOW + BY]
    x_low[...] = nat[HIGH - LOW : HIGH, LOW : LOW + BY]
    ahead[...] = nat[BX:DEPX, LOW : LOW + BY]
    x_high[...] = nat[BX - LOW : BX, LOW : LOW + BY]
    y_low[...] = nat[0:DEPX, LOW : LOW + y_low.shape[1]]
    y_high[...] = nat[0:DEPX, BY : LOW + BY]


def edges():
    gx = lax.axis_index("gx")
    return jnp.where(gx > 0, 1.0, 0.0), jnp.where(gx < N_GX - 1, 1.0, 0.0)


def flank_first(*refs):
    b0, b1, rhs, inv, source, dens, x_below, x_above, c_below, c_above, d_below, d_above = refs[:12]
    outs, (s_low, s_high), nat, spare = refs[12:18], refs[18:20], refs[20], refs[21:]
    l0, l1, l_rhs, l_inv, h0, h1, h_rhs, h_inv = spare
    a, h = BLX - 2, BX + 1
    tiles = NEAR
    inside, (f_low, f_high) = inside_y(tiles), edges()
    s_low[0] = jnp.zeros((WY, NZ), F32)
    s_high[SRC] = jnp.zeros((WY, NZ), F32)
    for c, s, x, at in ((c_below, s_low, x_below, 1), (c_above, s_high, x_above, 0)):
        lay_charge(s, at, SRC, x[...], c[:, 0:8], c[:, 19:22], c[:, 8:19])
    s_low[LOW:HIGH] = source[0 : HIGH - LOW] + s_low[LOW:HIGH] * f_low
    s_high[0 : DEPX - BX] += source[BX:DEPX]

    def fill(count, s, s_at, d, d_at, f, at, p_out, rhs_out, inv_out):
        def body(r, c):
            for t in range(tiles):
                den = strided(d, r + d_at, t, tiles)
                scale = jnp.where(inside[t], f / (6.0 + den), 0.0)
                value = strided(s, r + s_at, t, tiles) - den
                rhs_out[r + at, t], inv_out[r + at, t] = value, scale
                p_out[r + at, t] = value * scale
            return c

        lax.fori_loop(0, count, body, 0, unroll=count)

    fill(LOW, s_low, 0, d_below, 0, f_low, 0, l1, l_rhs, l_inv)
    fill(BLX - 1, s_low, LOW, dens, 0, 1.0, LOW, l1, l_rhs, l_inv)
    fill(HIGH, s_high, 0, d_above, 0, f_high, LOW - 1, h1, h_rhs, h_inv)
    lows, highs = (l0, l1, l_rhs, l_inv), (h0, h1, h_rhs, h_inv)
    flanks(b0, b1, lows, highs, rhs, inv, 2, a, h)
    finish(b0, l0, h0, nat, a, h)
    hand_on(nat, *outs)


def next_flanks(refs, nat, spare):
    b0, b1, rhs, inv, ahead, y_below, y_above, x_below, x_above, c_below, c_above = refs[:11]
    s_low, s_high, d_low, d_high = refs[11:]
    l0, l1, l_rhs, l_inv, h0, h1, h_rhs, h_inv = spare
    inside, (f_low, f_high) = inside_y(b0.shape[1]), edges()

    def low_body(r, c):
        start(nat, HIGH, s_low, 0, d_low, inside, f_low, (l0, l_rhs, l_inv), 0, r)
        return c

    more = HIGH - LOW
    lay(nat, 0, more, ahead[...], y_below[BX:DEPX], y_above[BX:DEPX])
    lay(nat, more, LOW, x_above[...], c_above[:, 0:LOW], c_above[:, LOW:])
    lay(nat, HIGH, LOW, x_below[...], c_below[:, 0:LOW], c_below[:, LOW:])

    def high_body(r, c):
        start(nat, 0, s_high, 0, d_high, inside, f_high, (h0, h_rhs, h_inv), LOW, r)
        return c

    lax.fori_loop(0, LOW, low_body, 0, unroll=LOW)
    lax.fori_loop(0, HIGH, high_body, 0, unroll=HIGH)
    lows, highs = (l0, l1, l_rhs, l_inv), (h0, h1, h_rhs, h_inv)
    flanks(b0, b1, lows, highs, rhs, inv, 1, 0, BX)
    finish(b0, l0, h0, nat, 0, BX)


def flank_next(*refs):
    outs, (nat, *spare) = refs[15:21], refs[21:]
    next_flanks(refs[:15], nat, spare)
    hand_on(nat, *outs)


def flank_last(*refs):
    (got, out, sums, nat), spare, (turned, meta, sem, named, out_sem) = refs[15:19], refs[19:27], refs[27:]
    copy = numbers(got, turned, meta, sem)
    next_flanks(refs[:15], nat, spare)
    result = pltpu.make_async_copy(nat.at[0:BX, LOW : LOW + BY, :], out, out_sem)
    result.start()
    copy.wait()
    read(got, nat, sums, meta, named)
    result.wait()


def slab_kernel(x_low, x_high, below, above, low, high):
    lay(low, 0, HIGH, x_low[...], below[0:HIGH], above[0:HIGH])
    lay(high, 0, LOW, x_high[...], below[BX - LOW :], above[BX - LOW :])


def beside(x_low, x_high, y_low, y_high):
    y_below, y_above = ring(y_high, "gy", 1), ring(y_low, "gy", -1)
    low, high = call(slab_kernel, [(HIGH, WY, NZ), (LOW, WY, NZ)], [VMEM] * 4)(
        x_low, x_high, y_below, y_above
    )
    x_below, x_above = ring(high, "gx", 1), ring(low, "gx", -1)
    return (y_below, y_above), (x_below, x_above), (low, high)


def strip_kernel(below, above, low, high):
    for at, strip in ((HIGH - LOW, low), (BX - LOW, high)):
        strip[:, 0:LOW] = below[at : at + LOW]
        strip[:, LOW:] = above[at : at + LOW]


def corner_kernel(below, above, unused_low, unused_high, low, high):
    for at, strip in ((0, low), (DEPX - SRC, high)):
        strip[:, 0:8] = below[at : at + SRC, 0:8]
        strip[:, 8:16] = above[at : at + SRC, 0:8]
        strip[:, 16:19] = above[at : at + SRC, 8:HIGH]
        strip[:, 19:22] = below[at : at + SRC, 8:HIGH]
        strip[:, 22:24] = jnp.zeros((SRC, 2, NZ), F32)


def around(x_low, x_high, y_low, y_high, body, strip, first=()):
    x_below, x_above = ring(x_high, "gx", 1), ring(x_low, "gx", -1)
    y_below, y_above = ring(y_high, "gy", 1), ring(y_low, "gy", -1)
    low, high = call(body, [strip] * 2, [VMEM] * 2 + [ANY] * len(first))(y_below, y_above, *first)
    c_below, c_above = ring(high, "gx", 1), ring(low, "gx", -1)
    return (y_below, y_above), (x_below, x_above, c_below, c_above)


def read(got, field, out, meta, named):
    lane = iota((BLY, 128), 1)

    def note(p, n):
        named[n] = p
        return n + meta[CAP, p]

    count = lax.fori_loop(0, PAN_DEV, note, 0, unroll=8)
    for u in range(READ):
        named[count + u] = 0

    def body(j, c):
        for u in range(READ):
            p = named[READ * j + u]
            v = got[pl.ds(p * MSG, CAP), :]
            total = jnp.zeros((BLY, 128), F32)
            for k in range(CAP):
                x, y, z = corner(meta, p, k)
                for i in range(BLX):
                    piece = field[x + i, pl.ds(y + LOW, BLY), :]
                    total += block_rows(v, z, k, i, lane) * piece
            out[p] = jnp.sum(total, axis=0, keepdims=True)
        return c

    lax.fori_loop(0, (count + READ - 1) // READ, body, 0)


def pick_kernel(table, got, out, rows):
    lane = iota((1, APER_DEV), 1)
    live = jnp.ones((1, APER_DEV), F32)
    for a in range(APER_DEV):
        rows[a : a + 1, :] = got[table[0, a].astype(jnp.int32)]
        live = jnp.where(lane == a, table[0, APER_DEV + a], live)
    out[...] = jnp.sum(rows[...], axis=1) / live[0]


def ring(array, axis, by):
    size = lax.axis_size(axis)
    return lax.ppermute(array, axis, [(i, (i + by) % size) for i in range(size)])


def on_device(
    ion_charge, density, charge_blocks, panel_brick, row_counts, block_offset, aperture_panel
):
    everyone = ("gx", "gy")
    ints = [pltpu.SMEM((n,), jnp.int32) for n in (PAN_DEV, PAN_DEV, PAN_DEV * CAP, APER_DEV)]
    send, d_low, d_high, table = call(
        pack_kernel,
        [(PAN_DEV * MSG, 128), (BX, 16, NZ), (BX, LOW, NZ), (1, 128)],
        [ANY] * 6,
        ints
        + [
            pltpu.VMEM((PAN_DEV * CAP, 128), F32),
            pltpu.SMEM((PAN_DEV,), jnp.int32),
            pltpu.SemaphoreType.DMA((7,)),
        ],
        60,
    )(panel_brick, row_counts, block_offset, aperture_panel, charge_blocks, density)
    send = send.reshape(PAN_DEV, 1, MSG * 128)
    got = lax.all_to_all(send, everyone, split_axis=0, concat_axis=0, tiled=True)
    got = got.reshape(PAN_DEV * MSG, 128)
    dy, dx, d_slabs = beside(density[:HIGH], density[BX - LOW :], d_low, d_high)

    meta = [
        pltpu.VMEM((8, 128), jnp.int32),
        pltpu.SMEM((8, 128), jnp.int32),
        pltpu.SemaphoreType.DMA,
    ]
    charge, *slabs = call(
        deposit_kernel,
        [(DEPX, DEPY, NZ)] + [(SRC, DEPY, NZ)] * 2 + [(DEPX, 16, NZ)] * 2,
        [VMEM] * 2 + [ANY] * 2,
        meta,
    )(got, ion_charge, *d_slabs)

    def tiles(n, width):
        return (n, width, 8, NZ)

    def layers(n):
        return pltpu.VMEM((n, WY, NZ), F32)

    def brick(width):
        slabs = [(HIGH - LOW, BY, NZ), (LOW, BY, NZ), (LOW, BY, NZ), (DEPX, width, NZ), (DEPX, LOW, NZ)]
        return [(BX, BY, NZ)] + slabs

    def spare(width):
        return [pltpu.VMEM(tiles(LOW + LOW + BLX, width), F32)] * 8

    work = 20_000_000_000
    cy, cx = around(*slabs, corner_kernel, (SRC, 24, NZ), dx)
    *state, source, dens = call(
        inner_first,
        [tiles(BX, NEAR)] * 4 + [(DEPX, WY, NZ), (BX, WY, NZ)],
        [VMEM] * 6,
        (),
        32,
        work,
    )(charge, *cy, density, *dy)
    pot, ahead, *slabs, s_low, s_high = call(
        flank_first,
        brick(8) + [(HIGH, WY, NZ)] * 2,
        [VMEM] * 12,
        [layers(DEPX)] + spare(NEAR),
        32,
    )(*state, source, dens, *cx, *dx)
    for step in range(1, NEWTON):
        width = NEAR if step < NEWTON - 1 else TILES
        py, px = around(*slabs, strip_kernel, (LOW, 8 * width - BY, NZ))
        state = call(inner_next, [tiles(BX, width)] * 4, [VMEM] * 6, [layers(BX)], 32, work)(
            pot, *py, source, s_low, dens
        )
        operands = (*state, ahead, *py, *px, s_low, s_high, *dx)
        if step < NEWTON - 1:
            pot, ahead, *slabs = call(
                flank_next, brick(16), [VMEM] * 15, [layers(DEPX)] + spare(width), 32
            )(*operands)
    pot, sums = call(
        flank_last,
        [(BX, BY, NZ), (PAN_DEV, 1, 128)],
        [VMEM] * 16,
        [layers(DEPX)] + spare(TILES) + meta + [pltpu.SMEM((PAN_DEV + READ,), jnp.int32), pltpu.SemaphoreType.DMA],
        32,
        out_specs=[ANY, VMEM],
    )(*operands, got)
    back = lax.all_to_all(sums, everyone, split_axis=0, concat_axis=0, tiled=True)
    (picked,) = call(
        pick_kernel,
        [(APER_DEV,)],
        [SMEM, VMEM],
        [pltpu.VMEM((APER_DEV, 128), F32)],
    )(table, back)
    return pot, picked


def solution(mesh):
    everyone = P(("gx", "gy"))
    grid = P("gx", "gy", None)
    return jax.shard_map(
        on_device,
        mesh=mesh,
        in_specs=(grid, grid, P(("gx", "gy"), None)) + (everyone,) * 4,
        out_specs=(grid, everyone),
        check_vma=False,
    )
```
